32 devices in a mesh: expert: 4 (over z), cuts: 2 (over core), dp: 4 (over y, x).
Axes of the slice: x: 2, y: 2, z: 4, core: 2. Of those that a mesh axis runs over, the one named last changes fastest.
Arguments:
- tokens: float32 [4096, 1024], P(('expert', 'dp')), may hold values from -6 to 6
- cotangent: float32 [4096, 1024], P(('expert', 'dp')), may hold values from -1.25 to 1.25
- routes: int32 [4096, 2], P(('expert', 'dp')), may hold values from 0 to 3, all different within a row; in each aligned block of 256 rows (0 to 255, 256 to 511, ...) at most 192 rows name the same one
- combine_index: int32 [4096, 2], P(('expert', 'dp')), may hold values from 0 to 255
- combine_table: float32 [256], replicated, may hold values from 0.1 to 1
- w_in: bfloat16 [4, 1024, 2688], P('expert', None, 'cuts'), may hold values from -0.1875 to 0.1875
- w_out: bfloat16 [4, 2688, 1024], P('expert', 'cuts'), may hold values from -0.125 to 0.125
Outputs:
- layer_out: float32 [4096, 1024], P(('expert', 'dp'))
- d_tokens: float32 [4096, 1024], P(('expert', 'dp'))
- grad_in: float32 [4, 1024, 2688], P('expert', 'dp', 'cuts')
- grad_out: float32 [4, 2688, 1024], P('expert', 'cuts', 'dp')
The draws below stay inside these ranges and needn't reach their ends.
Inputs may be any that keep to these rules, and one draw needn't show every extreme that they name: `routes`: each row names 2 different experts. Among the rows of one device no expert is named more than 192 times, and in the rows of some device some expert is named exactly 192 times.
All inputs are finite; a program needn't handle non-finite values.
Results may differ from the reference program's by a relative error of at most 0.011.
Values may be sent and summed in bfloat16 or wider, within the bound.
No kernel may reach another device: no remote copies, remote signals or barrier semaphores. Data moves between devices by JAX's collectives and lax.ppermute only.
A program may use at most 128 MiB of HBM per device.

```python
import math
import jax
import jax.numpy as jnp
import numpy as np
from jax import lax

L = 1024
H = 2688
TOPK = 2
LEVELS = 256
TOK_DEV = 256
EXPERTS = 4
TOKENS = 4096
MOST = 192
ROWS_EXPERT = 2048
N_EXPERT = 4
N_DP = 4


def place_ends(values, key, smallest, top_value):
    longest = values.shape.index(max(values.shape))
    spots = []
    for shift in (0, 1):
        where = [jax.random.randint(jax.random.fold_in(key, axis), (), 0, length) for axis, length in enumerate(values.shape)]
        where[longest] = (where[longest] + shift) % values.shape[longest]
        spots.append(tuple(where))
    return values.at[spots[0]].set(smallest).at[spots[1]].set(top_value)


def shard_levels(own_key, extent, split, low, high):
    loudness = 1.0
    for axis_at, parts in split:
        steps = jax.random.uniform(jax.random.fold_in(jax.random.fold_in(own_key, 6), axis_at), (parts,), jnp.float32, low / len(split), high / len(split))
        loudness = loudness * jnp.repeat(jnp.exp(steps), extent[axis_at] // parts).reshape((-1,) + (1,) * (len(extent) - 1 - axis_at))
    return loudness


def routed_block(key, own, number, rows, count, top, reach, skew):
    order = jax.random.permutation(key, count)
    packed, common = portions_of(count, rows * top, reach, skew, True), portions_of(count, rows * top, reach, skew, False)
    places = jnp.arange(count)

    def named(sizes, offset_by):
        used = int((sizes > 0).sum())
        fixed = max(1, used // 4)
        passed = fixed + (places - fixed + offset_by * (used - fixed)) % max(1, count - fixed)
        return jnp.zeros((count,), jnp.int32).at[order[jnp.where(places < fixed, places, passed)]].set(jnp.asarray(sizes, jnp.int32))

    sizes = jnp.where(number % 4 == 0, named(packed, number // 4), named(common, number - number // 4 - 1))
    mixed = jax.random.permutation(jax.random.fold_in(own, 3), count)
    donor, receiver = mixed[0:count // 2 * 2:2], mixed[1:count // 2 * 2:2]
    room = jnp.minimum(sizes[donor] - 1, reach - sizes[receiver]) // 2
    room = jnp.where((donor == order[0]) | (receiver == order[0]) | (sizes[receiver] == 0), 0, jnp.maximum(room, 0))
    passed = jax.random.randint(jax.random.fold_in(own, 4), (count // 2,), 0, 1 << 20) % (room + 1)
    sizes = sizes.at[donor].add(-passed).at[receiver].add(passed)
    labels = jnp.searchsorted(jnp.cumsum(sizes), jnp.arange(rows * top), side="right").astype(jnp.int32)
    table = labels.reshape(top, rows).T
    table = table[jax.random.permutation(jax.random.fold_in(own, 1), rows)]
    offset_by = jax.random.randint(jax.random.fold_in(own, 2), (rows, 1), 0, top)
    return jnp.take_along_axis(table, (jnp.arange(top)[None, :] + offset_by) % top, axis=1)


def portions_of(number_of, total, most, slope, full):
    loads = [(1 << 20) // math.isqrt(grade ** slope) + 1 for grade in range(1, number_of + 1)]
    largest = most if full else min(most, max(-(-total // number_of), total * loads[0] // sum(loads)))
    least = 1 if total - largest >= number_of - 1 else 0
    holding, spare = [largest] + [least] * (number_of - 1), total - largest - least * (number_of - 1)
    while spare > 0:
        candidates = [i for i in range(1, number_of) if holding[i] < largest] or [i for i in range(1, number_of) if holding[i] < most]
        whole, remaining = sum([loads[i] for i in candidates]), spare
        for i in candidates:
            extra = min(most - holding[i], max(1, remaining * loads[i] // whole), spare)
            holding[i] = holding[i] + extra
            spare = spare - extra
    return np.array(holding)


def noise(key, extent, scale, limit, split=(), kind=jnp.bfloat16):
    factor_of = shard_levels(key, extent, split, -0.22, 0.18) if split else 1.0
    result = jax.random.normal(key, extent, jnp.float32) * scale * factor_of
    return jnp.minimum(jnp.maximum(result, -limit), limit).astype(kind)


def setup_inputs(seed: int = 0) -> dict:
    seeds = jax.random.split(jax.random.key(seed), 8)
    tokens = noise(seeds[0], (TOKENS, L), 1.0, 6.0, ((0, 16),), jnp.float32)
    cotangent = noise(seeds[1], (TOKENS, L), (4.0 / ROWS_EXPERT ** 0.5), 1.25, ((0, 16),), jnp.float32)
    routes_keys = jax.random.split(jax.random.fold_in(seeds[2], 1), TOKENS // TOK_DEV)
    routes_turns = jax.random.permutation(jax.random.fold_in(seeds[2], 3), TOKENS // TOK_DEV)
    routes = jax.vmap(lambda own, number: routed_block(jax.random.fold_in(seeds[2], 2), own, number, TOK_DEV, EXPERTS, TOPK, MOST, 2))(routes_keys, routes_turns).reshape((TOKENS, TOPK))
    combine_index = place_ends(jax.random.randint(seeds[3], (TOKENS, TOPK), 0, LEVELS), jax.random.fold_in(seeds[3], 1), 0, LEVELS - 1).astype(jnp.int32)
    combine_table = jnp.clip(jnp.exp(jax.random.uniform(seeds[4], (LEVELS,), jnp.float32, math.log(0.1), math.log(1.0))), 0.1, 1.0)
    w_in = noise(seeds[5], (EXPERTS, L, H), L ** -0.5, 0.1875, ((0, 4), (2, 2)))
    w_out = noise(seeds[6], (EXPERTS, H, L), H ** -0.5, 0.125, ((0, 4), (1, 2)))
    return dict(tokens=tokens, cotangent=cotangent, routes=routes, combine_index=combine_index, combine_table=combine_table, w_in=w_in, w_out=w_out)


def by_group(array):
    width = array.shape[1]
    shaped = array.reshape(N_EXPERT, N_DP, MOST, width)
    return jnp.swapaxes(shaped, 0, 1).reshape(N_DP, N_EXPERT * MOST, width).astype(jnp.float32)


def reference(tokens, cotangent, routes, combine_index, combine_table, w_in, w_out):
    pair_count = TOKENS * TOPK
    blocks = TOKENS // TOK_DEV
    slots = blocks * MOST
    table_ids = jnp.arange(LEVELS, dtype=jnp.int32)
    weight = jnp.sum(jnp.where(combine_index[:, :, None] == table_ids, combine_table, 0.0), axis=2).reshape(pair_count)
    routes_block = routes.reshape(blocks, TOK_DEV * TOPK)
    onehot = (routes_block[:, :, None] == jnp.arange(EXPERTS, dtype=jnp.int32)).astype(jnp.int32)
    before = jnp.cumsum(onehot, axis=1).astype(jnp.int32) - onehot
    row_rank = jnp.sum(before * onehot, axis=2).astype(jnp.int32)
    block_start = (jnp.arange(blocks, dtype=jnp.int32) * MOST)[:, None]
    slot_index = (routes_block * slots + block_start + row_rank).reshape(pair_count).astype(jnp.int32)
    source = jnp.full((EXPERTS * slots,), pair_count, jnp.int32)
    source = source.at[slot_index].set(jnp.arange(pair_count, dtype=jnp.int32)).reshape(EXPERTS, slots)

    def expert_pass(operands):
        expert_source, inner_weight, outer_weight = operands
        filled = expert_source < pair_count
        picked = jnp.minimum(expert_source, pair_count - 1)
        token_row = picked // TOPK
        arrived = jnp.where(filled[:, None], tokens[token_row], 0.0).astype(jnp.bfloat16)
        scaled = jnp.where(filled, weight[picked], 0.0)
        grad_arrived = (scaled[:, None] * cotangent[token_row]).astype(jnp.bfloat16)
        activation = jnp.dot(arrived, inner_weight, preferred_element_type=jnp.float32)
        positive = jnp.maximum(activation, 0.0)
        hidden = (positive * positive).astype(jnp.bfloat16)
        expert_rows = jnp.dot(hidden, outer_weight, preferred_element_type=jnp.float32).astype(jnp.bfloat16)
        d_hidden = jnp.dot(grad_arrived, outer_weight.T, preferred_element_type=jnp.float32)
        d_act = (d_hidden * 2.0 * positive).astype(jnp.bfloat16)
        back_rows = jnp.dot(d_act, inner_weight.T, preferred_element_type=jnp.float32).astype(jnp.bfloat16)
        part_in = jnp.einsum("gsl,gsh->glh", by_group(arrived), by_group(d_act))
        part_out = jnp.einsum("gsh,gsl->ghl", by_group(hidden), by_group(grad_arrived))
        grad_inner = jnp.sum(lax.optimization_barrier(part_in.astype(jnp.bfloat16)).astype(jnp.float32), axis=0)
        grad_outer = jnp.sum(lax.optimization_barrier(part_out.astype(jnp.bfloat16)).astype(jnp.float32), axis=0)
        return expert_rows, back_rows, grad_inner, grad_outer

    expert_rows, back_rows, grad_in, grad_out = lax.map(expert_pass, (source, w_in, w_out))
    returned = expert_rows.reshape(EXPERTS * slots, L)[slot_index].astype(jnp.float32)
    layer_out = jnp.sum((weight[:, None] * returned).reshape(TOKENS, TOPK, L), axis=1)
    gradient_rows = back_rows.reshape(EXPERTS * slots, L)[slot_index].astype(jnp.float32)
    d_tokens = jnp.sum(gradient_rows.reshape(TOKENS, TOPK, L), axis=1)
    return layer_out, d_tokens, grad_in, grad_out
```

```python
import functools

import jax
import jax.numpy as jnp
from jax import lax
from jax.experimental import pallas as pl
from jax.experimental.pallas import tpu as pltpu
from jax.sharding import PartitionSpec as P

BF16 = jnp.bfloat16
F32 = jnp.float32
ROW_TILE = 16
COLUMN_TILE = 256
VMEM_BYTES = 56 * 1024 * 1024
MATMUL = (((1,), (0,)), ((), ()))
CONTRACT_LAST = (((1,), (1,)), ((), ()))
CONTRACT_FIRST = (((0,), (0,)), ((), ()))


def mxu(a, b, dims=MATMUL):
    return lax.dot_general(a, b, dims, preferred_element_type=F32)


def shape(rows, columns, dtype=BF16):
    return jax.ShapeDtypeStruct((rows, columns), dtype)


def local(body, outs, operands, flops, name, scratch=()):
    moved = sum(x.size * x.dtype.itemsize for x in (*operands, *outs))
    return pl.pallas_call(
        body,
        out_shape=tuple(outs),
        in_specs=[pl.BlockSpec(memory_space=pltpu.VMEM)] * len(operands),
        out_specs=tuple([pl.BlockSpec(memory_space=pltpu.VMEM)] * len(outs)),
        scratch_shapes=list(scratch),
        compiler_params=pltpu.CompilerParams(vmem_limit_bytes=VMEM_BYTES),
        cost_estimate=pl.CostEstimate(flops=flops, bytes_accessed=moved, transcendentals=0),
        name=name,
    )(*operands)


def window(index, width):
    return pl.ds(pl.multiple_of(index * width, width), width)


def over_columns(width, step):
    full = width // COLUMN_TILE

    def body(i, carry):
        step(window(i, COLUMN_TILE))
        return carry

    lax.fori_loop(0, full, body, 0)
    if width % COLUMN_TILE:
        step(pl.ds(full * COLUMN_TILE, width - full * COLUMN_TILE))


def picks(meta, k, shift, capacity):
    rows = lax.broadcasted_iota(jnp.int32, (meta.shape[0], capacity), 1) + shift * capacity
    return (meta[:, k : k + 1].astype(jnp.int32) == rows).astype(F32).astype(BF16)


def route_body(owners, capacity, routes_ref, index_ref, table_ref, tokens_ref, meta_ref, own_ref, *sends):
    me, core = lax.axis_index("expert"), lax.axis_index("cuts")
    count, top = routes_ref.shape
    width = -(-owners // 128) * 128
    half = tokens_ref.shape[1] // lax.axis_size("cuts")
    routes, index = routes_ref[...], index_ref[...]
    expert_lane = lax.broadcasted_iota(jnp.int32, (count, width), 1)
    named = [routes[:, k : k + 1] == expert_lane for k in range(top)]
    onehot = sum(n.astype(F32) for n in named).astype(BF16)
    earlier = lax.broadcasted_iota(jnp.int32, (count, count), 0) > lax.broadcasted_iota(
        jnp.int32, (count, count), 1
    )
    before = mxu(earlier.astype(F32).astype(BF16), onehot)
    level = lax.broadcasted_iota(jnp.int32, (count, table_ref.shape[1]), 1)
    lane = lax.broadcasted_iota(jnp.int32, meta_ref.shape, 1)
    meta = jnp.zeros(meta_ref.shape, F32)
    for k in range(top):
        rank = jnp.sum(jnp.where(named[k], before, 0.0), axis=1, keepdims=True)
        shift = routes[:, k : k + 1] - me
        shift = jnp.where(shift < 0, shift + owners, shift)
        slot = (shift * capacity).astype(F32) + rank
        weight = jnp.sum(
            jnp.where(index[:, k : k + 1] == level, table_ref[...], 0.0), axis=1, keepdims=True
        )
        meta = jnp.where(lane == k, slot, jnp.where(lane == top + k, weight, meta))
    meta_ref[...] = meta
    wide = tokens_ref[...].astype(BF16)
    narrow = tokens_ref[:, window(core, half)].astype(BF16)
    for shift, ref in enumerate((own_ref, *sends)):
        chosen = sum(picks(meta, k, shift, capacity) for k in range(top))
        ref[...] = mxu(chosen, narrow if shift else wide, CONTRACT_FIRST).astype(BF16)


def weigh_body(top, capacity, meta_ref, cotangent_ref, own_ref, *sends):
    core = lax.axis_index("cuts")
    meta = meta_ref[...]
    half = cotangent_ref.shape[1] // lax.axis_size("cuts")

    def scaled(values):
        return [(meta[:, top + k : top + k + 1] * values).astype(BF16) for k in range(top)]

    wide, narrow = scaled(cotangent_ref[...]), scaled(cotangent_ref[:, window(core, half)])
    for shift, ref in enumerate((own_ref, *sends)):
        rows = narrow if shift else wide
        ref[...] = sum(
            mxu(picks(meta, k, shift, capacity), rows[k], CONTRACT_FIRST) for k in range(top)
        ).astype(BF16)


def assemble(full_ref, own, mine, other):
    core = lax.axis_index("cuts")
    capacity, half = mine[0].shape
    full_ref[:capacity, :] = own[...]
    for i, (a, b) in enumerate(zip(mine, other, strict=True), 1):
        rows = slice(i * capacity, (i + 1) * capacity)
        full_ref[rows, window(core, half)] = a[...]
        full_ref[rows, window(1 - core, half)] = b[...]


def forward_body(remote, own, *refs):
    mine, other = refs[:remote], refs[remote : 2 * remote]
    inner_ref, outer_ref, x_ref, positive_ref, hidden_ref, keep_ref, give_ref = refs[2 * remote :]
    core = lax.axis_index("cuts")
    assemble(x_ref, own, mine, other)

    def activate(columns):
        positive = jnp.maximum(mxu(x_ref[...], inner_ref[:, columns]), 0.0)
        positive_ref[:, columns] = positive.astype(BF16)
        hidden_ref[:, columns] = (positive * positive).astype(BF16)

    over_columns(inner_ref.shape[1], activate)
    to_halves(hidden_ref, outer_ref, MATMUL, keep_ref, give_ref)


def to_halves(rows_ref, weight_ref, dims, keep_ref, give_ref):
    core = lax.axis_index("cuts")
    half = keep_ref.shape[1]
    for owner, ref in ((1 - core, give_ref), (core, keep_ref)):

        def step(i, carry, owner=owner, ref=ref):
            features = window(owner * (half // COLUMN_TILE) + i, COLUMN_TILE)
            weight = weight_ref[:, features] if dims == MATMUL else weight_ref[features, :]
            ref[:, window(i, COLUMN_TILE)] = mxu(rows_ref[...], weight, dims).astype(BF16)
            return carry

        lax.fori_loop(0, half // COLUMN_TILE, step, 0)


def split_body(keep_ref, came_ref, *outs):
    capacity = outs[0].shape[0]
    for i, ref in enumerate(outs):
        rows = slice(i * capacity, (i + 1) * capacity)
        ref[...] = (keep_ref[rows, :].astype(F32) + came_ref[rows, :].astype(F32)).astype(BF16)


def outer_grad_body(remote, own, *refs):
    mine, other = refs[:remote], refs[remote : 2 * remote]
    hidden_ref, g_ref, *outs = refs[2 * remote :]
    me = lax.axis_index("dp")
    assemble(g_ref, own, mine, other)
    groups = len(outs) // 2
    rows = outs[0].shape[0]
    width = outs[0].shape[1]
    for k in reversed(range(groups)):
        block = g_ref[:, window(me ^ k, width)]
        for part in range(2):
            hidden = hidden_ref[:, part * rows : (part + 1) * rows]
            outs[2 * k + part][...] = mxu(hidden, block, CONTRACT_FIRST).astype(BF16)


def backward_body(g_ref, positive_ref, inner_ref, outer_ref, d_act_ref, keep_ref, give_ref):
    def step(columns):
        d_hidden = mxu(g_ref[...], outer_ref[columns, :], CONTRACT_LAST)
        d_act_ref[:, columns] = (d_hidden * 2.0 * positive_ref[:, columns].astype(F32)).astype(BF16)

    over_columns(positive_ref.shape[1], step)
    to_halves(d_act_ref, inner_ref, CONTRACT_LAST, keep_ref, give_ref)


def inner_grad_body(x_ref, d_act_ref, *outs):
    me = lax.axis_index("dp")
    groups = len(outs) // 2
    rows = outs[0].shape[0]
    for k in reversed(range(groups)):
        for part in range(2):
            block = x_ref[:, window((me ^ k) * 2 + part, rows)]
            ref = outs[2 * k + part]

            def step(columns, block=block, ref=ref):
                ref[:, columns] = mxu(block, d_act_ref[:, columns], CONTRACT_FIRST).astype(BF16)

            over_columns(d_act_ref.shape[1], step)


def combine_body(top, weighted, meta_ref, *refs):
    *chunks, wide_ref, narrow_ref = refs
    meta = meta_ref[...]
    capacity = chunks[0].shape[0]
    total = 0.0
    if weighted:
        for k in range(top):
            got = sum(mxu(picks(meta, k, s, capacity), c[...]) for s, c in enumerate(chunks))
            total += meta[:, top + k : top + k + 1] * got
    else:
        for s, c in enumerate(chunks):
            total += mxu(sum(picks(meta, k, s, capacity) for k in range(top)), c[...])
    wide_ref[...] = total
    narrow_ref[...] = total.astype(BF16)


def join_body(mine_ref, other_ref, out_ref):
    core = lax.axis_index("cuts")
    half = mine_ref.shape[1]
    out_ref[:, window(core, half)] = mine_ref[...]
    out_ref[:, window(1 - core, half)] = other_ref[...].astype(F32)


def shifted(x, axis, shift):
    size = lax.axis_size(axis)
    return lax.ppermute(x, axis, [(i, (i + shift) % size) for i in range(size)])


def partner(x, axis, bit):
    return lax.ppermute(x, axis, [(i, i ^ bit) for i in range(lax.axis_size(axis))])


def sum_over_groups(blocks, bits):
    blocks = dict(blocks)
    for at, bit in enumerate(bits):
        came = {r ^ bit: partner(blocks[r], "dp", bit) for r in sorted(blocks, reverse=True) if r & bit}
        last = at == len(bits) - 1
        blocks = {
            r: (blocks[r].astype(F32) + came[r].astype(F32)).astype(F32 if last else BF16) for r in came
        }
    return blocks[0]


def shards(tokens, cotangent, routes, combine_index, combine_table, w_in, w_out):
    owners, groups = lax.axis_size("expert"), lax.axis_size("dp")
    count, features = tokens.shape
    top = routes.shape[1]
    half = features // lax.axis_size("cuts")
    capacity = -(-max(2, 3 * count * top // (2 * owners)) // ROW_TILE) * ROW_TILE
    slots = owners * capacity
    remote = owners - 1
    inner, outer = w_in[0], w_out[0]
    units = inner.shape[1]
    bits = [1 << i for i in range(groups.bit_length() - 1)]

    def exchange(sends):
        mine = [shifted(x, "expert", s) for s, x in enumerate(sends, 1)]
        return mine, [partner(x, "cuts", 1) for x in mine]

    def give_back(keep, give):
        chunks = local(
            split_body, [shape(capacity, half)] * owners, [keep, partner(give, "cuts", 1)], 0, "split"
        )
        return [chunks[0]] + [shifted(x, "expert", -s) for s, x in enumerate(chunks[1:], 1)]

    def combine(chunks, weighted):
        wide, narrow = local(
            functools.partial(combine_body, top, weighted),
            [shape(count, half, F32), shape(count, half)],
            [meta, *chunks],
            2 * count * slots * half,
            "combine",
        )
        (out,) = local(
            join_body, [shape(count, features, F32)], [wide, partner(narrow, "cuts", 1)], 0, "join"
        )
        return out

    meta, own, *sends = local(
        functools.partial(route_body, owners, capacity),
        [shape(count, 128, F32), shape(capacity, features)] + [shape(capacity, half)] * remote,
        [routes, combine_index, combine_table[None, :], tokens],
        2 * count * slots * features,
        "route",
    )
    mine, other = exchange(sends)
    grad_own, *grad_sends = local(
        functools.partial(weigh_body, top, capacity),
        [shape(capacity, features)] + [shape(capacity, half)] * remote,
        [meta, cotangent],
        4 * count * slots * features,
        "weigh",
    )
    grad_mine, grad_other = exchange(grad_sends)
    work = 2 * slots * features * units
    arrived, positive, hidden, keep, give = local(
        functools.partial(forward_body, remote),
        [shape(slots, features), shape(slots, units), shape(slots, units)] + [shape(slots, half)] * 2,
        [own, *mine, *other, inner, outer],
        2 * work,
        "forward",
    )
    returned = give_back(keep, give)
    grad_rows, *outer_parts = local(
        functools.partial(outer_grad_body, remote),
        [shape(slots, features)] + [shape(units // 2, features // groups)] * (2 * groups),
        [grad_own, *grad_mine, *grad_other, hidden],
        work,
        "outer_grad",
    )
    outer_sums = [
        sum_over_groups({r: outer_parts[2 * r + part] for r in range(groups)}, order)
        for part, order in enumerate((bits, bits[::-1]))
    ]
    d_act, grad_keep, grad_give = local(
        backward_body,
        [shape(slots, units)] + [shape(slots, half)] * 2,
        [grad_rows, positive, inner, outer],
        2 * work,
        "backward",
    )
    grad_returned = give_back(grad_keep, grad_give)
    inner_parts = local(
        inner_grad_body,
        [shape(features // groups // 2, units)] * (2 * groups),
        [arrived, d_act],
        work,
        "inner_grad",
    )
    inner_sums = [
        sum_over_groups({r: inner_parts[2 * r + part] for r in range(groups)}, order)
        for part, order in enumerate((bits, bits[::-1]))
    ]
    layer_out = combine(returned, True)
    d_tokens = combine(grad_returned, False)
    grad_in = jnp.concatenate(inner_sums, axis=0)[None]
    grad_out = jnp.concatenate(outer_sums, axis=0)[None]
    return (layer_out, d_tokens, grad_in, grad_out)


def solution(mesh):
    in_specs = (
        P(("expert", "dp"), None),
        P(("expert", "dp"), None),
        P(("expert", "dp"), None),
        P(("expert", "dp"), None),
        P(),
        P("expert", None, "cuts"),
        P("expert", "cuts", None),
    )
    out_specs = (
        P(("expert", "dp"), None),
        P(("expert", "dp"), None),
        P("expert", "dp", "cuts"),
        P("expert", "cuts", "dp"),
    )
    return jax.shard_map(shards, mesh=mesh, in_specs=in_specs, out_specs=out_specs, check_vma=False)
```

```python
import functools

import jax
import jax.numpy as jnp
from jax import lax
from jax.experimental import pallas as pl
from jax.experimental.pallas import tpu as pltpu
from jax.sharding import PartitionSpec as P

BF16 = jnp.bfloat16
F32 = jnp.float32
ROW_TILE = 16
TILE = 256
VMEM_BYTES = 56 * 1024 * 1024
MATMUL = (((1,), (0,)), ((), ()))
CONTRACT_LAST = (((1,), (1,)), ((), ()))
CONTRACT_FIRST = (((0,), (0,)), ((), ()))


def mxu(a, b, dims=MATMUL):
    return lax.dot_general(a, b, dims, preferred_element_type=F32)


def shape(rows, columns, dtype=BF16):
    return jax.ShapeDtypeStruct((rows, columns), dtype)


def local(body, outs, operands, flops, name, scratch=()):
    moved = sum(x.size * x.dtype.itemsize for x in (*operands, *outs))
    return pl.pallas_call(
        body,
        out_shape=tuple(outs),
        in_specs=[pl.BlockSpec(memory_space=pltpu.VMEM)] * len(operands),
        out_specs=tuple([pl.BlockSpec(memory_space=pltpu.VMEM)] * len(outs)),
        scratch_shapes=list(scratch),
        compiler_params=pltpu.CompilerParams(vmem_limit_bytes=VMEM_BYTES),
        cost_estimate=pl.CostEstimate(flops=flops, bytes_accessed=moved, transcendentals=0),
        name=name,
    )(*operands)


def window(index, width):
    return pl.ds(pl.multiple_of(index * width, width), width)


def over_tiles(width, step):
    full = width // TILE

    def body(i, carry):
        step(window(i, TILE))
        return carry

    lax.fori_loop(0, full, body, 0)
    if width % TILE:
        step(pl.ds(full * TILE, width - full * TILE))


def picks(meta, k, shift, capacity):
    rows = lax.broadcasted_iota(jnp.int32, (meta.shape[0], capacity), 1) + shift * capacity
    return (meta[:, k : k + 1].astype(jnp.int32) == rows).astype(F32).astype(BF16)


def columns_of(table_t):
    count = table_t.shape[1]
    unit = lax.broadcasted_iota(jnp.int32, (count, count), 0) == lax.broadcasted_iota(
        jnp.int32, (count, count), 1
    )
    return mxu(unit.astype(F32).astype(BF16), table_t.astype(F32).astype(BF16), CONTRACT_LAST).astype(jnp.int32)


def route_body(owners, capacity, routes_ref, index_ref, table_ref, tokens_ref, meta_ref, own_ref, *sends):
    me, core = lax.axis_index("expert"), lax.axis_index("cuts")
    top, count = routes_ref.shape
    width = -(-owners // 128) * 128
    half = tokens_ref.shape[1] // lax.axis_size("cuts")
    routes, index = columns_of(routes_ref[...]), columns_of(index_ref[...])
    expert_lane = lax.broadcasted_iota(jnp.int32, (count, width), 1)
    named = [routes[:, k : k + 1] == expert_lane for k in range(top)]
    onehot = sum(n.astype(F32) for n in named).astype(BF16)
    earlier = lax.broadcasted_iota(jnp.int32, (count, count), 0) > lax.broadcasted_iota(
        jnp.int32, (count, count), 1
    )
    before = mxu(earlier.astype(F32).astype(BF16), onehot)
    level = lax.broadcasted_iota(jnp.int32, (count, table_ref.shape[1]), 1)
    lane = lax.broadcasted_iota(jnp.int32, meta_ref.shape, 1)
    meta = jnp.zeros(meta_ref.shape, F32)
    for k in range(top):
        rank = jnp.sum(jnp.where(named[k], before, 0.0), axis=1, keepdims=True)
        shift = routes[:, k : k + 1] - me
        shift = jnp.where(shift < 0, shift + owners, shift)
        slot = (shift * capacity).astype(F32) + rank
        weight = jnp.sum(
            jnp.where(index[:, k : k + 1] == level, table_ref[...], 0.0), axis=1, keepdims=True
        )
        meta = jnp.where(lane == k, slot, jnp.where(lane == top + k, weight, meta))
    meta_ref[...] = meta
    wide = tokens_ref[...].astype(BF16)
    narrow = tokens_ref[:, window(core, half)].astype(BF16)
    for shift, ref in enumerate((own_ref, *sends)):
        chosen = sum(picks(meta, k, shift, capacity) for k in range(top))
        ref[...] = mxu(chosen, narrow if shift else wide, CONTRACT_FIRST).astype(BF16)


def weigh_body(top, capacity, meta_ref, cotangent_ref, own_ref, *sends):
    core = lax.axis_index("cuts")
    meta = meta_ref[...]
    half = cotangent_ref.shape[1] // lax.axis_size("cuts")

    def scaled(values):
        return [(meta[:, top + k : top + k + 1] * values).astype(BF16) for k in range(top)]

    wide, narrow = scaled(cotangent_ref[...]), scaled(cotangent_ref[:, window(core, half)])
    for shift, ref in enumerate((own_ref, *sends)):
        rows = narrow if shift else wide
        ref[...] = sum(
            mxu(picks(meta, k, shift, capacity), rows[k], CONTRACT_FIRST) for k in range(top)
        ).astype(BF16)


def assemble(full_ref, own, mine, other):
    core = lax.axis_index("cuts")
    capacity, half = mine[0].shape
    full_ref[:capacity, :] = own[...]
    for i, (a, b) in enumerate(zip(mine, other, strict=True), 1):
        rows = slice(i * capacity, (i + 1) * capacity)
        full_ref[rows, window(core, half)] = a[...]
        full_ref[rows, window(1 - core, half)] = b[...]


def to_halves(rows_ref, weight_ref, keep_ref, give_ref):
    core = lax.axis_index("cuts")
    half = keep_ref.shape[1]
    for owner, ref in ((1 - core, give_ref), (core, keep_ref)):

        def step(i, carry, owner=owner, ref=ref):
            features = window(owner * (half // TILE) + i, TILE)
            ref[:, window(i, TILE)] = mxu(rows_ref[...], weight_ref[:, features]).astype(BF16)
            return carry

        lax.fori_loop(0, half // TILE, step, 0)


def forward_body(remote, own, *refs):
    mine, other = refs[:remote], refs[remote : 2 * remote]
    inner_ref, outer_ref, x_ref, positive_ref, hidden_ref, keep_ref, give_ref, turned = refs[2 * remote :]
    assemble(x_ref, own, mine, other)

    def activate(units):
        positive = jnp.maximum(mxu(inner_ref[units, :], x_ref[...], CONTRACT_LAST), 0.0)
        positive_ref[units, :] = positive.astype(BF16)
        hidden = (positive * positive).astype(BF16)
        hidden_ref[units, :] = hidden
        turned[:, units] = hidden.T

    over_tiles(inner_ref.shape[0], activate)
    to_halves(turned, outer_ref, keep_ref, give_ref)


def backward_body(g_ref, positive_ref, inner_ref, outer_ref, d_act_ref, keep_ref, give_ref, turned):
    def step(units):
        d_hidden = mxu(outer_ref[units, :], g_ref[...], CONTRACT_LAST)
        d_act = (d_hidden * 2.0 * positive_ref[units, :].astype(F32)).astype(BF16)
        d_act_ref[units, :] = d_act
        turned[:, units] = d_act.T

    over_tiles(outer_ref.shape[0], step)
    to_halves(turned, inner_ref, keep_ref, give_ref)


def split_body(keep_ref, came_ref, *outs):
    capacity = outs[0].shape[0]
    for i, ref in enumerate(outs):
        rows = slice(i * capacity, (i + 1) * capacity)
        ref[...] = (keep_ref[rows, :].astype(F32) + came_ref[rows, :].astype(F32)).astype(BF16)


def gather_body(remote, own, *refs):
    assemble(refs[2 * remote], own, refs[:remote], refs[remote : 2 * remote])


def pieces(keys, units_ref, rows_ref, outs):
    me = lax.axis_index("dp")
    for (block, part), ref in zip(keys, outs, strict=True):
        rows, width = ref.shape
        features = rows_ref[:, window(me ^ block, width)]
        ref[...] = mxu(units_ref[part * rows : (part + 1) * rows, :], features).astype(BF16)


def grad_body(keys, units_ref, rows_ref, *outs):
    pieces(keys, units_ref, rows_ref, outs)


def first_grad_body(keys, remote, own, *refs):
    units_ref, rows_ref, *outs = refs[2 * remote :]
    assemble(rows_ref, own, refs[:remote], refs[remote : 2 * remote])
    pieces(keys, units_ref, rows_ref, outs)


def combine_body(top, weighted, meta_ref, *refs):
    *chunks, wide_ref, narrow_ref = refs
    meta = meta_ref[...]
    capacity = chunks[0].shape[0]
    total = 0.0
    if weighted:
        for k in range(top):
            got = sum(mxu(picks(meta, k, s, capacity), c[...]) for s, c in enumerate(chunks))
            total += meta[:, top + k : top + k + 1] * got
    else:
        for s, c in enumerate(chunks):
            total += mxu(sum(picks(meta, k, s, capacity) for k in range(top)), c[...])
    wide_ref[...] = total
    narrow_ref[...] = total.astype(BF16)


def join_body(mine_ref, other_ref, out_ref):
    core = lax.axis_index("cuts")
    half = mine_ref.shape[1]
    out_ref[:, window(core, half)] = mine_ref[...]
    out_ref[:, window(1 - core, half)] = other_ref[...].astype(F32)


def shifted(x, axis, shift):
    size = lax.axis_size(axis)
    return lax.ppermute(x, axis, [(i, (i + shift) % size) for i in range(size)])


def partner(x, axis, bit):
    return lax.ppermute(x, axis, [(i, i ^ bit) for i in range(lax.axis_size(axis))])


def after(values, *earlier):
    return lax.optimization_barrier((values, earlier))[0]


def halve(blocks, bit, dtype):
    came = {r ^ bit: partner(blocks[r], "dp", bit) for r in sorted(blocks, reverse=True) if r & bit}
    return {r: (blocks[r].astype(F32) + came[r].astype(F32)).astype(dtype) for r in came}


def shards(tokens, cotangent, routes, combine_index, combine_table, w_in, w_out):
    owners, groups = lax.axis_size("expert"), lax.axis_size("dp")
    count, features = tokens.shape
    top = routes.shape[1]
    half = features // lax.axis_size("cuts")
    capacity = -(-max(2, 3 * count * top // (2 * owners)) // ROW_TILE) * ROW_TILE
    slots = owners * capacity
    remote = owners - 1
    inner, outer = w_in[0].T, w_out[0]
    units = outer.shape[0]
    bits = [1 << i for i in range(groups.bit_length() - 1)]
    orders = (bits, bits[::-1])
    piece = shape(units // 2, features // groups)
    keys = [(r, part) for r in reversed(range(groups)) for part in range(2)]
    leaving = [(r, part) for r, part in keys if r & orders[part][0]]
    staying = [key for key in keys if key not in leaving]
    work = 2 * slots * features * units

    def across_cores(chunks):
        return [partner(x, "cuts", 1) for x in chunks]

    def over_experts(chunks, sign):
        return [shifted(x, "expert", sign * s) for s, x in enumerate(chunks, 1)]

    def split(keep, came):
        return local(split_body, [shape(capacity, half)] * owners, [keep, came], 0, "split")

    def combine(chunks, weighted):
        return local(
            functools.partial(combine_body, top, weighted),
            [shape(count, half, F32), shape(count, half)],
            [meta, *chunks],
            2 * count * slots * half,
            "combine",
        )

    def join(wide, came):
        return local(join_body, [shape(count, features, F32)], [wide, came], 0, "join")[0]

    def halved(pieces, step, dtype=BF16):
        out = {}
        for part, order in enumerate(orders):
            mine = {r: x for (r, p), x in pieces.items() if p == part}
            out |= {(r, part): x for r, x in halve(mine, order[step], dtype).items()}
        return out

    meta, own, *sends = local(
        functools.partial(route_body, owners, capacity),
        [shape(count, 128, F32), shape(capacity, features)] + [shape(capacity, half)] * remote,
        [routes.T, combine_index.T, combine_table[None, :], tokens],
        2 * count * slots * features,
        "route",
    )
    mine = over_experts(sends, 1)
    grad_own, *grad_sends = local(
        functools.partial(weigh_body, top, capacity),
        [shape(capacity, features)] + [shape(capacity, half)] * remote,
        [meta, cotangent],
        4 * count * slots * features,
        "weigh",
    )
    grad_mine = over_experts(grad_sends, 1)
    mine = after(mine, grad_sends)
    other = across_cores(mine)
    arrived, positive, hidden, keep, give = local(
        functools.partial(forward_body, remote),
        [shape(slots, features), shape(units, slots), shape(units, slots)] + [shape(slots, half)] * 2,
        [own, *mine, *other, inner, outer],
        2 * work,
        "forward",
        [pltpu.VMEM((slots, units), BF16)],
    )
    grad_mine, hidden, keep, give = after((grad_mine, hidden, keep, give))
    came = partner(give, "cuts", 1)
    grad_other = across_cores(grad_mine)
    grad_rows, *out = local(
        functools.partial(first_grad_body, leaving, remote),
        [shape(slots, features)] + [piece] * len(leaving),
        [grad_own, *grad_mine, *grad_other, hidden],
        work // 2,
        "outer_leaving",
    )
    outer_pieces = dict(zip(leaving, out, strict=True))
    keep, came = after((keep, came), grad_rows)
    chunks = split(keep, came)
    returned = [chunks[0]] + over_experts(chunks[1:], -1)
    hidden, grad_rows = after((hidden, grad_rows), chunks)
    out = local(
        functools.partial(grad_body, staying), [piece] * len(staying), [hidden, grad_rows], work // 2, "outer_staying"
    )
    outer_pieces |= dict(zip(staying, out, strict=True))
    grad_rows, positive = after((grad_rows, positive), out)
    d_act, grad_keep, grad_give = local(
        backward_body,
        [shape(units, slots)] + [shape(slots, half)] * 2,
        [grad_rows, positive, inner, outer],
        2 * work,
        "backward",
        [pltpu.VMEM((slots, units), BF16)],
    )
    outer_pieces = halved(outer_pieces, 0)
    d_act, grad_give, outer_pieces, returned = after((d_act, grad_give, outer_pieces, returned))
    grad_came = partner(grad_give, "cuts", 1)
    out = local(
        functools.partial(grad_body, leaving), [piece] * len(leaving), [d_act, arrived], work // 2, "inner_leaving"
    )
    inner_pieces = dict(zip(leaving, out, strict=True))
    grad_keep, grad_came = after((grad_keep, grad_came), out)
    chunks = split(grad_keep, grad_came)
    grad_returned = [chunks[0]] + over_experts(chunks[1:], -1)
    d_act, arrived = after((d_act, arrived), chunks)
    out = local(
        functools.partial(grad_body, staying), [piece] * len(staying), [d_act, arrived], work // 2, "inner_staying"
    )
    inner_pieces |= dict(zip(staying, out, strict=True))
    returned = after(returned, out)
    wide, narrow = combine(returned, True)
    layer_out = join(wide, partner(narrow, "cuts", 1))
    outer_pieces = halved(outer_pieces, 1, F32)
    inner_pieces = halved(inner_pieces, 0)
    inner_pieces, grad_returned = after((inner_pieces, grad_returned), wide)
    wide, narrow = combine(grad_returned, False)
    d_tokens = join(wide, partner(narrow, "cuts", 1))
    inner_pieces = halved(inner_pieces, 1, F32)
    grad_in, grad_out = (
        jnp.concatenate([p[0, 0], p[0, 1]], axis=0) for p in (inner_pieces, outer_pieces)
    )
    return (layer_out, d_tokens, grad_in.T[None], grad_out[None])


def solution(mesh):
    in_specs = (
        P(("expert", "dp"), None),
        P(("expert", "dp"), None),
        P(("expert", "dp"), None),
        P(("expert", "dp"), None),
        P(),
        P("expert", None, "cuts"),
        P("expert", "cuts", None),
    )
    out_specs = (
        P(("expert", "dp"), None),
        P(("expert", "dp"), None),
        P("expert", "dp", "cuts"),
        P("expert", "cuts", "dp"),
    )
    return jax.shard_map(shards, mesh=mesh, in_specs=in_specs, out_specs=out_specs, check_vma=False)
```

```python
import functools

import jax
import jax.numpy as jnp
from jax import lax
from jax.experimental import pallas as pl
from jax.experimental.pallas import tpu as pltpu
from jax.sharding import PartitionSpec as P

BF16 = jnp.bfloat16
F32 = jnp.float32
ROW_TILE = 16
TILE = 256
VMEM_BYTES = 24 * 1024 * 1024
COST = 64
MATMUL = (((1,), (0,)), ((), ()))
CONTRACT_LAST = (((1,), (1,)), ((), ()))
CONTRACT_FIRST = (((0,), (0,)), ((), ()))


def mxu(a, b, dims=MATMUL):
    return lax.dot_general(a, b, dims, preferred_element_type=F32)


def shape(rows, columns, dtype=BF16):
    return jax.ShapeDtypeStruct((rows, columns), dtype)


def local(body, outs, operands, flops, name, scratch=()):
    moved = sum(x.size * x.dtype.itemsize for x in (*operands, *outs))
    return pl.pallas_call(
        body,
        out_shape=tuple(pltpu.VMEM(x.shape, x.dtype) for x in outs),
        in_specs=[pl.BlockSpec(memory_space=pltpu.VMEM)] * len(operands),
        out_specs=tuple([pl.BlockSpec(memory_space=pltpu.VMEM)] * len(outs)),
        scratch_shapes=list(scratch),
        compiler_params=pltpu.CompilerParams(vmem_limit_bytes=VMEM_BYTES),
        cost_estimate=pl.CostEstimate(flops=flops // COST, bytes_accessed=moved // COST, transcendentals=0),
        name=name,
    )(*[pltpu.with_memory_space_constraint(x, pltpu.VMEM) for x in operands])


def window(index, width):
    return pl.ds(pl.multiple_of(index * width, width), width)


def over_tiles(width, step):
    full = width // TILE

    def body(i, carry):
        step(window(i, TILE))
        return carry

    lax.fori_loop(0, full, body, 0)
    if width % TILE:
        step(pl.ds(full * TILE, width - full * TILE))


def picks(meta, k, shift, capacity):
    rows = lax.broadcasted_iota(jnp.int32, (meta.shape[0], capacity), 1) + shift * capacity
    return (meta[:, k : k + 1].astype(jnp.int32) == rows).astype(F32).astype(BF16)


def columns_of(table_t):
    count = table_t.shape[1]
    unit = lax.broadcasted_iota(jnp.int32, (count, count), 0) == lax.broadcasted_iota(
        jnp.int32, (count, count), 1
    )
    return mxu(unit.astype(F32).astype(BF16), table_t.astype(F32).astype(BF16), CONTRACT_LAST).astype(jnp.int32)


def route_body(owners, capacity, routes_ref, index_ref, table_ref, tokens_ref, meta_ref, own_ref, *sends):
    me, core = lax.axis_index("expert"), lax.axis_index("cuts")
    top, count = routes_ref.shape
    width = -(-owners // 128) * 128
    half = tokens_ref.shape[1] // lax.axis_size("cuts")
    routes, index = columns_of(routes_ref[...]), columns_of(index_ref[...])
    expert_lane = lax.broadcasted_iota(jnp.int32, (count, width), 1)
    named = [routes[:, k : k + 1] == expert_lane for k in range(top)]
    onehot = sum(n.astype(F32) for n in named).astype(BF16)
    earlier = lax.broadcasted_iota(jnp.int32, (count, count), 0) > lax.broadcasted_iota(
        jnp.int32, (count, count), 1
    )
    before = mxu(earlier.astype(F32).astype(BF16), onehot)
    level = lax.broadcasted_iota(jnp.int32, (count, table_ref.shape[1]), 1)
    lane = lax.broadcasted_iota(jnp.int32, meta_ref.shape, 1)
    meta = jnp.zeros(meta_ref.shape, F32)
    for k in range(top):
        rank = jnp.sum(jnp.where(named[k], before, 0.0), axis=1, keepdims=True)
        shift = routes[:, k : k + 1] ^ me
        slot = (shift * capacity).astype(F32) + rank
        weight = jnp.sum(
            jnp.where(index[:, k : k + 1] == level, table_ref[...], 0.0), axis=1, keepdims=True
        )
        meta = jnp.where(lane == k, slot, jnp.where(lane == top + k, weight, meta))
    meta_ref[...] = meta
    wide = tokens_ref[...].astype(BF16)
    narrow = tokens_ref[:, window(core, half)].astype(BF16)
    for shift, ref in enumerate((own_ref, *sends)):
        chosen = sum(picks(meta, k, shift, capacity) for k in range(top))
        ref[...] = mxu(chosen, narrow if shift else wide, CONTRACT_FIRST).astype(BF16)


def weigh_body(top, capacity, meta_ref, cotangent_ref, own_ref, *sends):
    core = lax.axis_index("cuts")
    meta = meta_ref[...]
    half = cotangent_ref.shape[1] // lax.axis_size("cuts")

    def scaled(values):
        return [(meta[:, top + k : top + k + 1] * values).astype(BF16) for k in range(top)]

    wide, narrow = scaled(cotangent_ref[...]), scaled(cotangent_ref[:, window(core, half)])
    for shift, ref in enumerate((own_ref, *sends)):
        rows = narrow if shift else wide
        ref[...] = sum(
            mxu(picks(meta, k, shift, capacity), rows[k], CONTRACT_FIRST) for k in range(top)
        ).astype(BF16)


def assemble(full_ref, own, mine, other):
    core = lax.axis_index("cuts")
    capacity, half = mine[0].shape
    full_ref[:capacity, :] = own[...]
    for i, (a, b) in enumerate(zip(mine, other, strict=True), 1):
        rows = slice(i * capacity, (i + 1) * capacity)
        full_ref[rows, window(core, half)] = a[...]
        full_ref[rows, window(1 - core, half)] = b[...]


def hidden_body(remote, own, *refs):
    mine, other = refs[:remote], refs[remote : 2 * remote]
    inner_ref, x_ref, positive_ref, hidden_ref = refs[2 * remote :]
    assemble(x_ref, own, mine, other)

    def step(units):
        positive = jnp.maximum(mxu(inner_ref[units, :], x_ref[...], CONTRACT_LAST), 0.0)
        positive_ref[units, :] = positive.astype(BF16)
        hidden_ref[units, :] = (positive * positive).astype(BF16)

    over_tiles(inner_ref.shape[0], step)


def d_act_body(g_ref, positive_ref, outer_ref, d_act_ref):
    def step(units):
        d_hidden = mxu(outer_ref[units, :], g_ref[...], CONTRACT_LAST)
        d_act_ref[units, :] = (d_hidden * 2.0 * positive_ref[units, :].astype(F32)).astype(BF16)

    over_tiles(outer_ref.shape[0], step)


def rows_body(units_ref, weight_ref, keep_ref, give_ref, turned):
    def turn(units):
        turned[:, units] = units_ref[units, :].T

    over_tiles(units_ref.shape[0], turn)
    core = lax.axis_index("cuts")
    half = keep_ref.shape[1]
    for owner, ref in ((1 - core, give_ref), (core, keep_ref)):

        def step(i, carry, owner=owner, ref=ref):
            features = window(owner * (half // TILE) + i, TILE)
            ref[:, window(i, TILE)] = mxu(turned[...], weight_ref[:, features]).astype(BF16)
            return carry

        lax.fori_loop(0, half // TILE, step, 0)


def split_body(keep_ref, came_ref, *outs):
    capacity = outs[0].shape[0]
    for i, ref in enumerate(outs):
        rows = slice(i * capacity, (i + 1) * capacity)
        ref[...] = (keep_ref[rows, :].astype(F32) + came_ref[rows, :].astype(F32)).astype(BF16)


def gather_body(remote, own, *refs):
    assemble(refs[2 * remote], own, refs[:remote], refs[remote : 2 * remote])


def pieces(keys, units_ref, rows_ref, outs):
    me = lax.axis_index("dp")
    for part, (blocks, ref) in enumerate(zip(keys, outs, strict=True)):
        rows = ref.shape[0] // len(blocks)
        for i, block in enumerate(blocks):
            features = rows_ref[:, window(me ^ block, ref.shape[1])]
            units = units_ref[part * rows : (part + 1) * rows, :]
            ref[i * rows : (i + 1) * rows, :] = mxu(units, features).astype(BF16)


def grad_body(keys, units_ref, rows_ref, *outs):
    pieces(keys, units_ref, rows_ref, outs)


def first_grad_body(keys, remote, own, *refs):
    units_ref, rows_ref, *outs = refs[2 * remote :]
    assemble(rows_ref, own, refs[:remote], refs[remote : 2 * remote])
    pieces(keys, units_ref, rows_ref, outs)


def combine_body(top, weighted, meta_ref, *refs):
    *chunks, wide_ref, narrow_ref = refs
    meta = meta_ref[...]
    capacity = chunks[0].shape[0]
    total = 0.0
    if weighted:
        for k in range(top):
            got = sum(mxu(picks(meta, k, s, capacity), c[...]) for s, c in enumerate(chunks))
            total += meta[:, top + k : top + k + 1] * got
    else:
        for s, c in enumerate(chunks):
            total += mxu(sum(picks(meta, k, s, capacity) for k in range(top)), c[...])
    wide_ref[...] = total
    narrow_ref[...] = total.astype(BF16)


def join_body(mine_ref, other_ref, out_ref):
    core = lax.axis_index("cuts")
    half = mine_ref.shape[1]
    out_ref[:, window(core, half)] = mine_ref[...]
    out_ref[:, window(1 - core, half)] = other_ref[...].astype(F32)


def partner(x, axis, bit):
    return lax.ppermute(x, axis, [(i, i ^ bit) for i in range(lax.axis_size(axis))])


def after(values, *earlier):
    return lax.optimization_barrier((values, earlier))[0]


def shards(tokens, cotangent, routes, combine_index, combine_table, w_in, w_out):
    owners, groups = lax.axis_size("expert"), lax.axis_size("dp")
    count, features = tokens.shape
    top = routes.shape[1]
    half = features // lax.axis_size("cuts")
    capacity = -(-max(2, 3 * count * top // (2 * owners)) // ROW_TILE) * ROW_TILE
    slots = owners * capacity
    remote = owners - 1
    inner, outer = w_in[0].T, w_out[0]
    units = outer.shape[0]
    bits = [1 << i for i in range(groups.bit_length() - 1)]
    orders = (bits, bits[::-1])
    leaving = [[r for r in range(groups) if r & order[0]] for order in orders]
    staying = [[r ^ order[0] for r in blocks] for order, blocks in zip(orders, leaving, strict=True)]
    part_rows = units // 2
    piece = shape(part_rows * groups // 2, features // groups)
    work = 2 * slots * features * units

    def across_cores(chunks):
        return [partner(x, "cuts", 1) for x in chunks]

    def over_experts(chunks):
        return [partner(x, "expert", s) for s, x in enumerate(chunks, 1)]

    def times_weight(units_rows, weight, name):
        return local(
            rows_body, [shape(slots, half)] * 2, [units_rows, weight], work, name, [pltpu.VMEM((slots, units), BF16)]
        )

    def split(keep, came):
        return local(split_body, [shape(capacity, half)] * owners, [keep, came], 0, "split")

    def combine(chunks, weighted):
        return local(
            functools.partial(combine_body, top, weighted),
            [shape(count, half, F32), shape(count, half)],
            [meta, *chunks],
            2 * count * slots * half,
            "combine",
        )

    def join(wide, came):
        return local(join_body, [shape(count, features, F32)], [wide, came], 0, "join")[0]

    def grads(keys, units_rows, rows, name):
        return local(functools.partial(grad_body, keys), [piece] * 2, [units_rows, rows], work // 2, name)

    def added(kept, came, dtype=BF16):
        return (kept.astype(F32) + came.astype(F32)).astype(dtype)

    def block(stack, i):
        return stack[i * part_rows : (i + 1) * part_rows]

    def halvings(blocks, order):
        for bit in order:
            came = {r ^ bit: partner(blocks[r], "dp", bit) for r in blocks if r & bit}
            dtype = F32 if bit == order[-1] else BF16
            blocks = {r: added(blocks[r], came[r], dtype) for r in came}
        return blocks[0]

    meta, own, *sends = local(
        functools.partial(route_body, owners, capacity),
        [shape(count, 128, F32), shape(capacity, features)] + [shape(capacity, half)] * remote,
        [routes.T, combine_index.T, combine_table[None, :], tokens],
        2 * count * slots * features,
        "route",
    )
    mine = over_experts(sends)
    grad_own, *grad_sends = local(
        functools.partial(weigh_body, top, capacity),
        [shape(capacity, features)] + [shape(capacity, half)] * remote,
        [meta, cotangent],
        4 * count * slots * features,
        "weigh",
    )
    grad_mine = over_experts(grad_sends)
    mine = after(mine, grad_sends)
    other = across_cores(mine)
    arrived, positive, hidden = local(
        functools.partial(hidden_body, remote),
        [shape(slots, features), shape(units, slots), shape(units, slots)],
        [own, *mine, *other, inner],
        work,
        "hidden",
    )
    keep, give = times_weight(hidden, outer, "rows")
    grad_mine, hidden, keep, give = after((grad_mine, hidden, keep, give))
    came = partner(give, "cuts", 1)
    grad_other = across_cores(grad_mine)
    grad_rows, *outer_sent = local(
        functools.partial(first_grad_body, leaving, remote),
        [shape(slots, features)] + [piece] * 2,
        [grad_own, *grad_mine, *grad_other, hidden],
        work // 2,
        "outer_leaving",
    )
    outer_came = [partner(x, "dp", order[0]) for x, order in zip(outer_sent, orders, strict=True)]
    keep, came = after((keep, came), grad_rows)
    chunks = split(keep, came)
    returned = [chunks[0]] + over_experts(chunks[1:])
    grad_rows, positive = after((grad_rows, positive), chunks)
    (d_act,) = local(
        d_act_body, [shape(units, slots)], [grad_rows, positive, outer], work, "d_act"
    )
    inner_sent = grads(leaving, d_act, arrived, "inner_leaving")
    hidden, grad_rows = after((hidden, grad_rows), inner_sent)
    outer_kept = grads(staying, hidden, grad_rows, "outer_staying")
    d_act_late = after(d_act, outer_kept)
    grad_keep, grad_give = times_weight(d_act_late, inner, "grad_rows")
    grad_give, outer_came, outer_kept, returned, d_act, arrived = after(
        (grad_give, outer_came, outer_kept, returned, d_act, arrived)
    )
    grad_came = partner(grad_give, "cuts", 1)
    inner_kept = grads(staying, d_act, arrived, "inner_staying")
    outer_own, mixed = [], []
    for part in range(2):
        sums = [added(block(outer_kept[part], i), block(outer_came[part], i)) for i in range(groups // 2)]
        outer_own.append(dict(zip(staying[part], sums, strict=True)))
    for part in range(2):
        other = outer_own[1 - part]
        moving = [other[r] for r in other if r & orders[part][0]]
        got = partner(jnp.concatenate([*moving, inner_sent[part]], axis=0), "dp", orders[part][0])
        mixed.append(got)
    chunks = split(grad_keep, grad_came)
    grad_returned = [chunks[0]] + over_experts(chunks[1:])
    wide, narrow = combine(returned, True)
    layer_out = join(wide, partner(narrow, "cuts", 1))
    mixed, inner_kept, grad_returned = after((mixed, inner_kept, grad_returned))
    outer_sums, inner_sums = [], []
    for part, order in enumerate(orders):
        bit = orders[1 - part][0]
        mine = [r for r in outer_own[part] if not r & bit]
        rest = {r: added(outer_own[part][r], block(mixed[1 - part], i), F32) for i, r in enumerate(mine)}
        outer_sums.append(halvings(rest, order[2:]) if order[2:] else rest[0])
        start = len(mine)
        sums = {
            r: added(block(inner_kept[part], i), block(mixed[part], start + i)) for i, r in enumerate(staying[part])
        }
        inner_sums.append(halvings(sums, order[1:]))
    grad_out = jnp.concatenate(outer_sums, axis=0)
    grad_in = jnp.concatenate(inner_sums, axis=0).T
    wide, narrow = combine(grad_returned, False)
    d_tokens = join(wide, partner(narrow, "cuts", 1))
    return (layer_out, d_tokens, grad_in[None], grad_out[None])


def solution(mesh):
    in_specs = (
        P(("expert", "dp"), None),
        P(("expert", "dp"), None),
        P(("expert", "dp"), None),
        P(("expert", "dp"), None),
        P(),
        P("expert", None, "cuts"),
        P("expert", "cuts", None),
    )
    out_specs = (
        P(("expert", "dp"), None),
        P(("expert", "dp"), None),
        P("expert", "dp", "cuts"),
        P("expert", "cuts", "dp"),
    )
    return jax.shard_map(shards, mesh=mesh, in_specs=in_specs, out_specs=out_specs, check_vma=False)
```

```python
import functools

import jax
import jax.numpy as jnp
from jax import lax
from jax.experimental import pallas as pl
from jax.experimental.pallas import tpu as pltpu
from jax.sharding import PartitionSpec as P

BF16 = jnp.bfloat16
F32 = jnp.float32
ROW_TILE = 16
TILE = 256
VMEM_BYTES = 24 * 1024 * 1024
COST = 64
MATMUL = (((1,), (0,)), ((), ()))
CONTRACT_LAST = (((1,), (1,)), ((), ()))
CONTRACT_FIRST = (((0,), (0,)), ((), ()))


def mxu(a, b, dims=MATMUL):
    return lax.dot_general(a, b, dims, preferred_element_type=F32)


def shape(rows, columns, dtype=BF16):
    return jax.ShapeDtypeStruct((rows, columns), dtype)


def local(body, outs, operands, flops, name, scratch=(), space=pltpu.VMEM, gives=pltpu.VMEM):
    moved = sum(x.size * x.dtype.itemsize for x in (*operands, *outs))
    return pl.pallas_call(
        body,
        out_shape=tuple(gives(x.shape, x.dtype) for x in outs),
        in_specs=[pl.BlockSpec(memory_space=pltpu.VMEM)] * len(operands),
        out_specs=tuple([pl.BlockSpec(memory_space=pltpu.VMEM)] * len(outs)),
        scratch_shapes=list(scratch),
        compiler_params=pltpu.CompilerParams(vmem_limit_bytes=VMEM_BYTES),
        cost_estimate=pl.CostEstimate(flops=flops // COST, bytes_accessed=moved // COST, transcendentals=0),
        name=name,
    )(*[pltpu.with_memory_space_constraint(x, space) for x in operands])


def window(index, width):
    return pl.ds(pl.multiple_of(index * width, width), width)


def over_tiles(width, step):
    full = width // TILE

    def body(i, carry):
        step(window(i, TILE))
        return carry

    lax.fori_loop(0, full, body, 0)
    if width % TILE:
        step(pl.ds(full * TILE, width - full * TILE))


def picks(meta, k, shift, capacity):
    rows = lax.broadcasted_iota(jnp.int32, (meta.shape[0], capacity), 1) + shift * capacity
    return (meta[:, k : k + 1].astype(jnp.int32) == rows).astype(F32).astype(BF16)


def columns_of(table_t):
    count = table_t.shape[1]
    unit = lax.broadcasted_iota(jnp.int32, (count, count), 0) == lax.broadcasted_iota(
        jnp.int32, (count, count), 1
    )
    return mxu(unit.astype(F32).astype(BF16), table_t.astype(F32).astype(BF16), CONTRACT_LAST).astype(jnp.int32)


def route_body(owners, capacity, routes_ref, index_ref, table_ref, tokens_ref, meta_ref, own_ref, *sends):
    me, core = lax.axis_index("expert"), lax.axis_index("cuts")
    top, count = routes_ref.shape
    width = -(-owners // 128) * 128
    half = tokens_ref.shape[1] // lax.axis_size("cuts")
    routes, index = columns_of(routes_ref[...]), columns_of(index_ref[...])
    expert_lane = lax.broadcasted_iota(jnp.int32, (count, width), 1)
    named = [routes[:, k : k + 1] == expert_lane for k in range(top)]
    onehot = sum(n.astype(F32) for n in named).astype(BF16)
    earlier = lax.broadcasted_iota(jnp.int32, (count, count), 0) > lax.broadcasted_iota(
        jnp.int32, (count, count), 1
    )
    before = mxu(earlier.astype(F32).astype(BF16), onehot)
    level = lax.broadcasted_iota(jnp.int32, (count, table_ref.shape[1]), 1)
    lane = lax.broadcasted_iota(jnp.int32, meta_ref.shape, 1)
    meta = jnp.zeros(meta_ref.shape, F32)
    for k in range(top):
        rank = jnp.sum(jnp.where(named[k], before, 0.0), axis=1, keepdims=True)
        shift = routes[:, k : k + 1] ^ me
        slot = (shift * capacity).astype(F32) + rank
        weight = jnp.sum(
            jnp.where(index[:, k : k + 1] == level, table_ref[...], 0.0), axis=1, keepdims=True
        )
        meta = jnp.where(lane == k, slot, jnp.where(lane == top + k, weight, meta))
    meta_ref[...] = meta
    wide = tokens_ref[...].astype(BF16)
    narrow = tokens_ref[:, window(core, half)].astype(BF16)
    for shift, ref in enumerate((own_ref, *sends)):
        chosen = sum(picks(meta, k, shift, capacity) for k in range(top))
        ref[...] = mxu(chosen, narrow if shift else wide, CONTRACT_FIRST).astype(BF16)


def weigh_body(top, capacity, meta_ref, cotangent_ref, own_ref, *sends):
    core = lax.axis_index("cuts")
    meta = meta_ref[...]
    half = cotangent_ref.shape[1] // lax.axis_size("cuts")

    def scaled(values):
        return [(meta[:, top + k : top + k + 1] * values).astype(BF16) for k in range(top)]

    wide, narrow = scaled(cotangent_ref[...]), scaled(cotangent_ref[:, window(core, half)])
    for shift, ref in enumerate((own_ref, *sends)):
        rows = narrow if shift else wide
        ref[...] = sum(
            mxu(picks(meta, k, shift, capacity), rows[k], CONTRACT_FIRST) for k in range(top)
        ).astype(BF16)


def assemble(full_ref, own, mine, other):
    core = lax.axis_index("cuts")
    capacity, half = mine[0].shape
    full_ref[:capacity, :] = own[...]
    for i, (a, b) in enumerate(zip(mine, other, strict=True), 1):
        rows = slice(i * capacity, (i + 1) * capacity)
        full_ref[rows, window(core, half)] = a[...]
        full_ref[rows, window(1 - core, half)] = b[...]


def hidden_body(remote, own, *refs):
    mine, other = refs[:remote], refs[remote : 2 * remote]
    inner_ref, x_ref, positive_ref, hidden_ref = refs[2 * remote :]
    assemble(x_ref, own, mine, other)

    def step(units):
        positive = jnp.maximum(mxu(inner_ref[units, :], x_ref[...], CONTRACT_LAST), 0.0)
        positive_ref[units, :] = positive.astype(BF16)
        hidden_ref[units, :] = (positive * positive).astype(BF16)

    over_tiles(inner_ref.shape[0], step)


def d_act_body(g_ref, positive_ref, outer_ref, d_act_ref):
    def step(units):
        d_hidden = mxu(outer_ref[units, :], g_ref[...], CONTRACT_LAST)
        d_act_ref[units, :] = (d_hidden * 2.0 * positive_ref[units, :].astype(F32)).astype(BF16)

    over_tiles(outer_ref.shape[0], step)


def rows_body(units_ref, weight_ref, keep_ref, give_ref, turned):
    def turn(units):
        turned[:, units] = units_ref[units, :].T

    over_tiles(units_ref.shape[0], turn)
    core = lax.axis_index("cuts")
    half = keep_ref.shape[1]
    for owner, ref in ((1 - core, give_ref), (core, keep_ref)):

        def step(i, carry, owner=owner, ref=ref):
            features = window(owner * (half // TILE) + i, TILE)
            ref[:, window(i, TILE)] = mxu(turned[...], weight_ref[:, features]).astype(BF16)
            return carry

        lax.fori_loop(0, half // TILE, step, 0)


def split_body(keep_ref, came_ref, *outs):
    capacity = outs[0].shape[0]
    for i, ref in enumerate(outs):
        rows = slice(i * capacity, (i + 1) * capacity)
        ref[...] = (keep_ref[rows, :].astype(F32) + came_ref[rows, :].astype(F32)).astype(BF16)


def gather_body(remote, own, *refs):
    assemble(refs[2 * remote], own, refs[:remote], refs[remote : 2 * remote])


def pieces(keys, units_ref, rows_ref, outs):
    me = lax.axis_index("dp")
    for part, (blocks, ref) in enumerate(zip(keys, outs, strict=True)):
        rows = ref.shape[0] // len(blocks)
        for i, block in enumerate(blocks):
            features = rows_ref[:, window(me ^ block, ref.shape[1])]
            units = units_ref[part * rows : (part + 1) * rows, :]
            ref[i * rows : (i + 1) * rows, :] = mxu(units, features).astype(BF16)


def grad_body(keys, units_ref, rows_ref, *outs):
    pieces(keys, units_ref, rows_ref, outs)


def first_grad_body(keys, remote, own, *refs):
    units_ref, rows_ref, *outs = refs[2 * remote :]
    assemble(rows_ref, own, refs[:remote], refs[remote : 2 * remote])
    pieces(keys, units_ref, rows_ref, outs)


def combine_body(top, weighted, meta_ref, *refs):
    *chunks, wide_ref, narrow_ref = refs
    meta = meta_ref[...]
    capacity = chunks[0].shape[0]
    total = 0.0
    if weighted:
        for k in range(top):
            got = sum(mxu(picks(meta, k, s, capacity), c[...]) for s, c in enumerate(chunks))
            total += meta[:, top + k : top + k + 1] * got
    else:
        for s, c in enumerate(chunks):
            total += mxu(sum(picks(meta, k, s, capacity) for k in range(top)), c[...])
    wide_ref[...] = total
    narrow_ref[...] = total.astype(BF16)


def join_body(mine_ref, other_ref, out_ref):
    core = lax.axis_index("cuts")
    half = mine_ref.shape[1]
    out_ref[:, window(core, half)] = mine_ref[...]
    out_ref[:, window(1 - core, half)] = other_ref[...].astype(F32)


def added(a, b):
    return a.astype(F32) + b.astype(F32)


def mix_body(kept0, kept1, came0, came1, inner0, inner1, send0, send1, own0, own1):
    rows = own0.shape[0]
    for kept, came, own, send, inner in ((kept0, came0, own0, send1, inner1), (kept1, came1, own1, send0, inner0)):
        own[...] = added(kept[:rows, :], came[:rows, :]).astype(BF16)
        send[:rows, :] = added(kept[rows:, :], came[rows:, :]).astype(BF16)
        send[rows:, :] = inner[...]


def inner_sum_body(kept0, kept1, mixed0, mixed1, move0, move1, own0, own1):
    rows = own0.shape[0]
    for kept, mixed, move, own in ((kept0, mixed0, move0, own0), (kept1, mixed1, move1, own1)):
        own[...] = added(kept[:rows, :], mixed[rows : 2 * rows, :]).astype(BF16)
        move[...] = added(kept[rows:, :], mixed[2 * rows :, :]).astype(BF16)


def last_sum_body(own0, own1, came0, came1, out_ref):
    rows = own0.shape[0]
    out_ref[:rows, :] = added(own0[...], came0[:rows, :])
    out_ref[rows:, :] = added(own1[...], came1[:rows, :])


def partner(x, axis, bit):
    return lax.ppermute(x, axis, [(i, i ^ bit) for i in range(lax.axis_size(axis))])


def after(values, *earlier):
    return lax.optimization_barrier((values, earlier))[0]


def shards(tokens, cotangent, routes, combine_index, combine_table, w_in, w_out):
    owners, groups = lax.axis_size("expert"), lax.axis_size("dp")
    count, features = tokens.shape
    top = routes.shape[1]
    half = features // lax.axis_size("cuts")
    capacity = -(-max(2, 3 * count * top // (2 * owners)) // ROW_TILE) * ROW_TILE
    slots = owners * capacity
    remote = owners - 1
    inner, outer = w_in[0].T, w_out[0]
    units = outer.shape[0]
    bits = [1 << i for i in range(groups.bit_length() - 1)]
    orders = (bits, bits[::-1])
    leaving = [[r for r in range(groups) if r & order[0]] for order in orders]
    staying = [[r ^ order[0] for r in blocks] for order, blocks in zip(orders, leaving, strict=True)]
    part_rows = units // 2
    piece = shape(part_rows * groups // 2, features // groups)
    quarter = shape(part_rows, features // groups)
    total = shape(units, features // groups, F32)
    work = 2 * slots * features * units

    def across_cores(chunks):
        return [partner(x, "cuts", 1) for x in chunks]

    def over_experts(chunks):
        got = {s: partner(chunks[s - 1], "expert", s) for s in reversed(range(1, owners))}
        return [got[s] for s in range(1, owners)]

    def times_weight(units_rows, weight, name):
        return local(
            rows_body, [shape(slots, half)] * 2, [units_rows, weight], work, name, [pltpu.VMEM((slots, units), BF16)]
        )

    def split(keep, came):
        return local(split_body, [shape(capacity, half)] * owners, [keep, came], 0, "split")

    def combine(chunks, weighted):
        return local(
            functools.partial(combine_body, top, weighted),
            [shape(count, half, F32), shape(count, half)],
            [meta, *chunks],
            2 * count * slots * half,
            "combine",
        )

    def join(wide, came):
        return local(join_body, [shape(count, features, F32)], [wide, came], 0, "join", gives=pltpu.HBM)[0]

    def grads(keys, units_rows, rows, name):
        return local(functools.partial(grad_body, keys), [piece] * 2, [units_rows, rows], work // 2, name)

    meta, own, *sends = local(
        functools.partial(route_body, owners, capacity),
        [shape(count, 128, F32), shape(capacity, features)] + [shape(capacity, half)] * remote,
        [routes.T, combine_index.T, combine_table[None, :], tokens],
        2 * count * slots * features,
        "route",
        space=pltpu.HBM,
    )
    mine = over_experts(sends)
    grad_own, *grad_sends = local(
        functools.partial(weigh_body, top, capacity),
        [shape(capacity, features)] + [shape(capacity, half)] * remote,
        [meta, cotangent],
        4 * count * slots * features,
        "weigh",
    )
    grad_mine = over_experts(grad_sends)
    mine = after(mine, grad_sends)
    other = across_cores(mine)
    arrived, positive, hidden = local(
        functools.partial(hidden_body, remote),
        [shape(slots, features), shape(units, slots), shape(units, slots)],
        [own, *mine, *other, inner],
        work,
        "hidden",
    )
    keep, give = times_weight(hidden, outer, "rows")
    grad_mine, hidden, keep, give = after((grad_mine, hidden, keep, give))
    came = partner(give, "cuts", 1)
    grad_other = across_cores(grad_mine)
    grad_rows, *outer_sent = local(
        functools.partial(first_grad_body, leaving, remote),
        [shape(slots, features)] + [piece] * 2,
        [grad_own, *grad_mine, *grad_other, hidden],
        work // 2,
        "outer_leaving",
    )
    outer_came = [partner(x, "dp", order[0]) for x, order in zip(outer_sent, orders, strict=True)]
    keep, came = after((keep, came), grad_rows)
    chunks = split(keep, came)
    returned = [chunks[0]] + over_experts(chunks[1:])
    grad_rows, positive = after((grad_rows, positive), chunks)
    (d_act,) = local(
        d_act_body, [shape(units, slots)], [grad_rows, positive, outer], work, "d_act"
    )
    inner_sent = grads(leaving, d_act, arrived, "inner_leaving")
    hidden, grad_rows = after((hidden, grad_rows), inner_sent)
    outer_kept = grads(staying, hidden, grad_rows, "outer_staying")
    d_act_late = after(d_act, outer_kept)
    grad_keep, grad_give = times_weight(d_act_late, inner, "grad_rows")
    outer_came = after(outer_came, grad_give)
    *sends, outer_own0, outer_own1 = local(
        mix_body,
        [shape(3 * part_rows, piece.shape[1])] * 2 + [quarter] * 2,
        [*outer_kept, *outer_came, *inner_sent],
        0,
        "mix",
    )
    mixed = [partner(x, "dp", order[0]) for x, order in zip(sends, orders, strict=True)]
    grad_give, returned = after((grad_give, returned))
    grad_came = partner(grad_give, "cuts", 1)
    inner_kept = grads(staying, d_act, arrived, "inner_staying")
    chunks = split(grad_keep, grad_came)
    grad_returned = [chunks[0]] + over_experts(chunks[1:])
    move0, move1, inner_own0, inner_own1 = local(
        inner_sum_body, [quarter] * 4, [*inner_kept, *mixed], 0, "inner_sum"
    )
    moved = [partner(x, "dp", order[1]) for x, order in zip((move0, move1), orders, strict=True)]
    (grad_out,) = local(
        last_sum_body, [total], [outer_own0, outer_own1, *mixed[::-1]], 0, "outer_last", gives=pltpu.HBM
    )
    (grad_in,) = local(last_sum_body, [total], [inner_own0, inner_own1, *moved], 0, "inner_last", gives=pltpu.HBM)
    wide, narrow = combine(returned, True)
    layer_out = join(wide, partner(narrow, "cuts", 1))
    wide, narrow = combine(grad_returned, False)
    d_tokens = join(wide, partner(narrow, "cuts", 1))
    grad_in = grad_in.T
    return (layer_out, d_tokens, grad_in[None], grad_out[None])


def solution(mesh):
    in_specs = (
        P(("expert", "dp"), None),
        P(("expert", "dp"), None),
        P(("expert", "dp"), None),
        P(("expert", "dp"), None),
        P(),
        P("expert", None, "cuts"),
        P("expert", "cuts", None),
    )
    out_specs = (
        P(("expert", "dp"), None),
        P(("expert", "dp"), None),
        P("expert", "dp", "cuts"),
        P("expert", "cuts", "dp"),
    )
    return jax.shard_map(shards, mesh=mesh, in_specs=in_specs, out_specs=out_specs, check_vma=False)
```

```python
import functools

import jax
import jax.numpy as jnp
from jax import lax
from jax.experimental import pallas as pl
from jax.experimental.pallas import tpu as pltpu
from jax.sharding import PartitionSpec as P

BF16 = jnp.bfloat16
F32 = jnp.float32
ROW_TILE = 16
TILE = 256
VMEM_BYTES = 24 * 1024 * 1024
COST = 64
MATMUL = (((1,), (0,)), ((), ()))
CONTRACT_LAST = (((1,), (1,)), ((), ()))
CONTRACT_FIRST = (((0,), (0,)), ((), ()))


def mxu(a, b, dims=MATMUL):
    return lax.dot_general(a, b, dims, preferred_element_type=F32)


def shape(rows, columns, dtype=BF16):
    return jax.ShapeDtypeStruct((rows, columns), dtype)


def local(body, outs, operands, flops, name, scratch=(), space=pltpu.VMEM, gives=pltpu.VMEM):
    moved = sum(x.size * x.dtype.itemsize for x in (*operands, *outs))
    return pl.pallas_call(
        body,
        out_shape=tuple(gives(x.shape, x.dtype) for x in outs),
        in_specs=[pl.BlockSpec(memory_space=pltpu.VMEM)] * len(operands),
        out_specs=tuple([pl.BlockSpec(memory_space=pltpu.VMEM)] * len(outs)),
        scratch_shapes=list(scratch),
        compiler_params=pltpu.CompilerParams(vmem_limit_bytes=VMEM_BYTES),
        cost_estimate=pl.CostEstimate(flops=flops // COST, bytes_accessed=moved // COST, transcendentals=0),
        name=name,
    )(*[pltpu.with_memory_space_constraint(x, space) for x in operands])


def window(index, width):
    return pl.ds(pl.multiple_of(index * width, width), width)


def over_tiles(width, step):
    full = width // TILE

    def body(i, carry):
        step(window(i, TILE))
        return carry

    lax.fori_loop(0, full, body, 0)
    if width % TILE:
        step(pl.ds(full * TILE, width - full * TILE))


def tiles(units, rows):
    for part in range(2):
        for i in range(0, rows, TILE):
            yield pl.ds(part * (units // 2), units // 2), pl.ds(i, min(TILE, rows - i))


def picks(meta, k, shift, capacity):
    rows = lax.broadcasted_iota(jnp.int32, (meta.shape[0], capacity), 1) + shift * capacity
    return (meta[:, k : k + 1].astype(jnp.int32) == rows).astype(F32).astype(BF16)


def ones(mask):
    return mask.astype(F32).astype(BF16)


def columns_of(table_t):
    count = table_t.shape[1]
    down, along = (lax.broadcasted_iota(jnp.int32, (count, count), i) for i in range(2))
    return mxu(ones(down == along), table_t.astype(F32).astype(BF16), CONTRACT_LAST).astype(jnp.int32)


def route_body(owners, capacity, routes_ref, tokens_ref, own_ref, *sends):
    me, core = lax.axis_index("expert"), lax.axis_index("cuts")
    top, count = routes_ref.shape
    half = tokens_ref.shape[1] // lax.axis_size("cuts")
    routes = routes_ref[...]
    expert = lax.broadcasted_iota(jnp.int32, (-(-owners // ROW_TILE) * ROW_TILE, count), 0)
    named = [routes[k : k + 1, :] == expert for k in range(top)]
    down, along = (lax.broadcasted_iota(jnp.int32, (count, count), i) for i in range(2))
    before = mxu(ones(sum(n.astype(F32) for n in named) > 0.0), ones(down < along))
    slots = [
        (routes[k : k + 1, :] ^ me) * capacity
        + jnp.sum(jnp.where(named[k], before, 0.0), axis=0, keepdims=True).astype(jnp.int32)
        for k in range(top)
    ]
    wide = tokens_ref[...].astype(BF16)
    narrow = tokens_ref[:, window(core, half)].astype(BF16)
    row = lax.broadcasted_iota(jnp.int32, (capacity, count), 0)
    for shift, ref in reversed(list(enumerate((own_ref, *sends)))):
        chosen = ones(sum((slot == row + shift * capacity).astype(F32) for slot in slots) > 0.0)
        ref[...] = mxu(chosen, narrow if shift else wide).astype(BF16)


def weigh_body(owners, capacity, routes_ref, index_ref, table_ref, cotangent_ref, meta_ref, own_ref, *sends):
    me, core = lax.axis_index("expert"), lax.axis_index("cuts")
    top, count = routes_ref.shape
    width = -(-owners // 128) * 128
    half = cotangent_ref.shape[1] // lax.axis_size("cuts")
    routes, index = columns_of(routes_ref[...]), columns_of(index_ref[...])
    expert_lane = lax.broadcasted_iota(jnp.int32, (count, width), 1)
    named = [routes[:, k : k + 1] == expert_lane for k in range(top)]
    down, along = (lax.broadcasted_iota(jnp.int32, (count, count), i) for i in range(2))
    before = mxu(ones(down > along), ones(sum(n.astype(F32) for n in named) > 0.0))
    level = lax.broadcasted_iota(jnp.int32, (count, table_ref.shape[1]), 1)
    lane = lax.broadcasted_iota(jnp.int32, meta_ref.shape, 1)
    meta = jnp.zeros(meta_ref.shape, F32)
    for k in range(top):
        rank = jnp.sum(jnp.where(named[k], before, 0.0), axis=1, keepdims=True)
        slot = ((routes[:, k : k + 1] ^ me) * capacity).astype(F32) + rank
        weight = jnp.sum(
            jnp.where(index[:, k : k + 1] == level, table_ref[...], 0.0), axis=1, keepdims=True
        )
        meta = jnp.where(lane == k, slot, jnp.where(lane == top + k, weight, meta))
    meta_ref[...] = meta

    def scaled(values):
        return [(meta[:, top + k : top + k + 1] * values).astype(BF16) for k in range(top)]

    wide, narrow = scaled(cotangent_ref[...]), scaled(cotangent_ref[:, window(core, half)])
    for shift, ref in enumerate((own_ref, *sends)):
        rows = narrow if shift else wide
        ref[...] = sum(
            mxu(picks(meta, k, shift, capacity), rows[k], CONTRACT_FIRST) for k in range(top)
        ).astype(BF16)


def assemble(full_ref, own, mine, other):
    core = lax.axis_index("cuts")
    capacity, half = mine[0].shape
    full_ref[:capacity, :] = own[...]
    for i, (a, b) in enumerate(zip(mine, other, strict=True), 1):
        rows = slice(i * capacity, (i + 1) * capacity)
        full_ref[rows, window(core, half)] = a[...]
        full_ref[rows, window(1 - core, half)] = b[...]


def hidden_body(remote, own, *refs):
    mine, other = refs[:remote], refs[remote : 2 * remote]
    inner_ref, x_ref, positive_ref, hidden_ref = refs[2 * remote :]
    assemble(x_ref, own, mine, other)

    for units, rows in tiles(inner_ref.shape[0], x_ref.shape[0]):
        positive = jnp.maximum(mxu(inner_ref[units, :], x_ref[rows, :], CONTRACT_LAST), 0.0)
        positive_ref[units, rows] = positive.astype(BF16)
        hidden_ref[units, rows] = (positive * positive).astype(BF16)


def d_act_body(g_ref, positive_ref, outer_ref, d_act_ref):
    for units, rows in tiles(outer_ref.shape[0], g_ref.shape[0]):
        d_hidden = mxu(outer_ref[units, :], g_ref[rows, :], CONTRACT_LAST)
        d_act_ref[units, rows] = (d_hidden * 2.0 * positive_ref[units, rows].astype(F32)).astype(BF16)


def features_of(owner, rows_ref, weight_ref, out_ref):
    half = out_ref.shape[1]
    for i in range(half // TILE):
        features = window(owner * (half // TILE) + i, TILE)
        out_ref[:, i * TILE : (i + 1) * TILE] = mxu(rows_ref[...], weight_ref[:, features]).astype(BF16)


def give_body(units_ref, weight_ref, turned_ref, give_ref):
    def turn(units):
        turned_ref[:, units] = units_ref[units, :].T

    over_tiles(units_ref.shape[0], turn)
    features_of(1 - lax.axis_index("cuts"), turned_ref, weight_ref, give_ref)


def keep_body(turned_ref, weight_ref, keep_ref):
    features_of(lax.axis_index("cuts"), turned_ref, weight_ref, keep_ref)


def split_body(keep_ref, came_ref, *outs):
    capacity = outs[0].shape[0]
    for i, ref in enumerate(outs):
        rows = slice(i * capacity, (i + 1) * capacity)
        ref[...] = (keep_ref[rows, :].astype(F32) + came_ref[rows, :].astype(F32)).astype(BF16)


def gather_body(remote, own, *refs):
    assemble(refs[2 * remote], own, refs[:remote], refs[remote : 2 * remote])


def pieces(keys, units_ref, rows_ref, outs):
    me = lax.axis_index("dp")
    for part, (blocks, ref) in enumerate(zip(keys, outs, strict=True)):
        rows = ref.shape[0] // len(blocks)
        for i, block in enumerate(blocks):
            features = rows_ref[:, window(me ^ block, ref.shape[1])]
            units = units_ref[part * rows : (part + 1) * rows, :]
            ref[i * rows : (i + 1) * rows, :] = mxu(units, features).astype(BF16)


def grad_body(keys, units_ref, rows_ref, *outs):
    pieces(keys, units_ref, rows_ref, outs)


def first_grad_body(keys, remote, own, *refs):
    units_ref, rows_ref, *outs = refs[2 * remote :]
    assemble(rows_ref, own, refs[:remote], refs[remote : 2 * remote])
    pieces(keys, units_ref, rows_ref, outs)


def combine_body(top, weighted, meta_ref, *refs):
    *chunks, wide_ref, narrow_ref = refs
    meta = meta_ref[...]
    capacity = chunks[0].shape[0]
    total = 0.0
    if weighted:
        for k in range(top):
            got = sum(mxu(picks(meta, k, s, capacity), c[...]) for s, c in enumerate(chunks))
            total += meta[:, top + k : top + k + 1] * got
    else:
        for s, c in enumerate(chunks):
            total += mxu(sum(picks(meta, k, s, capacity) for k in range(top)), c[...])
    wide_ref[...] = total
    narrow_ref[...] = total.astype(BF16)


def join_body(*refs):
    core = lax.axis_index("cuts")
    for mine_ref, other_ref, out_ref in (refs[::2], refs[1::2]):
        half = mine_ref.shape[1]
        out_ref[:, window(core, half)] = mine_ref[...]
        out_ref[:, window(1 - core, half)] = other_ref[...].astype(F32)


def added(a, b):
    return a.astype(F32) + b.astype(F32)


def mix_body(kept0, kept1, came0, came1, inner0, inner1, send0, send1, own0, own1):
    rows = own0.shape[0]
    for kept, came, own, send, inner in ((kept0, came0, own0, send1, inner1), (kept1, came1, own1, send0, inner0)):
        own[...] = added(kept[:rows, :], came[:rows, :]).astype(BF16)
        send[:rows, :] = added(kept[rows:, :], came[rows:, :]).astype(BF16)
        send[rows:, :] = inner[...]


def inner_sum_body(kept0, kept1, mixed0, mixed1, move0, move1, own0, own1):
    rows = own0.shape[0]
    for kept, mixed, move, own in ((kept0, mixed0, move0, own0), (kept1, mixed1, move1, own1)):
        own[...] = added(kept[:rows, :], mixed[rows : 2 * rows, :]).astype(BF16)
        move[...] = added(kept[rows:, :], mixed[2 * rows :, :]).astype(BF16)


def last_sum_body(own0, own1, came0, came1, out_ref):
    rows = own0.shape[0]
    out_ref[:rows, :] = added(own0[...], came0[:rows, :])
    out_ref[rows:, :] = added(own1[...], came1[:rows, :])


def partner(x, axis, bit):
    return lax.ppermute(x, axis, [(i, i ^ bit) for i in range(lax.axis_size(axis))])


def after(values, *earlier):
    return lax.optimization_barrier((values, earlier))[0]


def shards(tokens, cotangent, routes, combine_index, combine_table, w_in, w_out):
    owners, groups = lax.axis_size("expert"), lax.axis_size("dp")
    count, features = tokens.shape
    top = routes.shape[1]
    half = features // lax.axis_size("cuts")
    capacity = -(-max(2, 3 * count * top // (2 * owners)) // ROW_TILE) * ROW_TILE
    slots = owners * capacity
    remote = owners - 1
    inner, outer = w_in[0].T, w_out[0]
    units = outer.shape[0]
    bits = [1 << i for i in range(groups.bit_length() - 1)]
    orders = (bits, bits[::-1])
    leaving = [[r for r in range(groups) if r & order[0]] for order in orders]
    staying = [[r ^ order[0] for r in blocks] for order, blocks in zip(orders, leaving, strict=True)]
    part_rows = units // 2
    piece = shape(part_rows * groups // 2, features // groups)
    quarter = shape(part_rows, features // groups)
    total = shape(units, features // groups, F32)
    work = 2 * slots * features * units

    def across_cores(chunks):
        return [partner(x, "cuts", 1) for x in chunks]

    def over_experts(chunks):
        got = {s: partner(chunks[s - 1], "expert", s) for s in reversed(range(1, owners))}
        return [got[s] for s in range(1, owners)]

    def given(units_rows, weight, name):
        return local(
            give_body, [shape(slots, units), shape(slots, half)], [units_rows, weight], work // 2, name + "_give"
        )

    def kept(turned, weight, name):
        return local(keep_body, [shape(slots, half)], [turned, weight], work // 2, name + "_keep")[0]

    def split(keep, came):
        return local(split_body, [shape(capacity, half)] * owners, [keep, came], 0, "split")

    def combine(chunks, weighted):
        return local(
            functools.partial(combine_body, top, weighted),
            [shape(count, half, F32), shape(count, half)],
            [meta, *chunks],
            2 * count * slots * half,
            "combine",
        )

    def grads(keys, units_rows, rows, name):
        return local(functools.partial(grad_body, keys), [piece] * 2, [units_rows, rows], work // 2, name)

    own, *sends = local(
        functools.partial(route_body, owners, capacity),
        [shape(capacity, features)] + [shape(capacity, half)] * remote,
        [routes.T, tokens],
        2 * count * slots * features,
        "route",
        space=pltpu.HBM,
    )
    mine = over_experts(sends)
    meta, grad_own, *grad_sends = local(
        functools.partial(weigh_body, owners, capacity),
        [shape(count, 128, F32), shape(capacity, features)] + [shape(capacity, half)] * remote,
        [routes.T, combine_index.T, combine_table[None, :], cotangent],
        4 * count * slots * features,
        "weigh",
        space=pltpu.HBM,
    )
    grad_mine = over_experts(grad_sends)
    mine, nearest = after((mine, grad_mine[0]), grad_sends)
    grad_mine = [nearest, *grad_mine[1:]]
    other = across_cores(mine)
    arrived, positive, hidden = local(
        functools.partial(hidden_body, remote),
        [shape(slots, features), shape(units, slots), shape(units, slots)],
        [own, *mine, *other, inner],
        work,
        "hidden",
    )
    turned, give = given(hidden, outer, "rows")
    keep = kept(turned, outer, "rows")
    grad_mine, hidden, keep, give = after((grad_mine, hidden, keep, give))
    came = partner(give, "cuts", 1)
    grad_other = across_cores(grad_mine)
    grad_rows, *outer_sent = local(
        functools.partial(first_grad_body, leaving, remote),
        [shape(slots, features)] + [piece] * 2,
        [grad_own, *grad_mine, *grad_other, hidden],
        work // 2,
        "outer_leaving",
    )
    outer_came = [partner(x, "dp", order[0]) for x, order in zip(outer_sent, orders, strict=True)]
    keep, came = after((keep, came), grad_rows)
    chunks = split(keep, came)
    returned = [chunks[0]] + over_experts(chunks[1:])
    grad_rows, positive = after((grad_rows, positive), chunks)
    (d_act,) = local(
        d_act_body, [shape(units, slots)], [grad_rows, positive, outer], work, "d_act"
    )
    inner_sent = grads(leaving, d_act, arrived, "inner_leaving")
    hidden, grad_rows = after((hidden, grad_rows), inner_sent)
    outer_kept = grads(staying, hidden, grad_rows, "outer_staying")
    d_act_late = after(d_act, outer_kept)
    turned, grad_give = given(d_act_late, inner, "grad_rows")
    grad_keep = kept(turned, inner, "grad_rows")
    *sends, outer_own0, outer_own1 = local(
        mix_body,
        [shape(3 * part_rows, piece.shape[1])] * 2 + [quarter] * 2,
        [*outer_kept, *outer_came, *inner_sent],
        0,
        "mix",
    )
    mixed = [partner(x, "dp", order[0]) for x, order in zip(sends, orders, strict=True)]
    grad_give, returned = after((grad_give, returned))
    grad_came = partner(grad_give, "cuts", 1)
    inner_kept = grads(staying, d_act, arrived, "inner_staying")
    chunks = split(grad_keep, grad_came)
    grad_returned = [chunks[0]] + over_experts(chunks[1:])
    wide, narrow = combine(returned, True)
    mixed = after(mixed, wide)
    move0, move1, inner_own0, inner_own1 = local(
        inner_sum_body, [quarter] * 4, [*inner_kept, *mixed], 0, "inner_sum"
    )
    moved = [partner(x, "dp", order[1]) for x, order in zip((move0, move1), orders, strict=True)]
    (grad_out,) = local(
        last_sum_body, [total], [outer_own0, outer_own1, *mixed[::-1]], 0, "outer_last", gives=pltpu.HBM
    )
    (grad_in,) = local(last_sum_body, [total], [inner_own0, inner_own1, *moved], 0, "inner_last", gives=pltpu.HBM)
    came = partner(narrow, "cuts", 1)
    grad_returned = after(grad_returned, grad_out)
    grad_wide, narrow = combine(grad_returned, False)
    layer_out, d_tokens = local(
        join_body,
        [shape(count, features, F32)] * 2,
        [wide, grad_wide, came, partner(narrow, "cuts", 1)],
        0,
        "join",
        gives=pltpu.HBM,
    )
    grad_in = grad_in.T
    return (layer_out, d_tokens, grad_in[None], grad_out[None])


def solution(mesh):
    in_specs = (
        P(("expert", "dp"), None),
        P(("expert", "dp"), None),
        P(("expert", "dp"), None),
        P(("expert", "dp"), None),
        P(),
        P("expert", None, "cuts"),
        P("expert", "cuts", None),
    )
    out_specs = (
        P(("expert", "dp"), None),
        P(("expert", "dp"), None),
        P("expert", "dp", "cuts"),
        P("expert", "cuts", "dp"),
    )
    return jax.shard_map(shards, mesh=mesh, in_specs=in_specs, out_specs=out_specs, check_vma=False)
```

```python
import functools

import jax
import jax.numpy as jnp
from jax import lax
from jax.experimental import pallas as pl
from jax.experimental.pallas import tpu as pltpu
from jax.sharding import PartitionSpec as P

BF16 = jnp.bfloat16
F32 = jnp.float32
ROW_TILE = 16
TILE = 256
VMEM_BYTES = 24 * 1024 * 1024
COST = 64
MATMUL = (((1,), (0,)), ((), ()))
CONTRACT_LAST = (((1,), (1,)), ((), ()))
CONTRACT_FIRST = (((0,), (0,)), ((), ()))


def mxu(a, b, dims=MATMUL):
    return lax.dot_general(a, b, dims, preferred_element_type=F32)


def shape(rows, columns, dtype=BF16):
    return jax.ShapeDtypeStruct((rows, columns), dtype)


def local(body, outs, operands, flops, name, scratch=(), space=pltpu.VMEM, gives=pltpu.VMEM):
    moved = sum(x.size * x.dtype.itemsize for x in (*operands, *outs))
    return pl.pallas_call(
        body,
        out_shape=tuple(gives(x.shape, x.dtype) for x in outs),
        in_specs=[pl.BlockSpec(memory_space=pltpu.VMEM)] * len(operands),
        out_specs=tuple([pl.BlockSpec(memory_space=pltpu.VMEM)] * len(outs)),
        scratch_shapes=list(scratch),
        compiler_params=pltpu.CompilerParams(vmem_limit_bytes=VMEM_BYTES),
        cost_estimate=pl.CostEstimate(flops=flops // COST, bytes_accessed=moved // COST, transcendentals=0),
        name=name,
    )(*[pltpu.with_memory_space_constraint(x, space) for x in operands])


def window(index, width):
    return pl.ds(pl.multiple_of(index * width, width), width)


def over_tiles(width, step):
    full = width // TILE

    def body(i, carry):
        step(window(i, TILE))
        return carry

    lax.fori_loop(0, full, body, 0)
    if width % TILE:
        step(pl.ds(full * TILE, width - full * TILE))


def tiles(units, rows):
    for part in range(2):
        for i in range(0, rows, TILE):
            yield pl.ds(part * (units // 2), units // 2), pl.ds(i, min(TILE, rows - i))


def picks(meta, k, shift, capacity):
    rows = lax.broadcasted_iota(jnp.int32, (meta.shape[0], capacity), 1) + shift * capacity
    return (meta[:, k : k + 1].astype(jnp.int32) == rows).astype(F32).astype(BF16)


def ones(mask):
    return mask.astype(F32).astype(BF16)


def columns_of(table_t):
    count = table_t.shape[1]
    down, along = (lax.broadcasted_iota(jnp.int32, (count, count), i) for i in range(2))
    return mxu(ones(down == along), table_t.astype(F32).astype(BF16), CONTRACT_LAST).astype(jnp.int32)


def ranks(routes, owners):
    count = routes[0].shape[1]
    expert = lax.broadcasted_iota(jnp.int32, (-(-owners // ROW_TILE) * ROW_TILE, count), 0)
    named = [route == expert for route in routes]
    down, along = (lax.broadcasted_iota(jnp.int32, (count, count), i) for i in range(2))
    before = mxu(ones(sum(n.astype(F32) for n in named) > 0.0), ones(down < along))
    return [jnp.sum(jnp.where(n, before, 0.0), axis=0, keepdims=True).astype(jnp.int32) for n in named]


def rows_for(expert, routes, rank, tokens, capacity):
    row = lax.broadcasted_iota(jnp.int32, (capacity, tokens.shape[0]), 0)
    chosen = sum((route == expert).astype(F32) * (r == row).astype(F32) for route, r in zip(routes, rank, strict=True))
    return mxu(chosen.astype(BF16), tokens).astype(BF16)


def route_body(owners, relayed, routes_ref, tokens_ref, own_ref, *sends):
    me, core = lax.axis_index("expert"), lax.axis_index("cuts")
    top, count = routes_ref.shape
    half = tokens_ref.shape[1] // lax.axis_size("cuts")
    routes = [routes_ref[k : k + 1, :] for k in range(top)]
    rank = ranks(routes, owners)
    narrow = tokens_ref[:, window(core, half)].astype(BF16)
    if relayed:
        *sends, all_ref = sends
        line = lax.broadcasted_iota(jnp.int32, (ROW_TILE, count), 0)
        all_ref[:count, :] = narrow
        all_ref[count:, :] = jnp.zeros((ROW_TILE, half), BF16)
        all_ref[count:, :count] = sum(
            jnp.where(line == k, route, 0).astype(F32) for k, route in enumerate(routes)
        ).astype(BF16)
    for shift, ref in reversed(list(enumerate(sends, 1))):
        ref[...] = rows_for(me ^ shift, routes, rank, narrow, ref.shape[0])
    own_ref[...] = rows_for(me, routes, rank, tokens_ref[...].astype(BF16), own_ref.shape[0])


def pick_body(owners, top, all_ref, mine_ref, relay_ref):
    me = lax.axis_index("expert")
    count = all_ref.shape[0] - ROW_TILE
    lines = all_ref[count:, :count].astype(F32).astype(jnp.int32)
    routes = [lines[k : k + 1, :] for k in range(top)]
    rank = ranks(routes, owners)
    tokens = all_ref[:count, :]
    relay_ref[...] = rows_for(me ^ 1, routes, rank, tokens, relay_ref.shape[0])
    mine_ref[...] = rows_for(me, routes, rank, tokens, mine_ref.shape[0])


def weigh_body(owners, capacity, routes_ref, index_ref, table_ref, cotangent_ref, meta_ref, own_ref, *sends):
    me, core = lax.axis_index("expert"), lax.axis_index("cuts")
    top, count = routes_ref.shape
    width = -(-owners // 128) * 128
    half = cotangent_ref.shape[1] // lax.axis_size("cuts")
    routes, index = columns_of(routes_ref[...]), columns_of(index_ref[...])
    expert_lane = lax.broadcasted_iota(jnp.int32, (count, width), 1)
    named = [routes[:, k : k + 1] == expert_lane for k in range(top)]
    down, along = (lax.broadcasted_iota(jnp.int32, (count, count), i) for i in range(2))
    before = mxu(ones(down > along), ones(sum(n.astype(F32) for n in named) > 0.0))
    level = lax.broadcasted_iota(jnp.int32, (count, table_ref.shape[1]), 1)
    lane = lax.broadcasted_iota(jnp.int32, meta_ref.shape, 1)
    meta = jnp.zeros(meta_ref.shape, F32)
    for k in range(top):
        rank = jnp.sum(jnp.where(named[k], before, 0.0), axis=1, keepdims=True)
        slot = ((routes[:, k : k + 1] ^ me) * capacity).astype(F32) + rank
        weight = jnp.sum(
            jnp.where(index[:, k : k + 1] == level, table_ref[...], 0.0), axis=1, keepdims=True
        )
        meta = jnp.where(lane == k, slot, jnp.where(lane == top + k, weight, meta))
    meta_ref[...] = meta

    def scaled(values):
        return [(meta[:, top + k : top + k + 1] * values).astype(BF16) for k in range(top)]

    wide, narrow = scaled(cotangent_ref[...]), scaled(cotangent_ref[:, window(core, half)])
    for shift, ref in enumerate((own_ref, *sends)):
        rows = narrow if shift else wide
        ref[...] = sum(
            mxu(picks(meta, k, shift, capacity), rows[k], CONTRACT_FIRST) for k in range(top)
        ).astype(BF16)


def assemble(full_ref, whole, mine=(), other=()):
    core = lax.axis_index("cuts")
    capacity = whole[0].shape[0]
    for i, chunk in enumerate(whole):
        full_ref[i * capacity : (i + 1) * capacity, :] = chunk[...]
    for i, (a, b) in enumerate(zip(mine, other, strict=True), len(whole)):
        rows = slice(i * capacity, (i + 1) * capacity)
        full_ref[rows, window(core, a.shape[1])] = a[...]
        full_ref[rows, window(1 - core, a.shape[1])] = b[...]


def hidden_body(owners, *refs):
    inner_ref, x_ref, positive_ref, hidden_ref = refs[owners:]
    assemble(x_ref, refs[:owners])

    for units, rows in tiles(inner_ref.shape[0], x_ref.shape[0]):
        positive = jnp.maximum(mxu(inner_ref[units, :], x_ref[rows, :], CONTRACT_LAST), 0.0)
        positive_ref[units, rows] = positive.astype(BF16)
        hidden_ref[units, rows] = (positive * positive).astype(BF16)


def d_act_body(g_ref, positive_ref, outer_ref, d_act_ref):
    for units, rows in tiles(outer_ref.shape[0], g_ref.shape[0]):
        d_hidden = mxu(outer_ref[units, :], g_ref[rows, :], CONTRACT_LAST)
        d_act_ref[units, rows] = (d_hidden * 2.0 * positive_ref[units, rows].astype(F32)).astype(BF16)


def features_of(owner, rows_ref, weight_ref, out_ref):
    half = out_ref.shape[1]
    for i in range(half // TILE):
        features = window(owner * (half // TILE) + i, TILE)
        out_ref[:, i * TILE : (i + 1) * TILE] = mxu(rows_ref[...], weight_ref[:, features]).astype(BF16)


def give_body(units_ref, weight_ref, turned_ref, give_ref):
    def turn(units):
        turned_ref[:, units] = units_ref[units, :].T

    over_tiles(units_ref.shape[0], turn)
    features_of(1 - lax.axis_index("cuts"), turned_ref, weight_ref, give_ref)


def keep_body(turned_ref, weight_ref, keep_ref):
    features_of(lax.axis_index("cuts"), turned_ref, weight_ref, keep_ref)


def split_body(keep_ref, came_ref, *outs):
    capacity = outs[0].shape[0]
    for i, ref in enumerate(outs):
        rows = slice(i * capacity, (i + 1) * capacity)
        ref[...] = (keep_ref[rows, :].astype(F32) + came_ref[rows, :].astype(F32)).astype(BF16)


def gather_body(remote, own, *refs):
    assemble(refs[2 * remote], own, refs[:remote], refs[remote : 2 * remote])


def pieces(keys, units_ref, rows_ref, outs):
    me = lax.axis_index("dp")
    for part, (blocks, ref) in enumerate(zip(keys, outs, strict=True)):
        rows = ref.shape[0] // len(blocks)
        for i, block in enumerate(blocks):
            features = rows_ref[:, window(me ^ block, ref.shape[1])]
            units = units_ref[part * rows : (part + 1) * rows, :]
            ref[i * rows : (i + 1) * rows, :] = mxu(units, features).astype(BF16)


def grad_body(keys, units_ref, rows_ref, *outs):
    pieces(keys, units_ref, rows_ref, outs)


def first_grad_body(keys, halves, *refs):
    chunks, (units_ref, rows_ref), outs = refs[: -len(keys) - 2], refs[-len(keys) - 2 : -len(keys)], refs[-len(keys) :]
    whole = len(chunks) - 2 * halves
    assemble(rows_ref, chunks[:whole], chunks[whole : whole + halves], chunks[whole + halves :])
    pieces(keys, units_ref, rows_ref, outs)


def combine_body(top, weighted, meta_ref, *refs):
    *chunks, wide_ref, narrow_ref = refs
    meta = meta_ref[...]
    capacity = chunks[0].shape[0]
    total = 0.0
    if weighted:
        for k in range(top):
            got = sum(mxu(picks(meta, k, s, capacity), c[...]) for s, c in enumerate(chunks))
            total += meta[:, top + k : top + k + 1] * got
    else:
        for s, c in enumerate(chunks):
            total += mxu(sum(picks(meta, k, s, capacity) for k in range(top)), c[...])
    wide_ref[...] = total
    narrow_ref[...] = total.astype(BF16)


def join_body(*refs):
    core = lax.axis_index("cuts")
    for mine_ref, other_ref, out_ref in (refs[::2], refs[1::2]):
        half = mine_ref.shape[1]
        out_ref[:, window(core, half)] = mine_ref[...]
        out_ref[:, window(1 - core, half)] = other_ref[...].astype(F32)


def added(a, b):
    return a.astype(F32) + b.astype(F32)


def mix_body(kept0, kept1, came0, came1, inner0, inner1, send0, send1, own0, own1):
    rows = own0.shape[0]
    for kept, came, own, send, inner in ((kept0, came0, own0, send1, inner1), (kept1, came1, own1, send0, inner0)):
        own[...] = added(kept[:rows, :], came[:rows, :]).astype(BF16)
        send[:rows, :] = added(kept[rows:, :], came[rows:, :]).astype(BF16)
        send[rows:, :] = inner[...]


def inner_sum_body(kept0, kept1, mixed0, mixed1, move0, move1, own0, own1):
    rows = own0.shape[0]
    for kept, mixed, move, own in ((kept0, mixed0, move0, own0), (kept1, mixed1, move1, own1)):
        own[...] = added(kept[:rows, :], mixed[rows : 2 * rows, :]).astype(BF16)
        move[...] = added(kept[rows:, :], mixed[2 * rows :, :]).astype(BF16)


def last_sum_body(own0, own1, came0, came1, out_ref):
    rows = own0.shape[0]
    out_ref[:rows, :] = added(own0[...], came0[:rows, :])
    out_ref[rows:, :] = added(own1[...], came1[:rows, :])


def partner(x, axis, bit):
    return lax.ppermute(x, axis, [(i, i ^ bit) for i in range(lax.axis_size(axis))])


def after(values, *earlier):
    return lax.optimization_barrier((values, earlier))[0]


def shards(tokens, cotangent, routes, combine_index, combine_table, w_in, w_out):
    owners, groups = lax.axis_size("expert"), lax.axis_size("dp")
    count, features = tokens.shape
    top = routes.shape[1]
    half = features // lax.axis_size("cuts")
    capacity = -(-max(2, 3 * count * top // (2 * owners)) // ROW_TILE) * ROW_TILE
    slots = owners * capacity
    remote = owners - 1
    inner, outer = w_in[0].T, w_out[0]
    units = outer.shape[0]
    bits = [1 << i for i in range(groups.bit_length() - 1)]
    orders = (bits, bits[::-1])
    leaving = [[r for r in range(groups) if r & order[0]] for order in orders]
    staying = [[r ^ order[0] for r in blocks] for order, blocks in zip(orders, leaving, strict=True)]
    part_rows = units // 2
    piece = shape(part_rows * groups // 2, features // groups)
    quarter = shape(part_rows, features // groups)
    total = shape(units, features // groups, F32)
    work = 2 * slots * features * units

    def across_cores(chunks):
        return [partner(x, "cuts", 1) for x in chunks]

    def joined(chunks):
        return [lax.all_gather(x, "cuts", axis=1, tiled=True) for x in chunks]

    def over_experts(chunks, first=1):
        return [partner(x, "expert", s) for s, x in enumerate(chunks, first)]

    def given(units_rows, weight, name):
        return local(
            give_body, [shape(slots, units), shape(slots, half)], [units_rows, weight], work // 2, name + "_give"
        )

    def kept(turned, weight, name):
        return local(keep_body, [shape(slots, half)], [turned, weight], work // 2, name + "_keep")[0]

    def split(keep, came):
        return local(split_body, [shape(capacity, half)] * owners, [keep, came], 0, "split")

    def combine(chunks, weighted):
        return local(
            functools.partial(combine_body, top, weighted),
            [shape(count, half, F32), shape(count, half)],
            [meta, *chunks],
            2 * count * slots * half,
            "combine",
        )

    def grads(keys, units_rows, rows, name):
        return local(functools.partial(grad_body, keys), [piece] * 2, [units_rows, rows], work // 2, name)

    relayed = owners % 4 == 0 and count + ROW_TILE < 2 * capacity and count <= half
    pairs = range(2, owners, 2) if relayed else ()
    chunk = shape(capacity, half)
    own, *sends = local(
        functools.partial(route_body, owners, relayed),
        [shape(capacity, features)] + ([chunk, shape(count + ROW_TILE, half)] if relayed else [chunk] * remote),
        [routes.T, tokens],
        2 * count * slots * features,
        "route",
        space=pltpu.HBM,
    )
    dense = [partner(sends[-1], "expert", s) for s in pairs]
    mine = over_experts(sends[:1] if relayed else sends)
    meta, grad_own, *grad_sends = local(
        functools.partial(weigh_body, owners, capacity),
        [shape(count, 128, F32), shape(capacity, features)] + [shape(capacity, half)] * remote,
        [routes.T, combine_index.T, combine_table[None, :], cotangent],
        4 * count * slots * features,
        "weigh",
        space=pltpu.HBM,
    )
    nearest = [] if relayed else over_experts(grad_sends[:1])
    mine, dense, nearest, grad_sends = after((mine, dense, nearest, grad_sends))
    relays = []
    for came in dense:
        picked, relay = local(
            functools.partial(pick_body, owners, top), [chunk] * 2, [came], 4 * count * capacity * half, "pick"
        )
        mine += [picked, partner(relay, "expert", 1)]
        relays.append(relay)
    grad_first, *farther = after(grad_sends, relays)
    if relayed:
        nearest = [partner(grad_first, "expert", 1)]
    grad_mine = nearest + over_experts(farther, 2)
    grad_whole = [grad_own]
    arrived, positive, hidden = local(
        functools.partial(hidden_body, owners),
        [shape(slots, features), shape(units, slots), shape(units, slots)],
        [own, *joined(mine), inner],
        work,
        "hidden",
    )
    turned, give = given(hidden, outer, "rows")
    keep = kept(turned, outer, "rows")
    grad_mine, grad_whole, hidden, give = after((grad_mine, grad_whole, hidden, give))
    came = partner(give, "cuts", 1)
    grad_other = across_cores(grad_mine)
    grad_rows, *outer_sent = local(
        functools.partial(first_grad_body, leaving, len(grad_mine)),
        [shape(slots, features)] + [piece] * 2,
        [*grad_whole, *grad_mine, *grad_other, hidden],
        work // 2,
        "outer_leaving",
    )
    outer_came = [partner(x, "dp", order[0]) for x, order in zip(outer_sent, orders, strict=True)]
    keep, came = after((keep, came), grad_rows)
    chunks = split(keep, came)
    returned = [chunks[0]] + over_experts(chunks[1:])
    grad_rows, positive = after((grad_rows, positive), chunks)
    (d_act,) = local(
        d_act_body, [shape(units, slots)], [grad_rows, positive, outer], work, "d_act"
    )
    inner_sent = grads(leaving, d_act, arrived, "inner_leaving")
    hidden, grad_rows = after((hidden, grad_rows), inner_sent)
    outer_kept = grads(staying, hidden, grad_rows, "outer_staying")
    d_act_late = after(d_act, outer_kept)
    turned, grad_give = given(d_act_late, inner, "grad_rows")
    grad_keep = kept(turned, inner, "grad_rows")
    *sends, outer_own0, outer_own1 = local(
        mix_body,
        [shape(3 * part_rows, piece.shape[1])] * 2 + [quarter] * 2,
        [*outer_kept, *outer_came, *inner_sent],
        0,
        "mix",
    )
    mixed = [partner(x, "dp", order[0]) for x, order in zip(sends, orders, strict=True)]
    grad_give, returned = after((grad_give, returned))
    grad_came = partner(grad_give, "cuts", 1)
    inner_kept = grads(staying, d_act, arrived, "inner_staying")
    chunks = split(grad_keep, grad_came)
    grad_returned = [chunks[0]] + over_experts(chunks[1:])
    wide, narrow = combine(returned, True)
    mixed = after(mixed, wide)
    move0, move1, inner_own0, inner_own1 = local(
        inner_sum_body, [quarter] * 4, [*inner_kept, *mixed], 0, "inner_sum"
    )
    moved = [partner(x, "dp", order[1]) for x, order in zip((move0, move1), orders, strict=True)]
    (grad_out,) = local(
        last_sum_body, [total], [outer_own0, outer_own1, *mixed[::-1]], 0, "outer_last", gives=pltpu.HBM
    )
    (grad_in,) = local(last_sum_body, [total], [inner_own0, inner_own1, *moved], 0, "inner_last", gives=pltpu.HBM)
    came = partner(narrow, "cuts", 1)
    grad_returned = after(grad_returned, grad_out)
    grad_wide, narrow = combine(grad_returned, False)
    layer_out, d_tokens = local(
        join_body,
        [shape(count, features, F32)] * 2,
        [wide, grad_wide, came, partner(narrow, "cuts", 1)],
        0,
        "join",
        gives=pltpu.HBM,
    )
    grad_in = grad_in.T
    return (layer_out, d_tokens, grad_in[None], grad_out[None])


def solution(mesh):
    in_specs = (
        P(("expert", "dp"), None),
        P(("expert", "dp"), None),
        P(("expert", "dp"), None),
        P(("expert", "dp"), None),
        P(),
        P("expert", None, "cuts"),
        P("expert", "cuts", None),
    )
    out_specs = (
        P(("expert", "dp"), None),
        P(("expert", "dp"), None),
        P("expert", "dp", "cuts"),
        P("expert", "cuts", "dp"),
    )
    return jax.shard_map(shards, mesh=mesh, in_specs=in_specs, out_specs=out_specs, check_vma=False)
```

```python
import functools

import jax
import jax.numpy as jnp
from jax import lax
from jax.experimental import pallas as pl
from jax.experimental.pallas import tpu as pltpu
from jax.sharding import PartitionSpec as P

BF16 = jnp.bfloat16
F32 = jnp.float32
ROW_TILE = 16
TILE = 256
VMEM_BYTES = 24 * 1024 * 1024
COST = 64
MATMUL = (((1,), (0,)), ((), ()))
CONTRACT_LAST = (((1,), (1,)), ((), ()))
CONTRACT_FIRST = (((0,), (0,)), ((), ()))


def mxu(a, b, dims=MATMUL):
    return lax.dot_general(a, b, dims, preferred_element_type=F32)


def shape(rows, columns, dtype=BF16):
    return jax.ShapeDtypeStruct((rows, columns), dtype)


def local(body, outs, operands, flops, name, scratch=(), space=pltpu.VMEM, gives=pltpu.VMEM):
    moved = sum(x.size * x.dtype.itemsize for x in (*operands, *outs))
    return pl.pallas_call(
        body,
        out_shape=tuple(gives(x.shape, x.dtype) for x in outs),
        in_specs=[pl.BlockSpec(memory_space=pltpu.VMEM)] * len(operands),
        out_specs=tuple([pl.BlockSpec(memory_space=pltpu.VMEM)] * len(outs)),
        scratch_shapes=list(scratch),
        compiler_params=pltpu.CompilerParams(vmem_limit_bytes=VMEM_BYTES),
        cost_estimate=pl.CostEstimate(flops=flops // COST, bytes_accessed=moved // COST, transcendentals=0),
        name=name,
    )(*[pltpu.with_memory_space_constraint(x, space) for x in operands])


def window(index, width):
    return pl.ds(pl.multiple_of(index * width, width), width)


def over_tiles(width, step):
    full = width // TILE

    def body(i, carry):
        step(window(i, TILE))
        return carry

    lax.fori_loop(0, full, body, 0)
    if width % TILE:
        step(pl.ds(full * TILE, width - full * TILE))


def tiles(units, rows):
    for part in range(2):
        for i in range(0, rows, TILE):
            yield pl.ds(part * (units // 2), units // 2), pl.ds(i, min(TILE, rows - i))


def picks(meta, k, shift, capacity):
    rows = lax.broadcasted_iota(jnp.int32, (meta.shape[0], capacity), 1) + shift * capacity
    return (meta[:, k : k + 1].astype(jnp.int32) == rows).astype(F32).astype(BF16)


def ones(mask):
    return mask.astype(F32).astype(BF16)


def columns_of(table_t):
    count = table_t.shape[1]
    down, along = (lax.broadcasted_iota(jnp.int32, (count, count), i) for i in range(2))
    return mxu(ones(down == along), table_t.astype(F32).astype(BF16), CONTRACT_LAST).astype(jnp.int32)


def ranks(routes, owners):
    count = routes[0].shape[1]
    expert = lax.broadcasted_iota(jnp.int32, (-(-owners // ROW_TILE) * ROW_TILE, count), 0)
    named = [route == expert for route in routes]
    down, along = (lax.broadcasted_iota(jnp.int32, (count, count), i) for i in range(2))
    before = mxu(ones(sum(n.astype(F32) for n in named) > 0.0), ones(down < along))
    return [jnp.sum(jnp.where(n, before, 0.0), axis=0, keepdims=True).astype(jnp.int32) for n in named]


def rows_for(expert, routes, rank, tokens, capacity):
    row = lax.broadcasted_iota(jnp.int32, (capacity, tokens.shape[0]), 0)
    chosen = sum((route == expert).astype(F32) * (r == row).astype(F32) for route, r in zip(routes, rank, strict=True))
    return mxu(chosen.astype(BF16), tokens).astype(BF16)


def all_body(routes_ref, tokens_ref, all_ref):
    top, count = routes_ref.shape
    half = all_ref.shape[1]
    line = lax.broadcasted_iota(jnp.int32, (ROW_TILE, count), 0)
    lines = sum(jnp.where(line == k, routes_ref[k : k + 1, :], 0) for k in range(top))
    all_ref[:count, :] = tokens_ref[:, window(lax.axis_index("cuts"), half)].astype(BF16)
    all_ref[count:, :] = jnp.zeros((ROW_TILE, half), BF16)
    all_ref[count:, :count] = lines.astype(F32).astype(BF16)


def route_body(owners, routes_ref, tokens_ref, own_ref, *sends):
    me, core = lax.axis_index("expert"), lax.axis_index("cuts")
    top, count = routes_ref.shape
    half = tokens_ref.shape[1] // lax.axis_size("cuts")
    routes = [routes_ref[k : k + 1, :] for k in range(top)]
    rank = ranks(routes, owners)
    narrow = tokens_ref[:, window(core, half)].astype(BF16)
    for shift, ref in reversed(list(enumerate(sends, 1))):
        ref[...] = rows_for(me ^ shift, routes, rank, narrow, ref.shape[0])
    own_ref[...] = rows_for(me, routes, rank, tokens_ref[...].astype(BF16), own_ref.shape[0])


def pick_body(owners, top, all_ref, mine_ref, relay_ref):
    me = lax.axis_index("expert")
    count = all_ref.shape[0] - ROW_TILE
    lines = all_ref[count:, :count].astype(F32).astype(jnp.int32)
    routes = [lines[k : k + 1, :] for k in range(top)]
    rank = ranks(routes, owners)
    tokens = all_ref[:count, :]
    relay_ref[...] = rows_for(me ^ 1, routes, rank, tokens, relay_ref.shape[0])
    mine_ref[...] = rows_for(me, routes, rank, tokens, mine_ref.shape[0])


def weigh_body(owners, capacity, routes_ref, index_ref, table_ref, cotangent_ref, meta_ref, own_ref, *sends):
    me, core = lax.axis_index("expert"), lax.axis_index("cuts")
    top, count = routes_ref.shape
    width = -(-owners // 128) * 128
    half = cotangent_ref.shape[1] // lax.axis_size("cuts")
    routes, index = columns_of(routes_ref[...]), columns_of(index_ref[...])
    expert_lane = lax.broadcasted_iota(jnp.int32, (count, width), 1)
    named = [routes[:, k : k + 1] == expert_lane for k in range(top)]
    down, along = (lax.broadcasted_iota(jnp.int32, (count, count), i) for i in range(2))
    before = mxu(ones(down > along), ones(sum(n.astype(F32) for n in named) > 0.0))
    level = lax.broadcasted_iota(jnp.int32, (count, table_ref.shape[1]), 1)
    lane = lax.broadcasted_iota(jnp.int32, meta_ref.shape, 1)
    meta = jnp.zeros(meta_ref.shape, F32)
    for k in range(top):
        rank = jnp.sum(jnp.where(named[k], before, 0.0), axis=1, keepdims=True)
        slot = ((routes[:, k : k + 1] ^ me) * capacity).astype(F32) + rank
        weight = jnp.sum(
            jnp.where(index[:, k : k + 1] == level, table_ref[...], 0.0), axis=1, keepdims=True
        )
        meta = jnp.where(lane == k, slot, jnp.where(lane == top + k, weight, meta))
    meta_ref[...] = meta

    def scaled(values):
        return [(meta[:, top + k : top + k + 1] * values).astype(BF16) for k in range(top)]

    wide, narrow = scaled(cotangent_ref[...]), scaled(cotangent_ref[:, window(core, half)])
    for shift, ref in enumerate((own_ref, *sends)):
        rows = narrow if shift else wide
        ref[...] = sum(
            mxu(picks(meta, k, shift, capacity), rows[k], CONTRACT_FIRST) for k in range(top)
        ).astype(BF16)


def assemble(full_ref, whole, mine=(), other=()):
    core = lax.axis_index("cuts")
    capacity = whole[0].shape[0]
    for i, chunk in enumerate(whole):
        full_ref[i * capacity : (i + 1) * capacity, :] = chunk[...]
    for i, (a, b) in enumerate(zip(mine, other, strict=True), len(whole)):
        rows = slice(i * capacity, (i + 1) * capacity)
        full_ref[rows, window(core, a.shape[1])] = a[...]
        full_ref[rows, window(1 - core, a.shape[1])] = b[...]


def hidden_body(owners, *refs):
    inner_ref, x_ref, positive_ref, hidden_ref = refs[owners:]
    assemble(x_ref, refs[:owners])

    for units, rows in tiles(inner_ref.shape[0], x_ref.shape[0]):
        positive = jnp.maximum(mxu(inner_ref[units, :], x_ref[rows, :], CONTRACT_LAST), 0.0)
        positive_ref[units, rows] = positive.astype(BF16)
        hidden_ref[units, rows] = (positive * positive).astype(BF16)


def d_act_body(g_ref, positive_ref, outer_ref, d_act_ref):
    for units, rows in tiles(outer_ref.shape[0], g_ref.shape[0]):
        d_hidden = mxu(outer_ref[units, :], g_ref[rows, :], CONTRACT_LAST)
        d_act_ref[units, rows] = (d_hidden * 2.0 * positive_ref[units, rows].astype(F32)).astype(BF16)


def features_of(owner, rows_ref, weight_ref, out_ref):
    half = out_ref.shape[1]
    for i in range(half // TILE):
        features = window(owner * (half // TILE) + i, TILE)
        out_ref[:, i * TILE : (i + 1) * TILE] = mxu(rows_ref[...], weight_ref[:, features]).astype(BF16)


def give_body(units_ref, weight_ref, turned_ref, give_ref):
    def turn(units):
        turned_ref[:, units] = units_ref[units, :].T

    over_tiles(units_ref.shape[0], turn)
    features_of(1 - lax.axis_index("cuts"), turned_ref, weight_ref, give_ref)


def keep_body(turned_ref, weight_ref, keep_ref):
    features_of(lax.axis_index("cuts"), turned_ref, weight_ref, keep_ref)


def split_body(keep_ref, came_ref, *outs):
    capacity = outs[0].shape[0]
    for i, ref in enumerate(outs):
        rows = slice(i * capacity, (i + 1) * capacity)
        ref[...] = (keep_ref[rows, :].astype(F32) + came_ref[rows, :].astype(F32)).astype(BF16)


def gather_body(remote, own, *refs):
    assemble(refs[2 * remote], own, refs[:remote], refs[remote : 2 * remote])


def pieces(keys, units_ref, rows_ref, outs):
    me = lax.axis_index("dp")
    for part, (blocks, ref) in enumerate(zip(keys, outs, strict=True)):
        rows = ref.shape[0] // len(blocks)
        for i, block in enumerate(blocks):
            features = rows_ref[:, window(me ^ block, ref.shape[1])]
            units = units_ref[part * rows : (part + 1) * rows, :]
            ref[i * rows : (i + 1) * rows, :] = mxu(units, features).astype(BF16)


def grad_body(keys, units_ref, rows_ref, *outs):
    pieces(keys, units_ref, rows_ref, outs)


def first_grad_body(keys, halves, *refs):
    chunks, (units_ref, rows_ref), outs = refs[: -len(keys) - 2], refs[-len(keys) - 2 : -len(keys)], refs[-len(keys) :]
    whole = len(chunks) - 2 * halves
    assemble(rows_ref, chunks[:whole], chunks[whole : whole + halves], chunks[whole + halves :])
    pieces(keys, units_ref, rows_ref, outs)


def combine_body(top, weighted, meta_ref, *refs):
    *chunks, wide_ref, narrow_ref = refs
    meta = meta_ref[...]
    capacity = chunks[0].shape[0]
    total = 0.0
    if weighted:
        for k in range(top):
            got = sum(mxu(picks(meta, k, s, capacity), c[...]) for s, c in enumerate(chunks))
            total += meta[:, top + k : top + k + 1] * got
    else:
        for s, c in enumerate(chunks):
            total += mxu(sum(picks(meta, k, s, capacity) for k in range(top)), c[...])
    wide_ref[...] = total
    narrow_ref[...] = total.astype(BF16)


def join_body(*refs):
    core = lax.axis_index("cuts")
    for mine_ref, other_ref, out_ref in (refs[::2], refs[1::2]):
        half = mine_ref.shape[1]
        out_ref[:, window(core, half)] = mine_ref[...]
        out_ref[:, window(1 - core, half)] = other_ref[...].astype(F32)


def added(a, b):
    return a.astype(F32) + b.astype(F32)


def mix_body(kept0, kept1, came0, came1, inner0, inner1, send0, send1, own0, own1):
    rows = own0.shape[0]
    for kept, came, own, send, inner in ((kept0, came0, own0, send1, inner1), (kept1, came1, own1, send0, inner0)):
        own[...] = added(kept[:rows, :], came[:rows, :]).astype(BF16)
        send[:rows, :] = added(kept[rows:, :], came[rows:, :]).astype(BF16)
        send[rows:, :] = inner[...]


def inner_sum_body(kept0, kept1, mixed0, mixed1, move0, move1, own0, own1):
    rows = own0.shape[0]
    for kept, mixed, move, own in ((kept0, mixed0, move0, own0), (kept1, mixed1, move1, own1)):
        own[...] = added(kept[:rows, :], mixed[rows : 2 * rows, :]).astype(BF16)
        move[...] = added(kept[rows:, :], mixed[2 * rows :, :]).astype(BF16)


def last_sum_body(own0, own1, came0, came1, out_ref):
    rows = own0.shape[0]
    out_ref[:rows, :] = added(own0[...], came0[:rows, :])
    out_ref[rows:, :] = added(own1[...], came1[:rows, :])


def partner(x, axis, bit):
    return lax.ppermute(x, axis, [(i, i ^ bit) for i in range(lax.axis_size(axis))])


def after(values, *earlier):
    return lax.optimization_barrier((values, earlier))[0]


def shards(tokens, cotangent, routes, combine_index, combine_table, w_in, w_out):
    owners, groups = lax.axis_size("expert"), lax.axis_size("dp")
    count, features = tokens.shape
    top = routes.shape[1]
    half = features // lax.axis_size("cuts")
    capacity = -(-max(2, 3 * count * top // (2 * owners)) // ROW_TILE) * ROW_TILE
    slots = owners * capacity
    remote = owners - 1
    inner, outer = w_in[0].T, w_out[0]
    units = outer.shape[0]
    bits = [1 << i for i in range(groups.bit_length() - 1)]
    orders = (bits, bits[::-1])
    leaving = [[r for r in range(groups) if r & order[0]] for order in orders]
    staying = [[r ^ order[0] for r in blocks] for order, blocks in zip(orders, leaving, strict=True)]
    part_rows = units // 2
    piece = shape(part_rows * groups // 2, features // groups)
    quarter = shape(part_rows, features // groups)
    total = shape(units, features // groups, F32)
    work = 2 * slots * features * units

    def across_cores(chunks):
        return [partner(x, "cuts", 1) for x in chunks]

    def joined(chunks):
        return [lax.all_gather(x, "cuts", axis=1, tiled=True) for x in chunks]

    def over_experts(chunks, first=1):
        return [partner(x, "expert", s) for s, x in enumerate(chunks, first)]

    def far_first(chunks):
        return chunks[1:] + chunks[:1]

    def near_first(chunks):
        return chunks[-1:] + chunks[:-1]

    def given(units_rows, weight, name):
        return local(
            give_body, [shape(slots, units), shape(slots, half)], [units_rows, weight], work // 2, name + "_give"
        )

    def kept(turned, weight, name):
        return local(keep_body, [shape(slots, half)], [turned, weight], work // 2, name + "_keep")[0]

    def split(keep, came):
        return local(split_body, [shape(capacity, half)] * owners, [keep, came], 0, "split")

    def combine(chunks, weighted):
        return local(
            functools.partial(combine_body, top, weighted),
            [shape(count, half, F32), shape(count, half)],
            [meta, *chunks],
            2 * count * slots * half,
            "combine",
        )

    def grads(keys, units_rows, rows, name):
        return local(functools.partial(grad_body, keys), [piece] * 2, [units_rows, rows], work // 2, name)

    relayed = owners % 4 == 0 and count + ROW_TILE < 2 * capacity and count <= half
    pairs = range(2, owners, 2) if relayed else ()
    chunk = shape(capacity, half)
    if relayed:
        (everything,) = local(
            all_body, [shape(count + ROW_TILE, half)], [routes.T, tokens], 0, "all_tokens", space=pltpu.HBM
        )
    own, *sends = local(
        functools.partial(route_body, owners),
        [shape(capacity, features)] + [chunk] * (1 if relayed else remote),
        [routes.T, tokens],
        2 * count * slots * features,
        "route",
        space=pltpu.HBM,
    )
    dense = [partner(everything, "expert", s) for s in pairs]
    mine = over_experts(sends)
    meta, grad_own, *grad_sends = local(
        functools.partial(weigh_body, owners, capacity),
        [shape(count, 128, F32), shape(capacity, features)] + [shape(capacity, half)] * remote,
        [routes.T, combine_index.T, combine_table[None, :], cotangent],
        4 * count * slots * features,
        "weigh",
        space=pltpu.HBM,
    )
    nearest = [] if relayed else over_experts(grad_sends[:1])
    mine, dense, nearest, grad_sends = after((mine, dense, nearest, grad_sends))
    relays = []
    for came in dense:
        picked, relay = local(
            functools.partial(pick_body, owners, top), [chunk] * 2, [came], 4 * count * capacity * half, "pick"
        )
        mine += [picked, partner(relay, "expert", 1)]
        relays.append(relay)
    grad_first, *farther = after(grad_sends, relays)
    if relayed:
        nearest = [partner(grad_first, "expert", 1)]
    grad_mine = nearest + over_experts(farther, 2)
    grad_whole = [grad_own]
    arrived, positive, hidden = local(
        functools.partial(hidden_body, owners),
        [shape(slots, features), shape(units, slots), shape(units, slots)],
        [own, *joined(mine), inner],
        work,
        "hidden",
    )
    turned, give = given(hidden, outer, "rows")
    keep = kept(turned, outer, "rows")
    grad_mine, grad_whole, hidden, give = after((far_first(grad_mine), grad_whole, hidden, give))
    grad_mine = near_first(grad_mine)
    came = partner(give, "cuts", 1)
    grad_other = across_cores(grad_mine)
    grad_rows, *outer_sent = local(
        functools.partial(first_grad_body, leaving, len(grad_mine)),
        [shape(slots, features)] + [piece] * 2,
        [*grad_whole, *grad_mine, *grad_other, hidden],
        work // 2,
        "outer_leaving",
    )
    outer_came = [partner(x, "dp", order[0]) for x, order in zip(outer_sent, orders, strict=True)]
    keep, came = after((keep, came), grad_rows)
    chunks = split(keep, came)
    returned = [chunks[0]] + over_experts(chunks[1:])
    grad_rows, positive = after((grad_rows, positive), chunks)
    (d_act,) = local(
        d_act_body, [shape(units, slots)], [grad_rows, positive, outer], work, "d_act"
    )
    inner_sent = grads(leaving, d_act, arrived, "inner_leaving")
    hidden, grad_rows = after((hidden, grad_rows), inner_sent)
    outer_kept = grads(staying, hidden, grad_rows, "outer_staying")
    d_act_late = after(d_act, outer_kept)
    turned, grad_give = given(d_act_late, inner, "grad_rows")
    grad_keep = kept(turned, inner, "grad_rows")
    *sends, outer_own0, outer_own1 = local(
        mix_body,
        [shape(3 * part_rows, piece.shape[1])] * 2 + [quarter] * 2,
        [*outer_kept, *outer_came, *inner_sent],
        0,
        "mix",
    )
    mixed = [partner(x, "dp", order[0]) for x, order in zip(sends, orders, strict=True)]
    grad_give, returned = after((grad_give, returned))
    grad_came = partner(grad_give, "cuts", 1)
    inner_kept = grads(staying, d_act, arrived, "inner_staying")
    chunks = split(grad_keep, grad_came)
    grad_returned = [chunks[0]] + over_experts(chunks[1:])
    wide, narrow = combine(returned, True)
    mixed = after(mixed, wide)
    move0, move1, inner_own0, inner_own1 = local(
        inner_sum_body, [quarter] * 4, [*inner_kept, *mixed], 0, "inner_sum"
    )
    moved = [partner(x, "dp", order[1]) for x, order in zip((move0, move1), orders, strict=True)]
    (grad_out,) = local(
        last_sum_body, [total], [outer_own0, outer_own1, *mixed[::-1]], 0, "outer_last", gives=pltpu.HBM
    )
    (grad_in,) = local(last_sum_body, [total], [inner_own0, inner_own1, *moved], 0, "inner_last", gives=pltpu.HBM)
    came = partner(narrow, "cuts", 1)
    grad_returned = after(grad_returned, grad_out)
    grad_wide, narrow = combine(grad_returned, False)
    layer_out, d_tokens = local(
        join_body,
        [shape(count, features, F32)] * 2,
        [wide, grad_wide, came, partner(narrow, "cuts", 1)],
        0,
        "join",
        gives=pltpu.HBM,
    )
    grad_in = grad_in.T
    return (layer_out, d_tokens, grad_in[None], grad_out[None])


def solution(mesh):
    in_specs = (
        P(("expert", "dp"), None),
        P(("expert", "dp"), None),
        P(("expert", "dp"), None),
        P(("expert", "dp"), None),
        P(),
        P("expert", None, "cuts"),
        P("expert", "cuts", None),
    )
    out_specs = (
        P(("expert", "dp"), None),
        P(("expert", "dp"), None),
        P("expert", "dp", "cuts"),
        P("expert", "cuts", "dp"),
    )
    return jax.shard_map(shards, mesh=mesh, in_specs=in_specs, out_specs=out_specs, check_vma=False)
```

```python
import functools

import jax
import jax.numpy as jnp
from jax import lax
from jax.experimental import pallas as pl
from jax.experimental.pallas import tpu as pltpu
from jax.sharding import PartitionSpec as P

BF16 = jnp.bfloat16
F32 = jnp.float32
ROW_TILE = 16
TILE = 256
VMEM_BYTES = 24 * 1024 * 1024
COST = 64
MATMUL = (((1,), (0,)), ((), ()))
CONTRACT_LAST = (((1,), (1,)), ((), ()))
CONTRACT_FIRST = (((0,), (0,)), ((), ()))


def mxu(a, b, dims=MATMUL):
    return lax.dot_general(a, b, dims, preferred_element_type=F32)


def shape(rows, columns, dtype=BF16):
    return jax.ShapeDtypeStruct((rows, columns), dtype)


def local(body, outs, operands, flops, name, scratch=(), space=pltpu.VMEM, gives=pltpu.VMEM):
    moved = sum(x.size * x.dtype.itemsize for x in (*operands, *outs))
    return pl.pallas_call(
        body,
        out_shape=tuple(gives(x.shape, x.dtype) for x in outs),
        in_specs=[pl.BlockSpec(memory_space=pltpu.VMEM)] * len(operands),
        out_specs=tuple([pl.BlockSpec(memory_space=pltpu.VMEM)] * len(outs)),
        scratch_shapes=list(scratch),
        compiler_params=pltpu.CompilerParams(vmem_limit_bytes=VMEM_BYTES),
        cost_estimate=pl.CostEstimate(flops=flops // COST, bytes_accessed=moved // COST, transcendentals=0),
        name=name,
    )(*[pltpu.with_memory_space_constraint(x, space) for x in operands])


def window(index, width):
    return pl.ds(pl.multiple_of(index * width, width), width)


def over_tiles(width, step):
    full = width // TILE

    def body(i, carry):
        step(window(i, TILE))
        return carry

    lax.fori_loop(0, full, body, 0)
    if width % TILE:
        step(pl.ds(full * TILE, width - full * TILE))


def tiles(units, rows):
    for part in range(2):
        for i in range(0, rows, TILE):
            yield pl.ds(part * (units // 2), units // 2), pl.ds(i, min(TILE, rows - i))


def picks(meta, k, shift, capacity):
    rows = lax.broadcasted_iota(jnp.int32, (meta.shape[0], capacity), 1) + shift * capacity
    return (meta[:, k : k + 1].astype(jnp.int32) == rows).astype(F32).astype(BF16)


def ones(mask):
    return mask.astype(F32).astype(BF16)


def columns_of(table_t):
    count = table_t.shape[1]
    down, along = (lax.broadcasted_iota(jnp.int32, (count, count), i) for i in range(2))
    return mxu(ones(down == along), table_t.astype(F32).astype(BF16), CONTRACT_LAST).astype(jnp.int32)


def ranks(routes, owners):
    count = routes[0].shape[1]
    expert = lax.broadcasted_iota(jnp.int32, (-(-owners // ROW_TILE) * ROW_TILE, count), 0)
    named = [route == expert for route in routes]
    down, along = (lax.broadcasted_iota(jnp.int32, (count, count), i) for i in range(2))
    before = mxu(ones(sum(n.astype(F32) for n in named) > 0.0), ones(down < along))
    return [jnp.sum(jnp.where(n, before, 0.0), axis=0, keepdims=True).astype(jnp.int32) for n in named]


def rows_for(expert, routes, rank, tokens, capacity):
    row = lax.broadcasted_iota(jnp.int32, (capacity, tokens.shape[0]), 0)
    chosen = sum((route == expert).astype(F32) * (r == row).astype(F32) for route, r in zip(routes, rank, strict=True))
    return mxu(chosen.astype(BF16), tokens).astype(BF16)


def all_body(routes_ref, tokens_ref, all_ref):
    top, count = routes_ref.shape
    half = all_ref.shape[1]
    line = lax.broadcasted_iota(jnp.int32, (ROW_TILE, count), 0)
    lines = sum(jnp.where(line == k, routes_ref[k : k + 1, :], 0) for k in range(top))
    all_ref[:count, :] = tokens_ref[:, window(lax.axis_index("cuts"), half)].astype(BF16)
    all_ref[count:, :] = jnp.zeros((ROW_TILE, half), BF16)
    all_ref[count:, :count] = lines.astype(F32).astype(BF16)


def route_body(owners, routes_ref, tokens_ref, own_ref, *sends):
    me, core = lax.axis_index("expert"), lax.axis_index("cuts")
    top, count = routes_ref.shape
    half = tokens_ref.shape[1] // lax.axis_size("cuts")
    routes = [routes_ref[k : k + 1, :] for k in range(top)]
    rank = ranks(routes, owners)
    narrow = tokens_ref[:, window(core, half)].astype(BF16)
    for shift, ref in reversed(list(enumerate(sends, 1))):
        ref[...] = rows_for(me ^ shift, routes, rank, narrow, ref.shape[0])
    own_ref[...] = rows_for(me, routes, rank, tokens_ref[...].astype(BF16), own_ref.shape[0])


def pick_body(owners, top, all_ref, mine_ref, relay_ref):
    me = lax.axis_index("expert")
    count = all_ref.shape[0] - ROW_TILE
    lines = all_ref[count:, :count].astype(F32).astype(jnp.int32)
    routes = [lines[k : k + 1, :] for k in range(top)]
    rank = ranks(routes, owners)
    tokens = all_ref[:count, :]
    relay_ref[...] = rows_for(me ^ 1, routes, rank, tokens, relay_ref.shape[0])
    mine_ref[...] = rows_for(me, routes, rank, tokens, mine_ref.shape[0])


def weigh_body(owners, capacity, routes_ref, index_ref, table_ref, cotangent_ref, meta_ref, own_ref, *sends):
    me, core = lax.axis_index("expert"), lax.axis_index("cuts")
    top, count = routes_ref.shape
    width = -(-owners // 128) * 128
    half = cotangent_ref.shape[1] // lax.axis_size("cuts")
    routes, index = columns_of(routes_ref[...]), columns_of(index_ref[...])
    expert_lane = lax.broadcasted_iota(jnp.int32, (count, width), 1)
    named = [routes[:, k : k + 1] == expert_lane for k in range(top)]
    down, along = (lax.broadcasted_iota(jnp.int32, (count, count), i) for i in range(2))
    before = mxu(ones(down > along), ones(sum(n.astype(F32) for n in named) > 0.0))
    level = lax.broadcasted_iota(jnp.int32, (count, table_ref.shape[1]), 1)
    lane = lax.broadcasted_iota(jnp.int32, meta_ref.shape, 1)
    meta = jnp.zeros(meta_ref.shape, F32)
    for k in range(top):
        rank = jnp.sum(jnp.where(named[k], before, 0.0), axis=1, keepdims=True)
        slot = ((routes[:, k : k + 1] ^ me) * capacity).astype(F32) + rank
        weight = jnp.sum(
            jnp.where(index[:, k : k + 1] == level, table_ref[...], 0.0), axis=1, keepdims=True
        )
        meta = jnp.where(lane == k, slot, jnp.where(lane == top + k, weight, meta))
    meta_ref[...] = meta

    def scaled(values):
        return [(meta[:, top + k : top + k + 1] * values).astype(BF16) for k in range(top)]

    wide, narrow = scaled(cotangent_ref[...]), scaled(cotangent_ref[:, window(core, half)])
    for shift, ref in enumerate((own_ref, *sends)):
        rows = narrow if shift else wide
        ref[...] = sum(
            mxu(picks(meta, k, shift, capacity), rows[k], CONTRACT_FIRST) for k in range(top)
        ).astype(BF16)


def assemble(full_ref, whole, mine=(), other=()):
    core = lax.axis_index("cuts")
    capacity = whole[0].shape[0]
    for i, chunk in enumerate(whole):
        full_ref[i * capacity : (i + 1) * capacity, :] = chunk[...]
    for i, (a, b) in enumerate(zip(mine, other, strict=True), len(whole)):
        rows = slice(i * capacity, (i + 1) * capacity)
        full_ref[rows, window(core, a.shape[1])] = a[...]
        full_ref[rows, window(1 - core, a.shape[1])] = b[...]


def hidden_body(owners, *refs):
    inner_ref, x_ref, positive_ref, hidden_ref = refs[owners:]
    assemble(x_ref, refs[:owners])

    for units, rows in tiles(inner_ref.shape[0], x_ref.shape[0]):
        positive = jnp.maximum(mxu(inner_ref[units, :], x_ref[rows, :], CONTRACT_LAST), 0.0)
        positive_ref[units, rows] = positive.astype(BF16)
        hidden_ref[units, rows] = (positive * positive).astype(BF16)


def d_act_body(g_ref, positive_ref, outer_ref, d_act_ref):
    for units, rows in tiles(outer_ref.shape[0], g_ref.shape[0]):
        d_hidden = mxu(outer_ref[units, :], g_ref[rows, :], CONTRACT_LAST)
        d_act_ref[units, rows] = (d_hidden * 2.0 * positive_ref[units, rows].astype(F32)).astype(BF16)


def features_of(owner, rows_ref, weight_ref, out_ref):
    half = out_ref.shape[1]
    for i in range(half // TILE):
        features = window(owner * (half // TILE) + i, TILE)
        out_ref[:, i * TILE : (i + 1) * TILE] = mxu(rows_ref[...], weight_ref[:, features]).astype(BF16)


def give_body(units_ref, weight_ref, turned_ref, give_ref):
    def turn(units):
        turned_ref[:, units] = units_ref[units, :].T

    over_tiles(units_ref.shape[0], turn)
    features_of(1 - lax.axis_index("cuts"), turned_ref, weight_ref, give_ref)


def keep_body(turned_ref, weight_ref, keep_ref):
    features_of(lax.axis_index("cuts"), turned_ref, weight_ref, keep_ref)


def split_body(keep_ref, came_ref, *outs):
    capacity = outs[0].shape[0]
    for i, ref in enumerate(outs):
        rows = slice(i * capacity, (i + 1) * capacity)
        ref[...] = (keep_ref[rows, :].astype(F32) + came_ref[rows, :].astype(F32)).astype(BF16)


def gather_body(remote, own, *refs):
    assemble(refs[2 * remote], own, refs[:remote], refs[remote : 2 * remote])


def pieces(keys, units_ref, rows_ref, outs):
    me = lax.axis_index("dp")
    for part, (blocks, ref) in enumerate(zip(keys, outs, strict=True)):
        rows = ref.shape[0] // len(blocks)
        for i, block in enumerate(blocks):
            features = rows_ref[:, window(me ^ block, ref.shape[1])]
            units = units_ref[part * rows : (part + 1) * rows, :]
            ref[i * rows : (i + 1) * rows, :] = mxu(units, features).astype(BF16)


def grad_body(keys, units_ref, rows_ref, *outs):
    pieces(keys, units_ref, rows_ref, outs)


def first_grad_body(keys, halves, *refs):
    chunks, (units_ref, rows_ref), outs = refs[: -len(keys) - 2], refs[-len(keys) - 2 : -len(keys)], refs[-len(keys) :]
    whole = len(chunks) - 2 * halves
    assemble(rows_ref, chunks[:whole], chunks[whole : whole + halves], chunks[whole + halves :])
    pieces(keys, units_ref, rows_ref, outs)


def combine_body(top, weighted, meta_ref, *refs):
    *chunks, wide_ref, narrow_ref = refs
    meta = meta_ref[...]
    capacity = chunks[0].shape[0]
    total = 0.0
    if weighted:
        for k in range(top):
            got = sum(mxu(picks(meta, k, s, capacity), c[...]) for s, c in enumerate(chunks))
            total += meta[:, top + k : top + k + 1] * got
    else:
        for s, c in enumerate(chunks):
            total += mxu(sum(picks(meta, k, s, capacity) for k in range(top)), c[...])
    wide_ref[...] = total
    narrow_ref[...] = total.astype(BF16)


def join_body(*refs):
    core = lax.axis_index("cuts")
    for mine_ref, other_ref, out_ref in (refs[::2], refs[1::2]):
        half = mine_ref.shape[1]
        out_ref[:, window(core, half)] = mine_ref[...]
        out_ref[:, window(1 - core, half)] = other_ref[...].astype(F32)


def added(a, b):
    return a.astype(F32) + b.astype(F32)


def mix_body(kept, came, inner, send, own):
    rows = own.shape[0]
    own[...] = added(kept[:rows, :], came[:rows, :]).astype(BF16)
    send[:rows, :] = added(kept[rows:, :], came[rows:, :]).astype(BF16)
    send[rows:, :] = inner[...]


def inner_sum_body(kept, mixed, move, own):
    rows = own.shape[0]
    own[...] = added(kept[:rows, :], mixed[rows : 2 * rows, :]).astype(BF16)
    move[...] = added(kept[rows:, :], mixed[2 * rows :, :]).astype(BF16)


def last_sum_body(own0, own1, came0, came1, out_ref):
    rows = own0.shape[0]
    out_ref[:rows, :] = added(own0[...], came0[:rows, :])
    out_ref[rows:, :] = added(own1[...], came1[:rows, :])


def part_sum_body(own, came, *refs):
    refs[-1][...] = added(own[...], came[...])


def part_sum(part, own, came, total, filled=()):
    whole = pl.BlockSpec(memory_space=pltpu.VMEM)
    return pl.pallas_call(
        part_sum_body,
        grid=(1,),
        out_shape=(pltpu.HBM(total.shape, total.dtype),),
        in_specs=[whole] * 2 + [pl.BlockSpec(memory_space=pl.ANY)] * len(filled),
        out_specs=(pl.BlockSpec(own.shape, lambda i: (part, 0)),),
        input_output_aliases={2: 0} if filled else {},
        compiler_params=pltpu.CompilerParams(vmem_limit_bytes=VMEM_BYTES),
        name="inner_last",
    )(
        *[pltpu.with_memory_space_constraint(x, pltpu.VMEM) for x in (own, came)],
        *[pltpu.with_memory_space_constraint(x, pltpu.HBM) for x in filled],
    )


def partner(x, axis, bit):
    return lax.ppermute(x, axis, [(i, i ^ bit) for i in range(lax.axis_size(axis))])


def after(values, *earlier):
    return lax.optimization_barrier((values, earlier))[0]


def shards(tokens, cotangent, routes, combine_index, combine_table, w_in, w_out):
    owners, groups = lax.axis_size("expert"), lax.axis_size("dp")
    count, features = tokens.shape
    top = routes.shape[1]
    half = features // lax.axis_size("cuts")
    capacity = -(-max(2, 3 * count * top // (2 * owners)) // ROW_TILE) * ROW_TILE
    slots = owners * capacity
    remote = owners - 1
    inner, outer = w_in[0].T, w_out[0]
    units = outer.shape[0]
    bits = [1 << i for i in range(groups.bit_length() - 1)]
    orders = (bits, bits[::-1])
    leaving = [[r for r in range(groups) if r & order[0]] for order in orders]
    staying = [[r ^ order[0] for r in blocks] for order, blocks in zip(orders, leaving, strict=True)]
    part_rows = units // 2
    piece = shape(part_rows * groups // 2, features // groups)
    quarter = shape(part_rows, features // groups)
    total = shape(units, features // groups, F32)
    work = 2 * slots * features * units

    def across_cores(chunks):
        return [partner(x, "cuts", 1) for x in chunks]

    def joined(chunks):
        return [lax.all_gather(x, "cuts", axis=1, tiled=True) for x in chunks]

    def over_experts(chunks, first=1):
        return [partner(x, "expert", s) for s, x in enumerate(chunks, first)]

    def far_first(chunks):
        return chunks[1:] + chunks[:1]

    def near_first(chunks):
        return chunks[-1:] + chunks[:-1]

    def given(units_rows, weight, name):
        return local(
            give_body, [shape(slots, units), shape(slots, half)], [units_rows, weight], work // 2, name + "_give"
        )

    def kept(turned, weight, name):
        return local(keep_body, [shape(slots, half)], [turned, weight], work // 2, name + "_keep")[0]

    def split(keep, came):
        return local(split_body, [shape(capacity, half)] * owners, [keep, came], 0, "split")

    def combine(chunks, weighted):
        return local(
            functools.partial(combine_body, top, weighted),
            [shape(count, half, F32), shape(count, half)],
            [meta, *chunks],
            2 * count * slots * half,
            "combine",
        )

    def grads(keys, units_rows, rows, name):
        return local(functools.partial(grad_body, keys), [piece] * 2, [units_rows, rows], work // 2, name)

    relayed = owners % 4 == 0 and count + ROW_TILE < 2 * capacity and count <= half
    pairs = range(2, owners, 2) if relayed else ()
    chunk = shape(capacity, half)
    if relayed:
        (everything,) = local(
            all_body, [shape(count + ROW_TILE, half)], [routes.T, tokens], 0, "all_tokens", space=pltpu.HBM
        )
    own, *sends = local(
        functools.partial(route_body, owners),
        [shape(capacity, features)] + [chunk] * (1 if relayed else remote),
        [routes.T, tokens],
        2 * count * slots * features,
        "route",
        space=pltpu.HBM,
    )
    dense = [partner(everything, "expert", s) for s in pairs]
    mine = over_experts(sends)
    meta, grad_own, *grad_sends = local(
        functools.partial(weigh_body, owners, capacity),
        [shape(count, 128, F32), shape(capacity, features)] + [shape(capacity, half)] * remote,
        [routes.T, combine_index.T, combine_table[None, :], cotangent],
        4 * count * slots * features,
        "weigh",
        space=pltpu.HBM,
    )
    nearest = [] if relayed else over_experts(grad_sends[:1])
    mine, dense, nearest, grad_sends = after((mine, dense, nearest, grad_sends))
    relays = []
    for came in dense:
        picked, relay = local(
            functools.partial(pick_body, owners, top), [chunk] * 2, [came], 4 * count * capacity * half, "pick"
        )
        mine += [picked, partner(relay, "expert", 1)]
        relays.append(relay)
    grad_first, *farther = after(grad_sends, relays)
    if relayed:
        nearest = [partner(grad_first, "expert", 1)]
    grad_mine = nearest + over_experts(farther, 2)
    grad_whole = [grad_own]
    arrived, positive, hidden = local(
        functools.partial(hidden_body, owners),
        [shape(slots, features), shape(units, slots), shape(units, slots)],
        [own, *joined(mine), inner],
        work,
        "hidden",
    )
    turned, give = given(hidden, outer, "rows")
    keep = kept(turned, outer, "rows")
    grad_mine, grad_whole, hidden, give = after((far_first(grad_mine), grad_whole, hidden, give))
    grad_mine = near_first(grad_mine)
    came = partner(give, "cuts", 1)
    grad_other = across_cores(grad_mine)
    grad_rows, *outer_sent = local(
        functools.partial(first_grad_body, leaving, len(grad_mine)),
        [shape(slots, features)] + [piece] * 2,
        [*grad_whole, *grad_mine, *grad_other, hidden],
        work // 2,
        "outer_leaving",
    )
    outer_came = [partner(x, "dp", order[0]) for x, order in zip(outer_sent, orders, strict=True)]
    keep, came = after((keep, came), grad_rows)
    chunks = split(keep, came)
    returned = [chunks[0]] + over_experts(chunks[1:])
    grad_rows, positive = after((grad_rows, positive), chunks)
    (d_act,) = local(
        d_act_body, [shape(units, slots)], [grad_rows, positive, outer], work, "d_act"
    )
    inner_sent = grads(leaving, d_act, arrived, "inner_leaving")
    hidden, grad_rows = after((hidden, grad_rows), inner_sent)
    outer_kept = grads(staying, hidden, grad_rows, "outer_staying")
    d_act_late = after(d_act, outer_kept)
    turned, grad_give = given(d_act_late, inner, "grad_rows")
    grad_keep = kept(turned, inner, "grad_rows")
    sends, outer_own = zip(
        *[
            local(
                mix_body,
                [shape(3 * part_rows, piece.shape[1]), quarter],
                [outer_kept[part], outer_came[part], inner_sent[1 - part]],
                0,
                "mix",
            )
            for part in range(2)
        ],
        strict=True,
    )
    mixed = [partner(x, "dp", order[0]) for x, order in zip(sends[::-1], orders, strict=True)]
    grad_give, back = after((grad_give, far_first(returned[1:])))
    returned = returned[:1] + near_first(back)
    grad_came = partner(grad_give, "cuts", 1)
    inner_kept = grads(staying, d_act, arrived, "inner_staying")
    chunks = split(grad_keep, grad_came)
    grad_returned = [chunks[0]] + over_experts(chunks[1:])
    wide, narrow = combine(returned, True)
    mixed = [after(x, wide) for x in mixed]
    moving, inner_own = zip(
        *[local(inner_sum_body, [quarter] * 2, list(x), 0, "inner_sum") for x in zip(inner_kept, mixed, strict=True)],
        strict=True,
    )
    moved = [partner(x, "dp", order[1]) for x, order in zip(moving, orders, strict=True)]
    (grad_out,) = local(
        last_sum_body, [total], [*outer_own, *mixed[::-1]], 0, "outer_last", gives=pltpu.HBM
    )
    filled = part_sum(0, inner_own[0], moved[0], total)
    (grad_in,) = part_sum(1, inner_own[1], moved[1], total, filled)
    came = partner(narrow, "cuts", 1)
    back = after(far_first(grad_returned[1:]), grad_out)
    grad_returned = grad_returned[:1] + near_first(back)
    grad_wide, narrow = combine(grad_returned, False)
    layer_out, d_tokens = local(
        join_body,
        [shape(count, features, F32)] * 2,
        [wide, grad_wide, came, partner(narrow, "cuts", 1)],
        0,
        "join",
        gives=pltpu.HBM,
    )
    grad_in = grad_in.T
    return (layer_out, d_tokens, grad_in[None], grad_out[None])


def solution(mesh):
    in_specs = (
        P(("expert", "dp"), None),
        P(("expert", "dp"), None),
        P(("expert", "dp"), None),
        P(("expert", "dp"), None),
        P(),
        P("expert", None, "cuts"),
        P("expert", "cuts", None),
    )
    out_specs = (
        P(("expert", "dp"), None),
        P(("expert", "dp"), None),
        P("expert", "dp", "cuts"),
        P("expert", "cuts", "dp"),
    )
    return jax.shard_map(shards, mesh=mesh, in_specs=in_specs, out_specs=out_specs, check_vma=False)
```

```python
import functools

import jax
import jax.numpy as jnp
from jax import lax
from jax.experimental import pallas as pl
from jax.experimental.pallas import tpu as pltpu
from jax.sharding import PartitionSpec as P

BF16 = jnp.bfloat16
F32 = jnp.float32
ROW_TILE = 16
TILE = 256
VMEM_BYTES = 24 * 1024 * 1024
COST = 64
MATMUL = (((1,), (0,)), ((), ()))
CONTRACT_LAST = (((1,), (1,)), ((), ()))
CONTRACT_FIRST = (((0,), (0,)), ((), ()))


def mxu(a, b, dims=MATMUL):
    return lax.dot_general(a, b, dims, preferred_element_type=F32)


def shape(rows, columns, dtype=BF16):
    return jax.ShapeDtypeStruct((rows, columns), dtype)


def local(body, outs, operands, flops, name, scratch=(), space=pltpu.VMEM, gives=pltpu.VMEM):
    moved = sum(x.size * x.dtype.itemsize for x in (*operands, *outs))
    return pl.pallas_call(
        body,
        out_shape=tuple(gives(x.shape, x.dtype) for x in outs),
        in_specs=[pl.BlockSpec(memory_space=pltpu.VMEM)] * len(operands),
        out_specs=tuple([pl.BlockSpec(memory_space=pltpu.VMEM)] * len(outs)),
        scratch_shapes=list(scratch),
        compiler_params=pltpu.CompilerParams(vmem_limit_bytes=VMEM_BYTES),
        cost_estimate=pl.CostEstimate(flops=flops // COST, bytes_accessed=moved // COST, transcendentals=0),
        name=name,
    )(*[pltpu.with_memory_space_constraint(x, space) for x in operands])


def window(index, width):
    return pl.ds(pl.multiple_of(index * width, width), width)


def over_tiles(width, step):
    full = width // TILE

    def body(i, carry):
        step(window(i, TILE))
        return carry

    lax.fori_loop(0, full, body, 0)
    if width % TILE:
        step(pl.ds(full * TILE, width - full * TILE))


def tiles(units, rows):
    for part in range(2):
        for i in range(0, rows, TILE):
            yield pl.ds(part * (units // 2), units // 2), pl.ds(i, min(TILE, rows - i))


def picks(meta, k, shift, capacity):
    rows = lax.broadcasted_iota(jnp.int32, (meta.shape[0], capacity), 1) + shift * capacity
    return (meta[:, k : k + 1].astype(jnp.int32) == rows).astype(F32).astype(BF16)


def ones(mask):
    return mask.astype(F32).astype(BF16)


def columns_of(table_t):
    count = table_t.shape[1]
    down, along = (lax.broadcasted_iota(jnp.int32, (count, count), i) for i in range(2))
    return mxu(ones(down == along), table_t.astype(F32).astype(BF16), CONTRACT_LAST).astype(jnp.int32)


def ranks(routes, owners):
    count = routes[0].shape[1]
    expert = lax.broadcasted_iota(jnp.int32, (-(-owners // ROW_TILE) * ROW_TILE, count), 0)
    named = [route == expert for route in routes]
    down, along = (lax.broadcasted_iota(jnp.int32, (count, count), i) for i in range(2))
    before = mxu(ones(sum(n.astype(F32) for n in named) > 0.0), ones(down < along))
    return [jnp.sum(jnp.where(n, before, 0.0), axis=0, keepdims=True).astype(jnp.int32) for n in named]


def rows_for(expert, routes, rank, tokens, capacity):
    row = lax.broadcasted_iota(jnp.int32, (capacity, tokens.shape[0]), 0)
    chosen = sum((route == expert).astype(F32) * (r == row).astype(F32) for route, r in zip(routes, rank, strict=True))
    return mxu(chosen.astype(BF16), tokens).astype(BF16)


def all_body(routes_ref, tokens_ref, all_ref, lines_ref):
    line = lax.broadcasted_iota(jnp.int32, lines_ref.shape, 0)
    lines = sum(jnp.where(line == k, routes_ref[k : k + 1, :], 0) for k in range(routes_ref.shape[0]))
    lines_ref[...] = lines.astype(F32).astype(BF16)
    all_ref[...] = tokens_ref[:, window(lax.axis_index("cuts"), all_ref.shape[1])].astype(BF16)


def route_body(owners, routes_ref, tokens_ref, own_ref, *sends):
    me, core = lax.axis_index("expert"), lax.axis_index("cuts")
    top, count = routes_ref.shape
    half = tokens_ref.shape[1] // lax.axis_size("cuts")
    routes = [routes_ref[k : k + 1, :] for k in range(top)]
    rank = ranks(routes, owners)
    narrow = tokens_ref[:, window(core, half)].astype(BF16)
    for shift, ref in reversed(list(enumerate(sends, 1))):
        ref[...] = rows_for(me ^ shift, routes, rank, narrow, ref.shape[0])
    own_ref[...] = rows_for(me, routes, rank, tokens_ref[...].astype(BF16), own_ref.shape[0])


def pick_body(owners, top, all_ref, lines_ref, mine_ref, relay_ref):
    me = lax.axis_index("expert")
    lines = lines_ref[...].astype(F32).astype(jnp.int32)
    routes = [lines[k : k + 1, :] for k in range(top)]
    rank = ranks(routes, owners)
    tokens = all_ref[...]
    relay_ref[...] = rows_for(me ^ 1, routes, rank, tokens, relay_ref.shape[0])
    mine_ref[...] = rows_for(me, routes, rank, tokens, mine_ref.shape[0])


def weigh_body(owners, capacity, routes_ref, index_ref, table_ref, cotangent_ref, meta_ref, own_ref, *sends):
    me, core = lax.axis_index("expert"), lax.axis_index("cuts")
    top, count = routes_ref.shape
    width = -(-owners // 128) * 128
    half = cotangent_ref.shape[1] // lax.axis_size("cuts")
    routes, index = columns_of(routes_ref[...]), columns_of(index_ref[...])
    expert_lane = lax.broadcasted_iota(jnp.int32, (count, width), 1)
    named = [routes[:, k : k + 1] == expert_lane for k in range(top)]
    down, along = (lax.broadcasted_iota(jnp.int32, (count, count), i) for i in range(2))
    before = mxu(ones(down > along), ones(sum(n.astype(F32) for n in named) > 0.0))
    level = lax.broadcasted_iota(jnp.int32, (count, table_ref.shape[1]), 1)
    lane = lax.broadcasted_iota(jnp.int32, meta_ref.shape, 1)
    meta = jnp.zeros(meta_ref.shape, F32)
    for k in range(top):
        rank = jnp.sum(jnp.where(named[k], before, 0.0), axis=1, keepdims=True)
        slot = ((routes[:, k : k + 1] ^ me) * capacity).astype(F32) + rank
        weight = jnp.sum(
            jnp.where(index[:, k : k + 1] == level, table_ref[...], 0.0), axis=1, keepdims=True
        )
        meta = jnp.where(lane == k, slot, jnp.where(lane == top + k, weight, meta))
    meta_ref[...] = meta

    def scaled(values):
        return [(meta[:, top + k : top + k + 1] * values).astype(BF16) for k in range(top)]

    wide, narrow = scaled(cotangent_ref[...]), scaled(cotangent_ref[:, window(core, half)])
    for shift, ref in enumerate((own_ref, *sends)):
        rows = narrow if shift else wide
        ref[...] = sum(
            mxu(picks(meta, k, shift, capacity), rows[k], CONTRACT_FIRST) for k in range(top)
        ).astype(BF16)


def assemble(full_ref, whole, mine=(), other=()):
    core = lax.axis_index("cuts")
    capacity = whole[0].shape[0]
    for i, chunk in enumerate(whole):
        full_ref[i * capacity : (i + 1) * capacity, :] = chunk[...]
    for i, (a, b) in enumerate(zip(mine, other, strict=True), len(whole)):
        rows = slice(i * capacity, (i + 1) * capacity)
        full_ref[rows, window(core, a.shape[1])] = a[...]
        full_ref[rows, window(1 - core, a.shape[1])] = b[...]


def hidden_body(owners, *refs):
    inner_ref, x_ref, positive_ref, hidden_ref = refs[owners:]
    assemble(x_ref, refs[:owners])

    for units, rows in tiles(inner_ref.shape[0], x_ref.shape[0]):
        positive = jnp.maximum(mxu(inner_ref[units, :], x_ref[rows, :], CONTRACT_LAST), 0.0)
        positive_ref[units, rows] = positive.astype(BF16)
        hidden_ref[units, rows] = (positive * positive).astype(BF16)


def d_act_body(g_ref, positive_ref, outer_ref, d_act_ref):
    for units, rows in tiles(outer_ref.shape[0], g_ref.shape[0]):
        d_hidden = mxu(outer_ref[units, :], g_ref[rows, :], CONTRACT_LAST)
        d_act_ref[units, rows] = (d_hidden * 2.0 * positive_ref[units, rows].astype(F32)).astype(BF16)


def features_of(owner, rows_ref, weight_ref, out_ref):
    half = out_ref.shape[1]
    for i in range(half // TILE):
        features = window(owner * (half // TILE) + i, TILE)
        out_ref[:, i * TILE : (i + 1) * TILE] = mxu(rows_ref[...], weight_ref[:, features]).astype(BF16)


def give_body(units_ref, weight_ref, turned_ref, give_ref):
    def turn(units):
        turned_ref[:, units] = units_ref[units, :].T

    over_tiles(units_ref.shape[0], turn)
    features_of(1 - lax.axis_index("cuts"), turned_ref, weight_ref, give_ref)


def keep_body(turned_ref, weight_ref, keep_ref):
    features_of(lax.axis_index("cuts"), turned_ref, weight_ref, keep_ref)


def split_body(keep_ref, came_ref, *outs):
    capacity = outs[0].shape[0]
    for i, ref in enumerate(outs):
        rows = slice(i * capacity, (i + 1) * capacity)
        ref[...] = (keep_ref[rows, :].astype(F32) + came_ref[rows, :].astype(F32)).astype(BF16)


def gather_body(remote, own, *refs):
    assemble(refs[2 * remote], own, refs[:remote], refs[remote : 2 * remote])


def pieces(keys, units_ref, rows_ref, outs):
    me = lax.axis_index("dp")
    for part, (blocks, ref) in enumerate(zip(keys, outs, strict=True)):
        rows = ref.shape[0] // len(blocks)
        for i, block in enumerate(blocks):
            features = rows_ref[:, window(me ^ block, ref.shape[1])]
            units = units_ref[part * rows : (part + 1) * rows, :]
            ref[i * rows : (i + 1) * rows, :] = mxu(units, features).astype(BF16)


def grad_body(keys, units_ref, rows_ref, *outs):
    pieces(keys, units_ref, rows_ref, outs)


def first_grad_body(keys, halves, *refs):
    chunks, (units_ref, rows_ref), outs = refs[: -len(keys) - 2], refs[-len(keys) - 2 : -len(keys)], refs[-len(keys) :]
    whole = len(chunks) - 2 * halves
    assemble(rows_ref, chunks[:whole], chunks[whole : whole + halves], chunks[whole + halves :])
    pieces(keys, units_ref, rows_ref, outs)


def combine_body(top, weighted, meta_ref, *refs):
    *chunks, wide_ref, narrow_ref = refs
    meta = meta_ref[...]
    capacity = chunks[0].shape[0]
    total = 0.0
    if weighted:
        for k in range(top):
            got = sum(mxu(picks(meta, k, s, capacity), c[...]) for s, c in enumerate(chunks))
            total += meta[:, top + k : top + k + 1] * got
    else:
        for s, c in enumerate(chunks):
            total += mxu(sum(picks(meta, k, s, capacity) for k in range(top)), c[...])
    wide_ref[...] = total
    narrow_ref[...] = total.astype(BF16)


def join_body(*refs):
    core = lax.axis_index("cuts")
    for mine_ref, other_ref, out_ref in (refs[::2], refs[1::2]):
        half = mine_ref.shape[1]
        out_ref[:, window(core, half)] = mine_ref[...]
        out_ref[:, window(1 - core, half)] = other_ref[...].astype(F32)


def added(a, b):
    return a.astype(F32) + b.astype(F32)


def mix_body(kept, came, inner, send, own):
    rows = own.shape[0]
    own[...] = added(kept[:rows, :], came[:rows, :]).astype(BF16)
    send[:rows, :] = added(kept[rows:, :], came[rows:, :]).astype(BF16)
    send[rows:, :] = inner[...]


def inner_sum_body(kept, mixed, move, own):
    rows = own.shape[0]
    own[...] = added(kept[:rows, :], mixed[rows : 2 * rows, :]).astype(BF16)
    move[...] = added(kept[rows:, :], mixed[2 * rows :, :]).astype(BF16)


def last_sum_body(own0, own1, came0, came1, out_ref):
    rows = own0.shape[0]
    out_ref[:rows, :] = added(own0[...], came0[:rows, :])
    out_ref[rows:, :] = added(own1[...], came1[:rows, :])


def part_sum_body(own, came, *refs):
    refs[-1][...] = added(own[...], came[...])


def part_sum(part, own, came, total, filled=()):
    whole = pl.BlockSpec(memory_space=pltpu.VMEM)
    return pl.pallas_call(
        part_sum_body,
        grid=(1,),
        out_shape=(pltpu.HBM(total.shape, total.dtype),),
        in_specs=[whole] * 2 + [pl.BlockSpec(memory_space=pl.ANY)] * len(filled),
        out_specs=(pl.BlockSpec(own.shape, lambda i: (part, 0)),),
        input_output_aliases={2: 0} if filled else {},
        compiler_params=pltpu.CompilerParams(vmem_limit_bytes=VMEM_BYTES),
        name="inner_last",
    )(
        *[pltpu.with_memory_space_constraint(x, pltpu.VMEM) for x in (own, came)],
        *[pltpu.with_memory_space_constraint(x, pltpu.HBM) for x in filled],
    )


def partner(x, axis, bit):
    return lax.ppermute(x, axis, [(i, i ^ bit) for i in range(lax.axis_size(axis))])


def after(values, *earlier):
    return lax.optimization_barrier((values, earlier))[0]


def shards(tokens, cotangent, routes, combine_index, combine_table, w_in, w_out):
    owners, groups = lax.axis_size("expert"), lax.axis_size("dp")
    count, features = tokens.shape
    top = routes.shape[1]
    half = features // lax.axis_size("cuts")
    capacity = -(-max(2, 3 * count * top // (2 * owners)) // ROW_TILE) * ROW_TILE
    slots = owners * capacity
    remote = owners - 1
    inner, outer = w_in[0].T, w_out[0]
    units = outer.shape[0]
    bits = [1 << i for i in range(groups.bit_length() - 1)]
    orders = (bits, bits[::-1])
    leaving = [[r for r in range(groups) if r & order[0]] for order in orders]
    staying = [[r ^ order[0] for r in blocks] for order, blocks in zip(orders, leaving, strict=True)]
    part_rows = units // 2
    piece = shape(part_rows * groups // 2, features // groups)
    quarter = shape(part_rows, features // groups)
    total = shape(units, features // groups, F32)
    work = 2 * slots * features * units

    def across_cores(chunks):
        return [partner(x, "cuts", 1) for x in chunks]

    def joined(chunks):
        return [lax.all_gather(x, "cuts", axis=1, tiled=True) for x in chunks]

    def over_experts(chunks, first=1):
        return [partner(x, "expert", s) for s, x in enumerate(chunks, first)]

    def far_first(chunks):
        return chunks[1:] + chunks[:1]

    def near_first(chunks):
        return chunks[-1:] + chunks[:-1]

    def given(units_rows, weight, name):
        return local(
            give_body, [shape(slots, units), shape(slots, half)], [units_rows, weight], work // 2, name + "_give"
        )

    def kept(turned, weight, name):
        return local(keep_body, [shape(slots, half)], [turned, weight], work // 2, name + "_keep")[0]

    def split(keep, came):
        return local(split_body, [shape(capacity, half)] * owners, [keep, came], 0, "split")

    def combine(chunks, weighted):
        return local(
            functools.partial(combine_body, top, weighted),
            [shape(count, half, F32), shape(count, half)],
            [meta, *chunks],
            2 * count * slots * half,
            "combine",
        )

    def grads(keys, units_rows, rows, name):
        return local(functools.partial(grad_body, keys), [piece] * 2, [units_rows, rows], work // 2, name)

    relayed = owners % 4 == 0 and count + ROW_TILE < 2 * capacity and count <= half
    pairs = range(2, owners, 2) if relayed else ()
    chunk = shape(capacity, half)
    if relayed:
        everything, lines = local(
            all_body, [shape(count, half), shape(ROW_TILE, count)], [routes.T, tokens], 0, "all_tokens", space=pltpu.HBM
        )
    own, *sends = local(
        functools.partial(route_body, owners),
        [shape(capacity, features)] + [chunk] * (1 if relayed else remote),
        [routes.T, tokens],
        2 * count * slots * features,
        "route",
        space=pltpu.HBM,
    )
    dense = [partner(everything, "expert", s) for s in pairs]
    mine = over_experts(sends)
    lines = [partner(lines, "expert", s) for s in pairs]
    meta, grad_own, *grad_sends = local(
        functools.partial(weigh_body, owners, capacity),
        [shape(count, 128, F32), shape(capacity, features)] + [shape(capacity, half)] * remote,
        [routes.T, combine_index.T, combine_table[None, :], cotangent],
        4 * count * slots * features,
        "weigh",
        space=pltpu.HBM,
    )
    nearest = [] if relayed else over_experts(grad_sends[:1])
    mine, dense, lines, nearest, grad_sends = after((mine, dense, lines, nearest, grad_sends))
    relays = []
    for came, named in zip(dense, lines, strict=True):
        picked, relay = local(
            functools.partial(pick_body, owners, top), [chunk] * 2, [came, named], 4 * count * capacity * half, "pick"
        )
        mine += [picked, partner(relay, "expert", 1)]
        relays.append(relay)
    grad_first, *farther = after(grad_sends, relays)
    if relayed:
        nearest = [partner(grad_first, "expert", 1)]
    grad_mine = nearest + over_experts(farther, 2)
    grad_whole = [grad_own]
    arrived, positive, hidden = local(
        functools.partial(hidden_body, owners),
        [shape(slots, features), shape(units, slots), shape(units, slots)],
        [own, *joined(mine), inner],
        work,
        "hidden",
    )
    turned, give = given(hidden, outer, "rows")
    keep = kept(turned, outer, "rows")
    grad_mine, grad_whole, hidden, give = after((far_first(grad_mine), grad_whole, hidden, give))
    grad_mine = near_first(grad_mine)
    came = partner(give, "cuts", 1)
    grad_other = across_cores(grad_mine)
    grad_rows, *outer_sent = local(
        functools.partial(first_grad_body, leaving, len(grad_mine)),
        [shape(slots, features)] + [piece] * 2,
        [*grad_whole, *grad_mine, *grad_other, hidden],
        work // 2,
        "outer_leaving",
    )
    outer_came = [partner(x, "dp", order[0]) for x, order in zip(outer_sent, orders, strict=True)]
    keep, came = after((keep, came), grad_rows)
    chunks = split(keep, came)
    returned = [chunks[0]] + over_experts(chunks[1:])
    grad_rows, positive = after((grad_rows, positive), chunks)
    (d_act,) = local(
        d_act_body, [shape(units, slots)], [grad_rows, positive, outer], work, "d_act"
    )
    inner_sent = grads(leaving, d_act, arrived, "inner_leaving")
    hidden, grad_rows = after((hidden, grad_rows), inner_sent)
    outer_kept = grads(staying, hidden, grad_rows, "outer_staying")
    d_act_late = after(d_act, outer_kept)
    turned, grad_give = given(d_act_late, inner, "grad_rows")
    grad_keep = kept(turned, inner, "grad_rows")
    sends, outer_own = zip(
        *[
            local(
                mix_body,
                [shape(3 * part_rows, piece.shape[1]), quarter],
                [outer_kept[part], outer_came[part], inner_sent[1 - part]],
                0,
                "mix",
            )
            for part in range(2)
        ],
        strict=True,
    )
    mixed = [partner(x, "dp", order[0]) for x, order in zip(sends[::-1], orders, strict=True)]
    grad_give, back = after((grad_give, far_first(returned[1:])))
    returned = returned[:1] + near_first(back)
    grad_came = partner(grad_give, "cuts", 1)
    inner_kept = grads(staying, d_act, arrived, "inner_staying")
    chunks = split(grad_keep, grad_came)
    grad_returned = [chunks[0]] + over_experts(chunks[1:])
    wide, narrow = combine(returned, True)
    mixed = [after(x, wide) for x in mixed]
    moving, inner_own = zip(
        *[local(inner_sum_body, [quarter] * 2, list(x), 0, "inner_sum") for x in zip(inner_kept, mixed, strict=True)],
        strict=True,
    )
    moved = [partner(x, "dp", order[1]) for x, order in zip(moving, orders, strict=True)]
    (grad_out,) = local(
        last_sum_body, [total], [*outer_own, *mixed[::-1]], 0, "outer_last", gives=pltpu.HBM
    )
    filled = part_sum(0, inner_own[0], moved[0], total)
    (grad_in,) = part_sum(1, inner_own[1], moved[1], total, filled)
    came = partner(narrow, "cuts", 1)
    back = after(far_first(grad_returned[1:]), grad_out)
    grad_returned = grad_returned[:1] + near_first(back)
    grad_wide, narrow = combine(grad_returned, False)
    layer_out, d_tokens = local(
        join_body,
        [shape(count, features, F32)] * 2,
        [wide, grad_wide, came, partner(narrow, "cuts", 1)],
        0,
        "join",
        gives=pltpu.HBM,
    )
    grad_in = grad_in.T
    return (layer_out, d_tokens, grad_in[None], grad_out[None])


def solution(mesh):
    in_specs = (
        P(("expert", "dp"), None),
        P(("expert", "dp"), None),
        P(("expert", "dp"), None),
        P(("expert", "dp"), None),
        P(),
        P("expert", None, "cuts"),
        P("expert", "cuts", None),
    )
    out_specs = (
        P(("expert", "dp"), None),
        P(("expert", "dp"), None),
        P("expert", "dp", "cuts"),
        P("expert", "cuts", "dp"),
    )
    return jax.shard_map(shards, mesh=mesh, in_specs=in_specs, out_specs=out_specs, check_vma=False)
```

```python
import functools

import jax
import jax.numpy as jnp
from jax import lax
from jax.experimental import pallas as pl
from jax.experimental.pallas import tpu as pltpu
from jax.sharding import PartitionSpec as P

BF16 = jnp.bfloat16
F32 = jnp.float32
ROW_TILE = 16
TILE = 256
VMEM_BYTES = 24 * 1024 * 1024
COST = 64
MATMUL = (((1,), (0,)), ((), ()))
CONTRACT_LAST = (((1,), (1,)), ((), ()))
CONTRACT_FIRST = (((0,), (0,)), ((), ()))


def mxu(a, b, dims=MATMUL):
    return lax.dot_general(a, b, dims, preferred_element_type=F32)


def shape(rows, columns, dtype=BF16):
    return jax.ShapeDtypeStruct((rows, columns), dtype)


def local(body, outs, operands, flops, name, scratch=(), space=pltpu.VMEM, gives=pltpu.VMEM):
    moved = sum(x.size * x.dtype.itemsize for x in (*operands, *outs))
    return pl.pallas_call(
        body,
        out_shape=tuple(gives(x.shape, x.dtype) for x in outs),
        in_specs=[pl.BlockSpec(memory_space=pltpu.VMEM)] * len(operands),
        out_specs=tuple([pl.BlockSpec(memory_space=pltpu.VMEM)] * len(outs)),
        scratch_shapes=list(scratch),
        compiler_params=pltpu.CompilerParams(vmem_limit_bytes=VMEM_BYTES),
        cost_estimate=pl.CostEstimate(flops=flops // COST, bytes_accessed=moved // COST, transcendentals=0),
        name=name,
    )(*[pltpu.with_memory_space_constraint(x, space) for x in operands])


def window(index, width):
    return pl.ds(pl.multiple_of(index * width, width), width)


def over_tiles(width, step):
    full = width // TILE

    def body(i, carry):
        step(window(i, TILE))
        return carry

    lax.fori_loop(0, full, body, 0)
    if width % TILE:
        step(pl.ds(full * TILE, width - full * TILE))


def tiles(units, rows):
    for part in range(2):
        for i in range(0, rows, TILE):
            yield pl.ds(part * (units // 2), units // 2), pl.ds(i, min(TILE, rows - i))


def picks(meta, k, shift, capacity):
    rows = lax.broadcasted_iota(jnp.int32, (meta.shape[0], capacity), 1) + shift * capacity
    return (meta[:, k : k + 1].astype(jnp.int32) == rows).astype(F32).astype(BF16)


def ones(mask):
    return mask.astype(F32).astype(BF16)


def columns_of(table_t):
    count = table_t.shape[1]
    down, along = (lax.broadcasted_iota(jnp.int32, (count, count), i) for i in range(2))
    return mxu(ones(down == along), table_t.astype(F32).astype(BF16), CONTRACT_LAST).astype(jnp.int32)


def ranks(routes, owners):
    count = routes[0].shape[1]
    expert = lax.broadcasted_iota(jnp.int32, (-(-owners // ROW_TILE) * ROW_TILE, count), 0)
    named = [route == expert for route in routes]
    down, along = (lax.broadcasted_iota(jnp.int32, (count, count), i) for i in range(2))
    before = mxu(ones(sum(n.astype(F32) for n in named) > 0.0), ones(down < along))
    return [jnp.sum(jnp.where(n, before, 0.0), axis=0, keepdims=True).astype(jnp.int32) for n in named]


def rows_for(expert, routes, rank, tokens, capacity):
    row = lax.broadcasted_iota(jnp.int32, (capacity, tokens.shape[0]), 0)
    chosen = sum((route == expert).astype(F32) * (r == row).astype(F32) for route, r in zip(routes, rank, strict=True))
    return mxu(chosen.astype(BF16), tokens).astype(BF16)


def all_body(routes_ref, tokens_ref, all_ref, lines_ref):
    line = lax.broadcasted_iota(jnp.int32, lines_ref.shape, 0)
    lines = sum(jnp.where(line == k, routes_ref[k : k + 1, :], 0) for k in range(routes_ref.shape[0]))
    lines_ref[...] = lines.astype(F32).astype(BF16)
    all_ref[...] = tokens_ref[:, window(lax.axis_index("cuts"), all_ref.shape[1])].astype(BF16)


def route_body(owners, routes_ref, tokens_ref, own_ref, *sends):
    me, core = lax.axis_index("expert"), lax.axis_index("cuts")
    top, count = routes_ref.shape
    half = tokens_ref.shape[1] // lax.axis_size("cuts")
    routes = [routes_ref[k : k + 1, :] for k in range(top)]
    rank = ranks(routes, owners)
    narrow = tokens_ref[:, window(core, half)].astype(BF16)
    for shift, ref in reversed(list(enumerate(sends, 1))):
        ref[...] = rows_for(me ^ shift, routes, rank, narrow, ref.shape[0])
    own_ref[...] = rows_for(me, routes, rank, tokens_ref[...].astype(BF16), own_ref.shape[0])


def pick_body(owners, top, all_ref, lines_ref, mine_ref, relay_ref):
    me = lax.axis_index("expert")
    lines = lines_ref[...].astype(F32).astype(jnp.int32)
    routes = [lines[k : k + 1, :] for k in range(top)]
    rank = ranks(routes, owners)
    tokens = all_ref[...]
    relay_ref[...] = rows_for(me ^ 1, routes, rank, tokens, relay_ref.shape[0])
    mine_ref[...] = rows_for(me, routes, rank, tokens, mine_ref.shape[0])


def weigh_body(owners, capacity, routes_ref, index_ref, table_ref, cotangent_ref, meta_ref, own_ref, *sends):
    me, core = lax.axis_index("expert"), lax.axis_index("cuts")
    top, count = routes_ref.shape
    width = -(-owners // 128) * 128
    half = cotangent_ref.shape[1] // lax.axis_size("cuts")
    routes, index = columns_of(routes_ref[...]), columns_of(index_ref[...])
    expert_lane = lax.broadcasted_iota(jnp.int32, (count, width), 1)
    named = [routes[:, k : k + 1] == expert_lane for k in range(top)]
    down, along = (lax.broadcasted_iota(jnp.int32, (count, count), i) for i in range(2))
    before = mxu(ones(down > along), ones(sum(n.astype(F32) for n in named) > 0.0))
    level = lax.broadcasted_iota(jnp.int32, (count, table_ref.shape[1]), 1)
    lane = lax.broadcasted_iota(jnp.int32, meta_ref.shape, 1)
    meta = jnp.zeros(meta_ref.shape, F32)
    for k in range(top):
        rank = jnp.sum(jnp.where(named[k], before, 0.0), axis=1, keepdims=True)
        slot = ((routes[:, k : k + 1] ^ me) * capacity).astype(F32) + rank
        weight = jnp.sum(
            jnp.where(index[:, k : k + 1] == level, table_ref[...], 0.0), axis=1, keepdims=True
        )
        meta = jnp.where(lane == k, slot, jnp.where(lane == top + k, weight, meta))
    meta_ref[...] = meta

    def scaled(values):
        return [(meta[:, top + k : top + k + 1] * values).astype(BF16) for k in range(top)]

    wide, narrow = scaled(cotangent_ref[...]), scaled(cotangent_ref[:, window(core, half)])
    for shift, ref in enumerate((own_ref, *sends)):
        rows = narrow if shift else wide
        ref[...] = sum(
            mxu(picks(meta, k, shift, capacity), rows[k], CONTRACT_FIRST) for k in range(top)
        ).astype(BF16)


def assemble(full_ref, whole, mine=(), other=()):
    core = lax.axis_index("cuts")
    capacity = whole[0].shape[0]
    for i, chunk in enumerate(whole):
        full_ref[i * capacity : (i + 1) * capacity, :] = chunk[...]
    for i, (a, b) in enumerate(zip(mine, other, strict=True), len(whole)):
        rows = slice(i * capacity, (i + 1) * capacity)
        full_ref[rows, window(core, a.shape[1])] = a[...]
        full_ref[rows, window(1 - core, a.shape[1])] = b[...]


def hidden_body(owners, *refs):
    inner_ref, x_ref, positive_ref, hidden_ref = refs[owners:]
    assemble(x_ref, refs[:owners])

    for units, rows in tiles(inner_ref.shape[0], x_ref.shape[0]):
        positive = jnp.maximum(mxu(inner_ref[units, :], x_ref[rows, :], CONTRACT_LAST), 0.0)
        positive_ref[units, rows] = positive.astype(BF16)
        hidden_ref[units, rows] = (positive * positive).astype(BF16)


def d_act_body(g_ref, positive_ref, outer_ref, d_act_ref):
    for units, rows in tiles(outer_ref.shape[0], g_ref.shape[0]):
        d_hidden = mxu(outer_ref[units, :], g_ref[rows, :], CONTRACT_LAST)
        d_act_ref[units, rows] = (d_hidden * 2.0 * positive_ref[units, rows].astype(F32)).astype(BF16)


def features_of(owner, rows_ref, weight_ref, out_ref):
    half = out_ref.shape[1]
    for i in range(half // TILE):
        features = window(owner * (half // TILE) + i, TILE)
        out_ref[:, i * TILE : (i + 1) * TILE] = mxu(rows_ref[...], weight_ref[:, features]).astype(BF16)


def give_body(units_ref, weight_ref, turned_ref, give_ref):
    def turn(units):
        turned_ref[:, units] = units_ref[units, :].T

    over_tiles(units_ref.shape[0], turn)
    features_of(1 - lax.axis_index("cuts"), turned_ref, weight_ref, give_ref)


def keep_body(turned_ref, weight_ref, keep_ref):
    features_of(lax.axis_index("cuts"), turned_ref, weight_ref, keep_ref)


def split_body(keep_ref, came_ref, *outs):
    capacity = outs[0].shape[0]
    for i, ref in enumerate(outs):
        rows = slice(i * capacity, (i + 1) * capacity)
        ref[...] = (keep_ref[rows, :].astype(F32) + came_ref[rows, :].astype(F32)).astype(BF16)


def gather_body(remote, own, *refs):
    assemble(refs[2 * remote], own, refs[:remote], refs[remote : 2 * remote])


def pieces(keys, units_ref, rows_ref, outs):
    me = lax.axis_index("dp")
    for part, (blocks, ref) in enumerate(zip(keys, outs, strict=True)):
        rows = ref.shape[0] // len(blocks)
        for i, block in enumerate(blocks):
            features = rows_ref[:, window(me ^ block, ref.shape[1])]
            units = units_ref[part * rows : (part + 1) * rows, :]
            ref[i * rows : (i + 1) * rows, :] = mxu(units, features).astype(BF16)


def grad_body(keys, units_ref, rows_ref, *outs):
    pieces(keys, units_ref, rows_ref, outs)


def first_grad_body(keys, halves, *refs):
    chunks, (units_ref, rows_ref), outs = refs[: -len(keys) - 2], refs[-len(keys) - 2 : -len(keys)], refs[-len(keys) :]
    whole = len(chunks) - 2 * halves
    assemble(rows_ref, chunks[:whole], chunks[whole : whole + halves], chunks[whole + halves :])
    pieces(keys, units_ref, rows_ref, outs)


def combine_body(top, weighted, meta_ref, *refs):
    *chunks, wide_ref, narrow_ref = refs
    meta = meta_ref[...]
    capacity = chunks[0].shape[0]
    total = 0.0
    if weighted:
        for k in range(top):
            got = sum(mxu(picks(meta, k, s, capacity), c[...]) for s, c in enumerate(chunks))
            total += meta[:, top + k : top + k + 1] * got
    else:
        for s, c in enumerate(chunks):
            total += mxu(sum(picks(meta, k, s, capacity) for k in range(top)), c[...])
    wide_ref[...] = total
    narrow_ref[...] = total.astype(BF16)


def join_body(*refs):
    core = lax.axis_index("cuts")
    for mine_ref, other_ref, out_ref in (refs[::2], refs[1::2]):
        half = mine_ref.shape[1]
        out_ref[:, window(core, half)] = mine_ref[...]
        out_ref[:, window(1 - core, half)] = other_ref[...].astype(F32)


def added(a, b):
    return a.astype(F32) + b.astype(F32)


def mix_body(kept, came, inner, send, own):
    rows = own.shape[0]
    own[...] = added(kept[:rows, :], came[:rows, :]).astype(BF16)
    send[:rows, :] = added(kept[rows:, :], came[rows:, :]).astype(BF16)
    send[rows:, :] = inner[...]


def inner_sum_body(kept, mixed, move, own):
    rows = own.shape[0]
    own[...] = added(kept[:rows, :], mixed[rows : 2 * rows, :]).astype(BF16)
    move[...] = added(kept[rows:, :], mixed[2 * rows :, :]).astype(BF16)


def last_sum_body(own0, own1, came0, came1, out_ref):
    rows = own0.shape[0]
    out_ref[:rows, :] = added(own0[...], came0[:rows, :])
    out_ref[rows:, :] = added(own1[...], came1[:rows, :])


def part_sum_body(own, came, *refs):
    refs[-1][...] = added(own[...], came[...])


def part_sum(part, own, came, total, filled=()):
    whole = pl.BlockSpec(memory_space=pltpu.VMEM)
    return pl.pallas_call(
        part_sum_body,
        grid=(1,),
        out_shape=(pltpu.HBM(total.shape, total.dtype),),
        in_specs=[whole] * 2 + [pl.BlockSpec(memory_space=pl.ANY)] * len(filled),
        out_specs=(pl.BlockSpec(own.shape, lambda i: (part, 0)),),
        input_output_aliases={2: 0} if filled else {},
        compiler_params=pltpu.CompilerParams(vmem_limit_bytes=VMEM_BYTES),
        name="inner_last",
    )(
        *[pltpu.with_memory_space_constraint(x, pltpu.VMEM) for x in (own, came)],
        *[pltpu.with_memory_space_constraint(x, pltpu.HBM) for x in filled],
    )


def partner(x, axis, bit):
    return lax.ppermute(x, axis, [(i, i ^ bit) for i in range(lax.axis_size(axis))])


def after(values, *earlier):
    return lax.optimization_barrier((values, earlier))[0]


def shards(tokens, cotangent, routes, combine_index, combine_table, w_in, w_out):
    owners, groups = lax.axis_size("expert"), lax.axis_size("dp")
    count, features = tokens.shape
    top = routes.shape[1]
    half = features // lax.axis_size("cuts")
    capacity = -(-max(2, 3 * count * top // (2 * owners)) // ROW_TILE) * ROW_TILE
    slots = owners * capacity
    remote = owners - 1
    inner, outer = w_in[0].T, w_out[0]
    units = outer.shape[0]
    bits = [1 << i for i in range(groups.bit_length() - 1)]
    orders = (bits, bits[::-1])
    leaving = [[r for r in range(groups) if r & order[0]] for order in orders]
    staying = [[r ^ order[0] for r in blocks] for order, blocks in zip(orders, leaving, strict=True)]
    part_rows = units // 2
    piece = shape(part_rows * groups // 2, features // groups)
    quarter = shape(part_rows, features // groups)
    total = shape(units, features // groups, F32)
    work = 2 * slots * features * units

    def across_cores(chunks):
        return [partner(x, "cuts", 1) for x in chunks]

    def joined(chunks):
        return [lax.all_gather(x, "cuts", axis=1, tiled=True) for x in chunks]

    def over_experts(chunks, first=1):
        return [partner(x, "expert", s) for s, x in enumerate(chunks, first)]

    def far_first(chunks):
        return chunks[1:] + chunks[:1]

    def far_started(chunks):
        return near_first([partner(x, "expert", s) for s, x in far_first(list(enumerate(chunks, 1)))])

    def near_first(chunks):
        return chunks[-1:] + chunks[:-1]

    def given(units_rows, weight, name):
        return local(
            give_body, [shape(slots, units), shape(slots, half)], [units_rows, weight], work // 2, name + "_give"
        )

    def kept(turned, weight, name):
        return local(keep_body, [shape(slots, half)], [turned, weight], work // 2, name + "_keep")[0]

    def split(keep, came):
        return local(split_body, [shape(capacity, half)] * owners, [keep, came], 0, "split")

    def combine(chunks, weighted):
        return local(
            functools.partial(combine_body, top, weighted),
            [shape(count, half, F32), shape(count, half)],
            [meta, *chunks],
            2 * count * slots * half,
            "combine",
        )

    def grads(keys, units_rows, rows, name):
        return local(functools.partial(grad_body, keys), [piece] * 2, [units_rows, rows], work // 2, name)

    relayed = owners % 4 == 0 and count + ROW_TILE < 2 * capacity and count <= half
    pairs = range(2, owners, 2) if relayed else ()
    chunk = shape(capacity, half)
    if relayed:
        everything, lines = local(
            all_body, [shape(count, half), shape(ROW_TILE, count)], [routes.T, tokens], 0, "all_tokens", space=pltpu.HBM
        )
    own, *sends = local(
        functools.partial(route_body, owners),
        [shape(capacity, features)] + [chunk] * (1 if relayed else remote),
        [routes.T, tokens],
        2 * count * slots * features,
        "route",
        space=pltpu.HBM,
    )
    dense = [partner(everything, "expert", s) for s in pairs]
    mine = over_experts(sends)
    lines = [partner(lines, "expert", s) for s in pairs]
    meta, grad_own, *grad_sends = local(
        functools.partial(weigh_body, owners, capacity),
        [shape(count, 128, F32), shape(capacity, features)] + [shape(capacity, half)] * remote,
        [routes.T, combine_index.T, combine_table[None, :], cotangent],
        4 * count * slots * features,
        "weigh",
        space=pltpu.HBM,
    )
    nearest = [] if relayed else over_experts(grad_sends[:1])
    mine, dense, lines, nearest, grad_sends = after((mine, dense, lines, nearest, grad_sends))
    relays = []
    for came, named in zip(dense, lines, strict=True):
        picked, relay = local(
            functools.partial(pick_body, owners, top), [chunk] * 2, [came, named], 4 * count * capacity * half, "pick"
        )
        mine += [picked, partner(relay, "expert", 1)]
        relays.append(relay)
    grad_first, *farther = after(grad_sends, relays)
    if relayed:
        nearest = [partner(grad_first, "expert", 1)]
    grad_mine = nearest + over_experts(farther, 2)
    grad_whole = [grad_own]
    arrived, positive, hidden = local(
        functools.partial(hidden_body, owners),
        [shape(slots, features), shape(units, slots), shape(units, slots)],
        [own, *joined(mine), inner],
        work,
        "hidden",
    )
    turned, give = given(hidden, outer, "rows")
    keep = kept(turned, outer, "rows")
    grad_mine, grad_whole, hidden, give = after((far_first(grad_mine), grad_whole, hidden, give))
    grad_mine = near_first(grad_mine)
    came = partner(give, "cuts", 1)
    grad_other = across_cores(grad_mine)
    grad_rows, *outer_sent = local(
        functools.partial(first_grad_body, leaving, len(grad_mine)),
        [shape(slots, features)] + [piece] * 2,
        [*grad_whole, *grad_mine, *grad_other, hidden],
        work // 2,
        "outer_leaving",
    )
    outer_came = [partner(x, "dp", order[0]) for x, order in zip(outer_sent, orders, strict=True)]
    keep, came = after((keep, came), grad_rows)
    chunks = split(keep, came)
    returned = [chunks[0]] + far_started(chunks[1:])
    grad_rows, positive = after((grad_rows, positive), chunks)
    (d_act,) = local(
        d_act_body, [shape(units, slots)], [grad_rows, positive, outer], work, "d_act"
    )
    inner_sent = grads(leaving, d_act, arrived, "inner_leaving")
    hidden, grad_rows = after((hidden, grad_rows), inner_sent)
    outer_kept = grads(staying, hidden, grad_rows, "outer_staying")
    d_act_late = after(d_act, outer_kept)
    turned, grad_give = given(d_act_late, inner, "grad_rows")
    grad_keep = kept(turned, inner, "grad_rows")
    sends, outer_own = zip(
        *[
            local(
                mix_body,
                [shape(3 * part_rows, piece.shape[1]), quarter],
                [outer_kept[part], outer_came[part], inner_sent[1 - part]],
                0,
                "mix",
            )
            for part in range(2)
        ],
        strict=True,
    )
    mixed = [partner(x, "dp", order[0]) for x, order in zip(sends[::-1], orders, strict=True)]
    back, grad_give = after((far_first(returned[1:]), grad_give))
    returned = returned[:1] + near_first(back)
    grad_came = partner(grad_give, "cuts", 1)
    inner_kept = grads(staying, d_act, arrived, "inner_staying")
    chunks = split(grad_keep, grad_came)
    grad_returned = [chunks[0]] + over_experts(chunks[1:])
    wide, narrow = combine(returned, True)
    mixed = [after(x, wide) for x in mixed]
    moving, inner_own = zip(
        *[local(inner_sum_body, [quarter] * 2, list(x), 0, "inner_sum") for x in zip(inner_kept, mixed, strict=True)],
        strict=True,
    )
    moved = [partner(x, "dp", order[1]) for x, order in zip(moving, orders, strict=True)]
    (grad_out,) = local(
        last_sum_body, [total], [*outer_own, *mixed[::-1]], 0, "outer_last", gives=pltpu.HBM
    )
    filled = part_sum(0, inner_own[0], moved[0], total)
    (grad_in,) = part_sum(1, inner_own[1], moved[1], total, filled)
    came = partner(narrow, "cuts", 1)
    back = after(far_first(grad_returned[1:]), grad_out)
    grad_returned = grad_returned[:1] + near_first(back)
    grad_wide, narrow = combine(grad_returned, False)
    layer_out, d_tokens = local(
        join_body,
        [shape(count, features, F32)] * 2,
        [wide, grad_wide, came, partner(narrow, "cuts", 1)],
        0,
        "join",
        gives=pltpu.HBM,
    )
    grad_in = grad_in.T
    return (layer_out, d_tokens, grad_in[None], grad_out[None])


def solution(mesh):
    in_specs = (
        P(("expert", "dp"), None),
        P(("expert", "dp"), None),
        P(("expert", "dp"), None),
        P(("expert", "dp"), None),
        P(),
        P("expert", None, "cuts"),
        P("expert", "cuts", None),
    )
    out_specs = (
        P(("expert", "dp"), None),
        P(("expert", "dp"), None),
        P("expert", "dp", "cuts"),
        P("expert", "cuts", "dp"),
    )
    return jax.shard_map(shards, mesh=mesh, in_specs=in_specs, out_specs=out_specs, check_vma=False)
```
